256 devices in a mesh: dp: 64 (over z, x, y_hi), mp: 4 (over y_lo, core).
Axes of the slice: x: 4, y: 4 (y_hi: 2, y_lo: 2; y = y_hi * 2 + y_lo), z: 8, core: 2. Of those that a mesh axis runs over, the one named last changes fastest.
Arguments:
- images: bfloat16 [12288, 1152], P('dp'), may hold values from -0.4375 to 0.4375
- hidden_in: float32 [12288, 1152], P('dp'), may hold values from -0.625 to 0.625
- norm1_gain: float32 [1152], replicated, may hold values from 0.1 to 1.9
- norm1_bias: float32 [1152], replicated, may hold values from -3 to 3
- fc1: bfloat16 [1152, 4304], P(None, 'mp'), may hold values from -0.1875 to 0.1875
- fc1_bias: float32 [4304], P('mp'), may hold values from -3 to 3
- fc2: bfloat16 [4304, 1152], P('mp'), may hold values from -0.01171875 to 0.01171875
- norm2_gain: float32 [1152], replicated, may hold values from 0.1 to 1.9
- norm2_bias: float32 [1152], replicated, may hold values from -3 to 3
- head: bfloat16 [1152, 1152], replicated, may hold values from -0.1875 to 0.1875
- log_scale: float32 [1], replicated, may hold values from 3 to 3.6
- logit_bias: float32 [1], replicated, may hold values from -6 to -4
Outputs:
- grad_images: float32 [12288, 1152], P('dp', 'mp')
- grad_hidden: float32 [12288, 1152], P('dp', 'mp')
The draws below stay inside these ranges and needn't reach their ends.
All inputs are finite; a program needn't handle non-finite values.
Results may differ from the reference program's by a relative error of at most 0.025.
Values may be sent and summed in bfloat16 or wider, within the bound.
No kernel may reach another device: no remote copies, remote signals or barrier semaphores. Data moves between devices by JAX's collectives and lax.ppermute only.
A program may use at most 128 MiB of HBM per device.

```python
import jax
import jax.numpy as jnp
from jax import lax

D = 1152
FF = 4304
TXT_DEV = 192
PAIRS = 12288
N_DP = 64


def block_scale(rng, shape, split, smallest, top_value):
    level, own = 1.0, jax.random.fold_in(rng, 6)
    for dim, shards_of in split:
        heights = jnp.exp(jax.random.uniform(jax.random.fold_in(own, dim), (shards_of,), jnp.float32, smallest / len(split), top_value / len(split)))
        level = level * jnp.repeat(heights, shape[dim] // shards_of).reshape([-1 if axis == dim else 1 for axis in range(len(shape))])
    return level


def centred(key, shape, deviation, limit, pieces=(), held_as=jnp.bfloat16):
    array = jax.random.normal(key, shape, jnp.float32) * deviation
    if len(pieces) > 0:
        array = block_scale(key, shape, pieces, -0.22, 0.18) * array
    return jnp.clip(array, min=-limit, max=limit).astype(held_as)


def setup_inputs(seed: int = 0) -> dict:
    key_of = jax.random.split(jax.random.key(seed), 13)
    images = centred(key_of[0], (PAIRS, D), 0.03, 0.4375, ((0, 64),))
    hidden_in = centred(key_of[1], (PAIRS, D), 0.04, 0.625, ((0, 64),), jnp.float32)
    norm1_gain = jnp.clip(1.0 + 0.18 * jax.random.normal(key_of[2], (D,), jnp.float32), 0.1, 1.9)
    norm1_bias = centred(key_of[3], (D,), 0.3, 3.0, (), jnp.float32)
    fc1 = centred(key_of[4], (D, FF), D ** -0.5, 0.1875, ((1, 4),))
    fc1_bias = centred(key_of[5], (FF,), 0.5, 3.0, ((0, 4),), jnp.float32)
    fc2 = centred(key_of[6], (FF, D), (64 * FF) ** -0.5, 0.01171875, ((0, 4),))
    norm2_gain = jnp.clip(1.0 + 0.18 * jax.random.normal(key_of[7], (D,), jnp.float32), 0.1, 1.9)
    norm2_bias = centred(key_of[8], (D,), 0.3, 3.0, (), jnp.float32)
    head = centred(key_of[9], (D, D), D ** -0.5, 0.1875)
    log_scale = jnp.clip(jax.random.uniform(key_of[10], (1,), jnp.float32, 3.0, 3.6), 3.0, 3.6)
    logit_bias = jnp.clip(jax.random.uniform(key_of[11], (1,), jnp.float32, -6.0, -4.0), -6.0, -4.0)
    return dict(images=images, hidden_in=hidden_in, norm1_gain=norm1_gain, norm1_bias=norm1_bias, fc1=fc1, fc1_bias=fc1_bias, fc2=fc2, norm2_gain=norm2_gain, norm2_bias=norm2_bias, head=head, log_scale=log_scale, logit_bias=logit_bias)


eps = 1e-06

def normalize(values, gain, shift):
    mean = lax.optimization_barrier(jnp.mean(values, axis=-1, keepdims=True))
    centered = values - mean
    inverse = lax.rsqrt(lax.optimization_barrier(jnp.mean(centered * centered, axis=-1, keepdims=True)) + eps)
    scaled = centered * inverse
    return (scaled * gain + shift, scaled, inverse)

def gelu_slope(values):
    factor = 0.7978845608028654
    inner = factor * (values + 0.044715 * values * values * values)
    tangent = jnp.tanh(inner)
    return 0.5 * (1.0 + tangent) + 0.5 * values * (1.0 - tangent * tangent) * factor * (1.0 + 3.0 * 0.044715 * values * values)

def norm_back(upstream, gain, scaled, inverse):
    grad = upstream * gain
    return inverse * (grad - lax.optimization_barrier(jnp.mean(grad, axis=-1, keepdims=True)) - scaled * lax.optimization_barrier(jnp.mean(grad * scaled, axis=-1, keepdims=True)))

def reference(images, hidden_in, norm1_gain, norm1_bias, fc1, fc1_bias, fc2, norm2_gain, norm2_bias, head, log_scale, logit_bias):
    normed_in, scaled_in, inverse_in = normalize(hidden_in, norm1_gain, norm1_bias)
    pre = jnp.dot(normed_in.astype(jnp.bfloat16), fc1, preferred_element_type=jnp.float32) + fc1_bias
    act = jax.nn.gelu(pre, approximate=True).astype(jnp.bfloat16)
    mixed = hidden_in + jnp.dot(act, fc2, preferred_element_type=jnp.float32)
    normed_out, scaled_out, inverse_out = normalize(mixed, norm2_gain, norm2_bias)
    embed = jnp.dot(normed_out.astype(jnp.bfloat16), head, preferred_element_type=jnp.float32)
    inverse_embed = lax.rsqrt(lax.optimization_barrier(jnp.sum(embed * embed, axis=-1, keepdims=True)) + eps)
    text_dir = embed * inverse_embed
    text_unit = text_dir.astype(jnp.bfloat16)
    image_wide = images.astype(jnp.float32)
    inverse_image = lax.rsqrt(lax.optimization_barrier(jnp.sum(image_wide * image_wide, axis=-1, keepdims=True)) + eps)
    image_dir = image_wide * inverse_image
    image_unit = image_dir.astype(jnp.bfloat16)
    scale = jnp.exp(log_scale[0])
    offset = logit_bias[0]
    pairs = images.shape[0]
    width = images.shape[1]
    columns = jnp.arange(pairs, dtype=jnp.int32)

    def one_block(carry, block_index):
        first = (block_index * TXT_DEV).astype(jnp.int32)
        rows = lax.dynamic_slice_in_dim(image_unit, first, TXT_DEV, 0)
        logits = scale * jnp.dot(rows, text_unit.T, preferred_element_type=jnp.float32) + offset
        row_ids = first + jnp.arange(TXT_DEV, dtype=jnp.int32)
        ident = (row_ids[:, None] == columns[None, :]).astype(jnp.float32)
        coef = (scale * (jax.nn.sigmoid(logits) - ident)).astype(jnp.bfloat16)
        grad_rows = jnp.dot(coef, text_unit, preferred_element_type=jnp.float32)
        carry = carry + lax.dot_general(coef, rows, (((0,), (0,)), ((), ())), preferred_element_type=jnp.float32)
        return (carry, grad_rows)
    grad_text_unit, grad_blocks = lax.scan(one_block, jnp.zeros((pairs, width), jnp.float32), jnp.arange(N_DP, dtype=jnp.int32))
    grad_image_unit = grad_blocks.reshape(pairs, width)
    image_inner = lax.optimization_barrier(jnp.sum(image_dir * grad_image_unit, axis=-1, keepdims=True))
    grad_images = (grad_image_unit - image_dir * image_inner) * inverse_image
    text_inner = lax.optimization_barrier(jnp.sum(text_dir * grad_text_unit, axis=-1, keepdims=True))
    grad_embed = ((grad_text_unit - text_dir * text_inner) * inverse_embed).astype(jnp.bfloat16)
    grad_normed_out = lax.dot_general(grad_embed, head, (((1,), (1,)), ((), ())), preferred_element_type=jnp.float32)
    grad_mixed = norm_back(grad_normed_out, norm2_gain, scaled_out, inverse_out)
    grad_act = lax.dot_general(grad_mixed.astype(jnp.bfloat16), fc2, (((1,), (1,)), ((), ())), preferred_element_type=jnp.float32)
    grad_pre = (grad_act * gelu_slope(pre)).astype(jnp.bfloat16)
    grad_normed_in = lax.dot_general(grad_pre, fc1, (((1,), (1,)), ((), ())), preferred_element_type=jnp.float32)
    grad_hidden = grad_mixed + norm_back(grad_normed_in, norm1_gain, scaled_in, inverse_in)
    return (grad_images, grad_hidden)
```

```python
import jax
import jax.numpy as jnp
from jax import lax
from jax.sharding import Mesh, PartitionSpec as P

eps = 1e-06
Y = ("yh", "yl")
hops = (0, 1, 3, 2)
f32 = jnp.float32
bf16 = jnp.bfloat16


def normalize(values, gain, shift):
    mean = jnp.mean(values, axis=-1, keepdims=True)
    centered = values - mean
    inverse = lax.rsqrt(jnp.mean(centered * centered, axis=-1, keepdims=True) + eps)
    scaled = centered * inverse
    return (scaled * gain + shift, scaled, inverse)


def gelu_slope(values):
    factor = 0.7978845608028654
    inner = factor * (values + 0.044715 * values * values * values)
    tangent = jnp.tanh(inner)
    return 0.5 * (1.0 + tangent) + 0.5 * values * (1.0 - tangent * tangent) * factor * (
        1.0 + 3.0 * 0.044715 * values * values
    )


def norm_back(upstream, gain, scaled, inverse):
    grad = upstream * gain
    return inverse * (
        grad
        - jnp.mean(grad, axis=-1, keepdims=True)
        - scaled * jnp.mean(grad * scaled, axis=-1, keepdims=True)
    )


def contract_rows(left, right):
    return lax.dot_general(left, right, (((0,), (0,)), ((), ())), preferred_element_type=f32)


def contract_cols(left, right):
    return lax.dot_general(left, right, (((1,), (1,)), ((), ())), preferred_element_type=f32)


def shift(values, axes, step):
    size = lax.axis_size(axes)
    return lax.ppermute(values, axes, [(i, (i + step) % size) for i in range(size)])


def swap(first, second, axis):
    low = lax.axis_index(axis) == 0
    keep = jnp.where(low, first, second)
    send = jnp.where(low, second, first)
    return keep.astype(f32) + shift(send.astype(bf16), axis, 1).astype(f32)


def columns(values, share):
    even = jnp.concatenate([values[:, :share], values[:, 2 * share : 3 * share]], axis=1)
    odd = jnp.concatenate([values[:, share : 2 * share], values[:, 3 * share :]], axis=1)
    return even, odd


def spread(own, cut):
    left, right = own[:, :cut], own[:, cut:]
    left_x, right_y = [left], [right]
    for hop in hops[1:]:
        left_x.append(shift(left, "x", hop))
        right_y.append(shift(right, Y, hop))
    left_x = jnp.stack(left_x)
    right_y = jnp.stack(right_y)
    left_all, right_all = [left_x], [right_y]
    for hop in hops[1:]:
        left_all.append(shift(left_x, Y, hop))
        right_all.append(shift(right_y, "x", hop))
    right_all = jnp.swapaxes(jnp.stack(right_all), 0, 1)
    return jnp.concatenate([jnp.stack(left_all), right_all], axis=-1)


def collect(parts, cut):
    left, right = parts[..., :cut], jnp.swapaxes(parts[..., cut:], 0, 1)
    left_sum, right_sum = left[0], right[0]
    left_low, right_low = left.astype(bf16), right.astype(bf16)
    got_left = []
    got_right = []
    for place in (1, 2, 3):
        got_left.append(shift(left_low[place], Y, 4 - hops[place]))
        got_right.append(shift(right_low[place], "x", 4 - hops[place]))
    for piece in got_left:
        left_sum = left_sum + piece.astype(f32)
    for piece in got_right:
        right_sum = right_sum + piece.astype(f32)
    left_low, right_low = left_sum.astype(bf16), right_sum.astype(bf16)
    left_sum, right_sum = left_sum[0], right_sum[0]
    got_left = []
    got_right = []
    for place in (1, 2, 3):
        got_left.append(shift(left_low[place], "x", 4 - hops[place]))
        got_right.append(shift(right_low[place], Y, 4 - hops[place]))
    for piece in got_left:
        left_sum = left_sum + piece.astype(f32)
    for piece in got_right:
        right_sum = right_sum + piece.astype(f32)
    return jnp.concatenate([left_sum, right_sum], axis=-1)


def shards(
    images,
    hidden_in,
    norm1_gain,
    norm1_bias,
    fc1,
    fc1_bias,
    fc2,
    norm2_gain,
    norm2_bias,
    head,
    log_scale,
    logit_bias,
):
    block, width = images.shape
    quarter = block // 4
    share = width // 4
    cut = (width // 2 + 127) // 128 * 128
    z_at, yl_at, c_at = (lax.axis_index(a) for a in ("z", "yl", "c"))
    place = yl_at * 2 + c_at

    own_images = lax.dynamic_slice_in_dim(images, place * quarter, quarter, 0)
    image_rows = lax.all_gather(own_images, ("z", "c"), axis=0, tiled=True)

    normed_in, scaled_in, inverse_in = normalize(hidden_in, norm1_gain, norm1_bias)
    pre = jnp.dot(normed_in.astype(bf16), fc1, preferred_element_type=f32) + fc1_bias
    act = jax.nn.gelu(pre, approximate=True).astype(bf16)
    part = jnp.dot(act, fc2, preferred_element_type=f32).reshape(2, 2, quarter, width)
    part = swap(part[:, 0], part[:, 1], "c")
    mlp_out = swap(part[0], part[1], "yl")
    mixed = lax.dynamic_slice_in_dim(hidden_in, place * quarter, quarter, 0) + mlp_out
    normed_out, scaled_out, inverse_out = normalize(mixed, norm2_gain, norm2_bias)
    embed = jnp.dot(normed_out.astype(bf16), head, preferred_element_type=f32)
    inverse_embed = lax.rsqrt(jnp.sum(embed * embed, axis=-1, keepdims=True) + eps)
    text_dir = embed * inverse_embed
    texts = spread(text_dir.astype(bf16), cut).reshape(16 * quarter, width)

    image_wide = image_rows.astype(f32)
    inverse_image = lax.rsqrt(jnp.sum(image_wide * image_wide, axis=-1, keepdims=True) + eps)
    image_dir = image_wide * inverse_image
    image_unit = image_dir.astype(bf16)
    scale = jnp.exp(log_scale[0])
    logits = scale * contract_cols(image_unit, texts) + logit_bias[0]
    rows = lax.broadcasted_iota(jnp.int32, logits.shape, 0) - (z_at * 2 + c_at) * quarter
    cols = lax.broadcasted_iota(jnp.int32, logits.shape, 1)
    ident = ((rows == cols) & (cols < quarter)).astype(f32)
    coef = (scale * (jax.nn.sigmoid(logits) - ident)).astype(bf16)

    text_part = contract_rows(coef, image_unit).reshape(4, 4, quarter, width)
    grad_text_unit = collect(text_part, cut)

    image_part = jnp.dot(coef, texts, preferred_element_type=f32)
    image_inner = jnp.sum(image_dir * image_part, axis=-1, keepdims=True)
    image_part = (image_part - image_dir * image_inner) * inverse_image
    image_part = swap(*columns(image_part, share), "c").astype(bf16)
    image_part = lax.psum_scatter(image_part, "z", scatter_dimension=0, tiled=True)

    text_inner = jnp.sum(text_dir * grad_text_unit, axis=-1, keepdims=True)
    grad_embed = ((grad_text_unit - text_dir * text_inner) * inverse_embed).astype(bf16)
    grad_normed_out = contract_cols(grad_embed, head)
    grad_mixed = norm_back(grad_normed_out, norm2_gain, scaled_out, inverse_out)
    grad_mixed = lax.all_gather(grad_mixed.astype(bf16), ("yl", "c"), axis=0, tiled=True)
    grad_act = contract_cols(grad_mixed, fc2)
    grad_pre = (grad_act * gelu_slope(pre)).astype(bf16)
    input_part = norm_back(contract_cols(grad_pre, fc1), norm1_gain, scaled_in, inverse_in)
    input_part = swap(*columns(input_part, share), "c")
    input_part = swap(input_part[:, :share], input_part[:, share:], "yl")
    residual = jnp.where(c_at == 0, *columns(grad_mixed, share))
    residual = jnp.where(yl_at == 0, residual[:, :share], residual[:, share:])
    grad_hidden = residual.astype(f32) + input_part

    keep = jnp.where(yl_at == 0, image_part[:, :share], image_part[:, share:])
    send = jnp.where(yl_at == 0, image_part[:, share:], image_part[:, :share])
    got = shift(send, "yl", 1)
    grad_images = jnp.concatenate(
        [jnp.where(yl_at == 0, keep, got), jnp.where(yl_at == 0, got, keep)], axis=0
    ).astype(f32)
    return (grad_images, grad_hidden)


def solution(mesh):
    grid = Mesh(mesh.devices.reshape(8, 4, 2, 2, 2), ("z", "x", "yh", "yl", "c"))
    dp, mp = ("z", "x", "yh"), ("yl", "c")
    placed = (
        P(dp, None),
        P(dp, None),
        P(),
        P(),
        P(None, mp),
        P(mp),
        P(mp, None),
        P(),
        P(),
        P(),
        P(),
        P(),
    )
    return jax.shard_map(
        shards,
        mesh=grid,
        in_specs=placed,
        out_specs=(P(dp, mp), P(dp, mp)),
        check_vma=False,
    )
```

```python
import functools

import jax
import jax.numpy as jnp
from jax import lax
from jax.experimental import pallas as pl
from jax.experimental.pallas import tpu as pltpu
from jax.sharding import Mesh, PartitionSpec as P

eps = 1e-06
hops = (0, 1, 3, 2)
f32 = jnp.float32
bf16 = jnp.bfloat16


def normalize(values, gain, shift):
    mean = jnp.mean(values, axis=-1, keepdims=True)
    centered = values - mean
    inverse = lax.rsqrt(jnp.mean(centered * centered, axis=-1, keepdims=True) + eps)
    scaled = centered * inverse
    return (scaled * gain + shift, scaled, inverse)


def gelu_slope(values):
    factor = 0.7978845608028654
    inner = factor * (values + 0.044715 * values * values * values)
    tangent = jnp.tanh(inner)
    return 0.5 * (1.0 + tangent) + 0.5 * values * (1.0 - tangent * tangent) * factor * (
        1.0 + 3.0 * 0.044715 * values * values
    )


def norm_back(upstream, gain, scaled, inverse):
    grad = upstream * gain
    return inverse * (
        grad
        - jnp.mean(grad, axis=-1, keepdims=True)
        - scaled * jnp.mean(grad * scaled, axis=-1, keepdims=True)
    )


def contract_rows(left, right):
    return lax.dot_general(left, right, (((0,), (0,)), ((), ())), preferred_element_type=f32)


def contract_cols(left, right):
    return lax.dot_general(left, right, (((1,), (1,)), ((), ())), preferred_element_type=f32)


def shift(values, axes, step):
    size = lax.axis_size(axes)
    return lax.ppermute(values, axes, [(i, (i + step) % size) for i in range(size)])


def columns(values, share):
    even = jnp.concatenate([values[..., :share], values[..., 2 * share : 3 * share]], axis=-1)
    odd = jnp.concatenate([values[..., share : 2 * share], values[..., 3 * share :]], axis=-1)
    return even, odd


vmem = pl.BlockSpec(memory_space=pltpu.VMEM)
smem = pl.BlockSpec(memory_space=pltpu.SMEM)
hbm = pl.BlockSpec(memory_space=pl.ANY)


def call(kernel, outs, in_specs, scratch=(), limit=16):
    return pl.pallas_call(
        kernel,
        out_shape=outs,
        in_specs=in_specs,
        out_specs=[vmem] * len(outs),
        scratch_shapes=scratch,
        cost_estimate=pl.CostEstimate(flops=1000, bytes_accessed=1000, transcendentals=0),
        compiler_params=pltpu.CompilerParams(vmem_limit_bytes=limit * 1024 * 1024),
    )


def shape(*dims, dtype=f32):
    return jax.ShapeDtypeStruct(dims, dtype)


def forward_kernel(
    at, hidden, gain, bias, fc1, fc1_bias, fc2, pre, scaled, inverse, keep, send, w1, w2, sems
):
    first = pltpu.make_async_copy(fc1, w1, sems.at[0])
    second = pltpu.make_async_copy(fc2, w2, sems.at[1])
    first.start()
    second.start()
    normed, scaled[...], inverse[...] = normalize(hidden[...], gain[...], bias[...])
    normed = normed.astype(bf16)
    first.wait()
    value = contract_cols(normed, w1[...]) + fc1_bias[...]
    pre[...] = value
    act = jax.nn.gelu(value, approximate=True).astype(bf16)
    second.wait()
    half = hidden.shape[0] // 2
    low = jnp.dot(act[:half], w2[...], preferred_element_type=f32)
    high = jnp.dot(act[half:], w2[...], preferred_element_type=f32)
    core = at[1] == 0
    keep[...] = jnp.where(core, low, high)
    send[...] = jnp.where(core, high, low).astype(bf16)


def divide_kernel(at, kept, got, keep, send):
    total = kept[...] + got[...].astype(f32)
    half = keep.shape[0]
    low, high = total[:half], total[half:]
    side = at[0] == 0
    keep[...] = jnp.where(side, low, high)
    send[...] = jnp.where(side, high, low).astype(bf16)


def embed_kernel(
    at, kept, got, hidden, gain, bias, head, unit, direct, inverse_embed, scaled, inverse
):
    rows = kept.shape[0]
    first = pl.multiple_of((at[1] * 2 + at[0]) * rows, rows)
    mixed = hidden[pl.ds(first, rows), :] + (kept[...] + got[...].astype(f32))
    normed, scaled[...], inverse[...] = normalize(mixed, gain[...], bias[...])
    embed = jnp.dot(normed.astype(bf16), head[...], preferred_element_type=f32)
    level = lax.rsqrt(jnp.sum(embed * embed, axis=-1, keepdims=True) + eps)
    inverse_embed[...] = level
    direct[...] = embed * level
    unit[...] = (embed * level).astype(bf16)


def stack_kernel(*refs):
    rows = refs[0].shape[0]
    for index, ref in enumerate(refs[:-1]):
        refs[-1][index * rows : (index + 1) * rows, :] = ref[...]


def pairs_kernel(
    at, level, images, own, other, link, unit, inverse, coef, keep, send, *, chunk, quarter
):
    scale, offset = level[0], level[1]
    half = own.shape[0]
    diagonal = (at[2] * 2 + at[0]) * quarter
    for first in range(0, images.shape[0], chunk):
        rows = slice(first, first + chunk)
        wide = images[rows, :].astype(f32)
        size = lax.rsqrt(jnp.sum(wide * wide, axis=-1, keepdims=True) + eps)
        inverse[rows, :] = size
        low = (wide * size).astype(bf16)
        unit[rows, :] = low
        chance = jax.nn.sigmoid(scale * contract_cols(low, own[...]) + offset)
        line = lax.broadcasted_iota(jnp.int32, chance.shape, 0) + (first - diagonal)
        cols = lax.broadcasted_iota(jnp.int32, chance.shape, 1)
        ident = ((line == cols) & (cols < quarter)).astype(f32)
        coef[rows, :half] = (scale * (chance - ident)).astype(bf16)
        chance = jax.nn.sigmoid(scale * contract_cols(low, other[...]) + offset)
        coef[rows, half:] = (scale * chance).astype(bf16)
    keep[...] = contract_rows(coef[:, :half], unit[...])
    send[...] = contract_rows(coef[:, half:], unit[...]).astype(bf16)


def images_kernel(images, inverse, coef, own, other, part, *, chunk):
    half = own.shape[0]
    for first in range(0, images.shape[0], chunk):
        rows = slice(first, first + chunk)
        grad = jnp.dot(coef[rows, :half], own[...], preferred_element_type=f32)
        grad = grad + jnp.dot(coef[rows, half:], other[...], preferred_element_type=f32)
        level = inverse[rows, :]
        direct = images[rows, :].astype(f32) * level
        inner = jnp.sum(direct * grad, axis=-1, keepdims=True)
        part[rows, :] = ((grad - direct * inner) * level).astype(bf16)


def split_kernel(kept, got, near, *far):
    rows = near.shape[0]
    near[...] = kept[:rows, :] + got[:rows, :].astype(f32)
    for index, ref in enumerate(far):
        part = slice((index + 1) * rows, (index + 2) * rows)
        ref[...] = (kept[part, :] + got[part, :].astype(f32)).astype(bf16)


def join_kernel(near, first, second, third, keep, send):
    total = near[...] + first[...].astype(f32) + second[...].astype(f32) + third[...].astype(f32)
    half = keep.shape[0]
    keep[...] = total[:half]
    send[...] = total[half:].astype(bf16)


def head_kernel(kept, got, direct, inverse_embed, head, gain, scaled, inverse, grad):
    upstream = kept[...] + got[...].astype(f32)
    text_dir = direct[...]
    inner = jnp.sum(text_dir * upstream, axis=-1, keepdims=True)
    grad_embed = ((upstream - text_dir * inner) * inverse_embed[...]).astype(bf16)
    grad_normed = contract_cols(grad_embed, head[...])
    grad[...] = norm_back(grad_normed, gain[...], scaled[...], inverse[...]).astype(bf16)


def backward_kernel(
    at, grad, pre, scaled, inverse, gain, fc1, fc2, keep, send, rest, w1, w2, sems
):
    first = pltpu.make_async_copy(fc1, w1, sems.at[0])
    second = pltpu.make_async_copy(fc2, w2, sems.at[1])
    second.start()
    first.start()
    share = grad.shape[1] // 4
    core = at[1] == 0
    own = jnp.where(core, *columns(grad[...], share))
    rest[...] = jnp.where(at[0] == 0, own[:, :share], own[:, share:])
    slope = gelu_slope(pre[...])
    second.wait()
    grad_pre = (contract_cols(grad[...], w2[...]) * slope).astype(bf16)
    first.wait()
    part = jnp.dot(grad_pre, w1[...], preferred_element_type=f32)
    part = norm_back(part, gain[...], scaled[...], inverse[...])
    even, odd = columns(part, share)
    keep[...] = jnp.where(core, even, odd)
    send[...] = jnp.where(core, odd, even).astype(bf16)


def halve_kernel(at, kept, got, keep, send):
    total = kept[...].astype(f32)
    if got is not None:
        total = total + got[...].astype(f32)
    half = keep.shape[1]
    low, high = total[:, :half], total[:, half:]
    side = at[0] == 0
    keep[...] = jnp.where(side, low, high)
    send[...] = jnp.where(side, high, low).astype(bf16)


def hidden_kernel(kept, got, rest, out):
    out[...] = rest[...].astype(f32) + (kept[...] + got[...].astype(f32))


def core_kernel(at, kept, got, keep, send):
    total = kept[...] + got[...].astype(f32)
    half = keep.shape[1]
    low, high = total[:, :half], total[:, half:]
    core = at[1] == 0
    keep[...] = jnp.where(core, low, high)
    send[...] = jnp.where(core, high, low).astype(bf16)


def rows_kernel(at, kept, got, out):
    half = kept.shape[0]
    core = at[1] == 0
    own, other = kept[...], got[...].astype(f32)
    out[:half, :] = jnp.where(core, own, other)
    out[half:, :] = jnp.where(core, other, own)


def shards(
    images,
    hidden_in,
    norm1_gain,
    norm1_bias,
    fc1,
    fc1_bias,
    fc2,
    norm2_gain,
    norm2_bias,
    head,
    log_scale,
    logit_bias,
):
    block, width = images.shape
    quarter = block // 4
    share = width // 4
    units = fc1.shape[1]
    half = block // 2
    z_at, yl_at, c_at = (lax.axis_index(a) for a in ("z", "yl", "c"))
    at = jnp.stack([yl_at, c_at, z_at]).astype(jnp.int32)
    level = jnp.concatenate([jnp.exp(log_scale), logit_bias])
    fc1 = fc1.T

    own_images = lax.dynamic_slice_in_dim(images, c_at * half, half, 0)
    own_images, hidden_in = lax.optimization_barrier((own_images, hidden_in))
    image_rows = lax.all_gather(own_images, "z", axis=0, tiled=True)

    weights = [
        pltpu.VMEM((units, width), bf16),
        pltpu.VMEM((units, width), bf16),
        pltpu.SemaphoreType.DMA((2,)),
    ]
    pre, scaled_in, inverse_in, keep, send = call(
        forward_kernel,
        [
            shape(block, units),
            shape(block, width),
            shape(block, 1),
            shape(half, width),
            shape(half, width, dtype=bf16),
        ],
        [smem, vmem, vmem, vmem, hbm, vmem, hbm],
        weights,
    )(at, hidden_in, norm1_gain, norm1_bias, fc1, fc1_bias, fc2)
    keep, send = call(
        divide_kernel,
        [shape(quarter, width), shape(quarter, width, dtype=bf16)],
        [smem, vmem, vmem],
    )(at, keep, shift(send, "c", 1))
    text_unit, text_dir, inverse_embed, scaled_out, inverse_out = call(
        embed_kernel,
        [
            shape(quarter, width, dtype=bf16),
            shape(quarter, width),
            shape(quarter, 1),
            shape(quarter, width),
            shape(quarter, 1),
        ],
        [smem] + [vmem] * 6,
    )(at, keep, shift(send, "yl", 1), hidden_in, norm2_gain, norm2_bias, head)

    near = call(stack_kernel, [shape(half, width, dtype=bf16)], [vmem] * 2)(
        text_unit, shift(text_unit, "yh", 1)
    )[0]
    own = call(stack_kernel, [shape(4 * half, width, dtype=bf16)], [vmem] * 4)(
        near, *(shift(near, "x", hop) for hop in hops[1:])
    )[0]
    other = shift(own, "c", 1)

    many = image_rows.shape[0]
    link = image_rows[:16, :128]
    for _ in range(2):
        link = shift(link, "c", 1)
    image_unit, inverse_image, coef, keep, send = call(
        functools.partial(pairs_kernel, chunk=many // 3, quarter=quarter),
        [
            shape(many, width, dtype=bf16),
            shape(many, 1),
            shape(many, 8 * half, dtype=bf16),
            shape(4 * half, width),
            shape(4 * half, width, dtype=bf16),
        ],
        [smem, smem] + [vmem] * 4,
        limit=24,
    )(at, level, image_rows, own, other, link)
    got = shift(send, "c", 1)
    near, *far = call(
        split_kernel,
        [shape(half, width)] + [shape(half, width, dtype=bf16)] * 3,
        [vmem] * 2,
    )(keep, got)
    far = [shift(far[index], "x", 4 - hop) for index, hop in enumerate(hops[1:])]

    image_part = call(
        functools.partial(images_kernel, chunk=many // 3),
        [shape(many, width, dtype=bf16)],
        [vmem] * 5,
        limit=24,
    )(image_rows, inverse_image, coef, own, other)[0]
    far, image_part = lax.optimization_barrier((far, image_part))
    image_part = lax.psum_scatter(image_part, "z", scatter_dimension=0, tiled=True)

    keep, send = call(
        join_kernel,
        [shape(quarter, width), shape(quarter, width, dtype=bf16)],
        [vmem] * 4,
    )(near, *far)
    grad_mixed = call(head_kernel, [shape(quarter, width, dtype=bf16)], [vmem] * 8)(
        keep,
        shift(send, "yh", 1),
        text_dir,
        inverse_embed,
        head,
        norm2_gain,
        scaled_out,
        inverse_out,
    )[0]
    grad_mixed = lax.all_gather(grad_mixed, ("c", "yl"), axis=0, tiled=True)
    keep, send, rest = call(
        backward_kernel,
        [
            shape(block, 2 * share),
            shape(block, 2 * share, dtype=bf16),
            shape(block, share, dtype=bf16),
        ],
        [smem, vmem, vmem, vmem, vmem, vmem, hbm, hbm],
        weights,
    )(at, grad_mixed, pre, scaled_in, inverse_in, norm1_gain, fc1, fc2)
    keep, send = call(
        halve_kernel,
        [shape(block, share), shape(block, share, dtype=bf16)],
        [smem, vmem, vmem],
    )(at, keep, shift(send, "c", 1))
    grad_hidden = call(hidden_kernel, [shape(block, share)], [vmem] * 3)(
        keep, shift(send, "yl", 1), rest
    )[0]

    keep, send = call(
        lambda at, kept, *out: halve_kernel(at, kept, None, *out),
        [shape(half, 2 * share), shape(half, 2 * share, dtype=bf16)],
        [smem, vmem],
    )(at, image_part)
    keep, send = call(
        core_kernel,
        [shape(half, share), shape(half, share, dtype=bf16)],
        [smem, vmem, vmem],
    )(at, keep, shift(send, "yl", 1))
    grad_images = call(rows_kernel, [shape(block, share)], [smem, vmem, vmem])(
        at, keep, shift(send, "c", 1)
    )[0]
    return (grad_images, grad_hidden)


def solution(mesh):
    grid = Mesh(mesh.devices.reshape(8, 4, 2, 2, 2), ("z", "x", "yh", "yl", "c"))
    dp, mp = ("z", "x", "yh"), ("yl", "c")
    placed = (
        P(dp, None),
        P(dp, None),
        P(),
        P(),
        P(None, mp),
        P(mp),
        P(mp, None),
        P(),
        P(),
        P(),
        P(),
        P(),
    )
    return jax.shard_map(
        shards,
        mesh=grid,
        in_specs=placed,
        out_specs=(P(dp, mp), P(dp, mp)),
        check_vma=False,
    )
```

```python
import functools

import jax
import jax.numpy as jnp
from jax import lax
from jax.experimental import pallas as pl
from jax.experimental.pallas import tpu as pltpu
from jax.sharding import Mesh, PartitionSpec as P

eps = 1e-06
hops = (0, 1, 3, 2)
f32 = jnp.float32
bf16 = jnp.bfloat16


def normalize(values, gain, shift):
    mean = jnp.mean(values, axis=-1, keepdims=True)
    centered = values - mean
    inverse = lax.rsqrt(jnp.mean(centered * centered, axis=-1, keepdims=True) + eps)
    scaled = centered * inverse
    return (scaled * gain + shift, scaled, inverse)


def gelu_slope(values):
    factor = 0.7978845608028654
    inner = factor * (values + 0.044715 * values * values * values)
    tangent = jnp.tanh(inner)
    return 0.5 * (1.0 + tangent) + 0.5 * values * (1.0 - tangent * tangent) * factor * (
        1.0 + 3.0 * 0.044715 * values * values
    )


def norm_back(upstream, gain, scaled, inverse):
    grad = upstream * gain
    return inverse * (
        grad
        - jnp.mean(grad, axis=-1, keepdims=True)
        - scaled * jnp.mean(grad * scaled, axis=-1, keepdims=True)
    )


def contract_rows(left, right):
    return lax.dot_general(left, right, (((0,), (0,)), ((), ())), preferred_element_type=f32)


def contract_cols(left, right):
    return lax.dot_general(left, right, (((1,), (1,)), ((), ())), preferred_element_type=f32)


def shift(values, axes, step):
    size = lax.axis_size(axes)
    return lax.ppermute(values, axes, [(i, (i + step) % size) for i in range(size)])


def columns(values, share):
    even = jnp.concatenate([values[..., :share], values[..., 2 * share : 3 * share]], axis=-1)
    odd = jnp.concatenate([values[..., share : 2 * share], values[..., 3 * share :]], axis=-1)
    return even, odd


vmem = pl.BlockSpec(memory_space=pltpu.VMEM)
smem = pl.BlockSpec(memory_space=pltpu.SMEM)
hbm = pl.BlockSpec(memory_space=pltpu.HBM)


def call(kernel, outs, in_specs, scratch=(), limit=6, out_specs=None):
    return pl.pallas_call(
        kernel,
        out_shape=outs,
        in_specs=in_specs,
        out_specs=out_specs or [vmem] * len(outs),
        scratch_shapes=scratch,
        cost_estimate=pl.CostEstimate(flops=1000, bytes_accessed=1000, transcendentals=0),
        compiler_params=pltpu.CompilerParams(vmem_limit_bytes=limit * 1024 * 1024),
    )


def shape(*dims, dtype=f32):
    return jax.ShapeDtypeStruct(dims, dtype)


def forward_kernel(
    at, hidden, gain, bias, fc1, fc1_bias, fc2, pre, scaled, keep, send_c, send_y, send_b,
    rows, line1, line2, line3, w1, w2, value, norm, part, sems,
):
    loads = [
        pltpu.make_async_copy(source, target, sems.at[index])
        for index, (source, target) in enumerate(
            [(hidden, rows), (gain, line1), (bias, line2), (fc1, w1), (fc1_bias, line3), (fc2, w2)]
        )
    ]
    for load in loads:
        load.start()
    for load in loads[:3]:
        load.wait()
    units = fc1.shape[0]
    normed, norm[...], inverse = normalize(rows[...], line1[...], line2[...])
    normed = normed.astype(bf16)
    save_norm = pltpu.make_async_copy(norm, scaled, sems.at[6])
    save_norm.start()
    loads[3].wait()
    loads[4].wait()
    linear = contract_cols(normed, w1[...]) + line3[...]
    value[:, :units] = linear
    value[:, units : units + 1] = inverse
    save_pre = pltpu.make_async_copy(value, pre, sems.at[7])
    save_pre.start()
    act = jax.nn.gelu(linear, approximate=True).astype(bf16)
    loads[5].wait()
    part[...] = jnp.dot(act, w2[...], preferred_element_type=f32)
    quarter = keep.shape[0]
    side, core = at[0], at[1]

    def own(core, side):
        return pl.ds(pl.multiple_of((core * 2 + side) * quarter, quarter), quarter)

    keep[...] = rows[own(core, side), :] + part[own(core, side), :]
    send_c[...] = part[own(1 - core, side), :].astype(bf16)
    send_y[...] = part[own(core, 1 - side), :].astype(bf16)
    send_b[...] = part[own(1 - core, 1 - side), :].astype(bf16)
    save_norm.wait()
    save_pre.wait()


def embed_kernel(kept, got_c, got_y, got_b, gain, bias, head, unit, state):
    width = unit.shape[1]
    mixed = kept[...] + got_c[...].astype(f32) + got_y[...].astype(f32) + got_b[...].astype(f32)
    normed, scaled, inverse = normalize(mixed, gain[...], bias[...])
    state[:, width : 2 * width] = scaled
    embed = jnp.dot(normed.astype(bf16), head[...], preferred_element_type=f32)
    level = lax.rsqrt(jnp.sum(embed * embed, axis=-1, keepdims=True) + eps)
    unit[...] = (embed * level).astype(bf16)
    state[:, :width] = embed * level
    state[:, 2 * width : 2 * width + 1] = level
    state[:, 2 * width + 1 : 2 * width + 2] = inverse


def stack_kernel(*refs, count):
    rows = refs[0].shape[0]
    for index, ref in enumerate(refs[:count]):
        refs[-1][index * rows : (index + 1) * rows, :] = ref[...]


def pairs_kernel(
    at, level, images, own, other, wide_rows, inverse, coef, keep, send, unit, sems, *, chunk, quarter
):
    scale, offset = level[0], level[1]
    half = own.shape[0]
    diagonal = (at[2] * 2 + at[0]) * quarter
    count = images.shape[0] // chunk
    loads = []
    for index in range(count):
        rows = pl.ds(index * chunk, chunk)
        loads.append(
            pltpu.make_async_copy(images.at[rows], wide_rows.at[rows], sems.at[index])
        )
        loads[-1].start()
    for index in range(count):
        first = index * chunk
        rows = slice(first, first + chunk)
        loads[index].wait()
        wide = wide_rows[rows, :].astype(f32)
        size = lax.rsqrt(jnp.sum(wide * wide, axis=-1, keepdims=True) + eps)
        inverse[rows, :] = size
        low = (wide * size).astype(bf16)
        unit[rows, :] = low
        chance = jax.nn.sigmoid(scale * contract_cols(low, own[...]) + offset)
        line = lax.broadcasted_iota(jnp.int32, chance.shape, 0) + (first - diagonal)
        cols = lax.broadcasted_iota(jnp.int32, chance.shape, 1)
        ident = ((line == cols) & (cols < quarter)).astype(f32)
        coef[rows, :half] = (scale * (chance - ident)).astype(bf16)
        chance = jax.nn.sigmoid(scale * contract_cols(low, other[...]) + offset)
        coef[rows, half:] = (scale * chance).astype(bf16)
    send[...] = contract_rows(coef[:, half:], unit[...]).astype(bf16)
    keep[...] = contract_rows(coef[:, :half], unit[...])


def images_kernel(images, inverse, coef, own, other, part, value, sems, *, chunk):
    half = own.shape[0]
    saves = []
    for index in range(images.shape[0] // chunk):
        rows = slice(index * chunk, (index + 1) * chunk)
        grad = jnp.dot(coef[rows, :half], own[...], preferred_element_type=f32)
        grad = grad + jnp.dot(coef[rows, half:], other[...], preferred_element_type=f32)
        level = inverse[rows, :]
        direct = images[rows, :].astype(f32) * level
        inner = jnp.sum(direct * grad, axis=-1, keepdims=True)
        value[rows, :] = ((grad - direct * inner) * level).astype(bf16)
        place = pl.ds(index * chunk, chunk)
        saves.append(pltpu.make_async_copy(value.at[place], part.at[place], sems.at[index]))
        saves[-1].start()
    for save in saves:
        save.wait()


def split_kernel(kept, got, after, near, *far):
    rows = near.shape[0]
    near[...] = kept[:rows, :] + got[:rows, :].astype(f32)
    for index, ref in enumerate(far):
        part = slice((index + 1) * rows, (index + 2) * rows)
        ref[...] = (kept[part, :] + got[part, :].astype(f32)).astype(bf16)


def join_kernel(near, first, second, third, keep, send):
    total = near[...] + first[...].astype(f32) + second[...].astype(f32) + third[...].astype(f32)
    half = keep.shape[0]
    keep[...] = total[:half]
    send[...] = total[half:].astype(bf16)


def head_kernel(kept, got, state, head, gain, grad):
    width = grad.shape[1]
    upstream = kept[...] + got[...].astype(f32)
    text_dir = state[:, :width]
    inner = jnp.sum(text_dir * upstream, axis=-1, keepdims=True)
    grad_embed = (upstream - text_dir * inner) * state[:, 2 * width : 2 * width + 1]
    grad_normed = contract_cols(grad_embed.astype(bf16), head[...])
    scaled, inverse = state[:, width : 2 * width], state[:, 2 * width + 1 : 2 * width + 2]
    grad[...] = norm_back(grad_normed, gain[...], scaled, inverse).astype(bf16)


def backward_kernel(
    at, gathered, pre, scaled, gain, fc1, fc2, keep, send, rest, value, norm, sems
):
    load_pre = pltpu.make_async_copy(pre, value, sems.at[0])
    load_norm = pltpu.make_async_copy(scaled, norm, sems.at[1])
    load_pre.start()
    load_norm.start()
    quarter = gathered.shape[0] // 4
    first, second, third, fourth = (
        gathered[index * quarter : (index + 1) * quarter, :] for index in range(4)
    )
    grad = jnp.concatenate([first, third, second, fourth], axis=0)
    share = grad.shape[1] // 4
    units = fc1.shape[0]
    core = at[1] == 0
    own = jnp.where(core, *columns(grad, share))
    rest[...] = jnp.where(at[0] == 0, own[:, :share], own[:, share:])
    grad_act = contract_cols(grad, fc2[...])
    load_pre.wait()
    grad_pre = (grad_act * gelu_slope(value[:, :units])).astype(bf16)
    part = jnp.dot(grad_pre, fc1[...], preferred_element_type=f32)
    load_norm.wait()
    part = norm_back(part, gain[...], norm[...], value[:, units : units + 1])
    even, odd = columns(part, share)
    keep[...] = jnp.where(core, even, odd)
    send[...] = jnp.where(core, odd, even).astype(bf16)


def halve_kernel(at, kept, got, keep, send):
    total = kept[...].astype(f32)
    if got is not None:
        total = total + got[...].astype(f32)
    half = keep.shape[1]
    low, high = total[:, :half], total[:, half:]
    side = at[0] == 0
    keep[...] = jnp.where(side, low, high)
    send[...] = jnp.where(side, high, low).astype(bf16)


def hidden_kernel(kept, got, rest, out):
    out[...] = rest[...].astype(f32) + (kept[...] + got[...].astype(f32))


def core_kernel(at, kept, got, keep, send):
    total = kept[...] + got[...].astype(f32)
    half = keep.shape[1]
    low, high = total[:, :half], total[:, half:]
    core = at[1] == 0
    keep[...] = jnp.where(core, low, high)
    send[...] = jnp.where(core, high, low).astype(bf16)


def rows_kernel(at, kept, got, out):
    half = kept.shape[0]
    core = at[1] == 0
    own, other = kept[...], got[...].astype(f32)
    out[:half, :] = jnp.where(core, own, other)
    out[half:, :] = jnp.where(core, other, own)


def shards(
    images,
    hidden_in,
    norm1_gain,
    norm1_bias,
    fc1,
    fc1_bias,
    fc2,
    norm2_gain,
    norm2_bias,
    head,
    log_scale,
    logit_bias,
):
    block, width = images.shape
    quarter = block // 4
    share = width // 4
    units = fc1.shape[1]
    half = block // 2
    z_at, yl_at, c_at = (lax.axis_index(a) for a in ("z", "yl", "c"))
    at = jnp.stack([yl_at, c_at, z_at]).astype(jnp.int32)
    level = jnp.concatenate([jnp.exp(log_scale), logit_bias])
    fc1 = fc1.T

    own_images = lax.dynamic_slice_in_dim(images, c_at * half, half, 0)
    own_images, hidden_in = lax.optimization_barrier((own_images, hidden_in))
    image_rows = lax.all_gather(own_images, "z", axis=0, tiled=True)

    pad = (units // 128 + 1) * 128
    pre, scaled_in, keep, *sends = call(
        forward_kernel,
        [shape(block, pad), shape(block, width), shape(quarter, width)]
        + [shape(quarter, width, dtype=bf16)] * 3,
        [smem] + [hbm] * 6,
        [
            pltpu.VMEM((block, width), f32),
            pltpu.VMEM((width,), f32),
            pltpu.VMEM((width,), f32),
            pltpu.VMEM((units,), f32),
            pltpu.VMEM((units, width), bf16),
            pltpu.VMEM((units, width), bf16),
            pltpu.VMEM((block, pad), f32),
            pltpu.VMEM((block, width), f32),
            pltpu.VMEM((block, width), f32),
            pltpu.SemaphoreType.DMA((8,)),
        ],
        limit=20,
        out_specs=[hbm] * 2 + [vmem] * 4,
    )(at, hidden_in, norm1_gain, norm1_bias, fc1, fc1_bias, fc2)
    text_unit, state = call(
        embed_kernel,
        [shape(quarter, width, dtype=bf16), shape(quarter, 2 * width + 128)],
        [vmem] * 7,
        limit=10,
    )(
        keep,
        *(
            lax.ppermute(send, ("yl", "c"), [(i, i ^ bits) for i in range(4)])
            for send, bits in zip(sends, (1, 2, 3))
        ),
        norm2_gain,
        norm2_bias,
        head,
    )

    near = call(
        functools.partial(stack_kernel, count=2), [shape(half, width, dtype=bf16)], [vmem] * 2
    )(text_unit, shift(text_unit, "yh", 1))[0]
    own = call(
        functools.partial(stack_kernel, count=4),
        [shape(4 * half, width, dtype=bf16)],
        [vmem] * 4 + [hbm],
    )(near, *(shift(near, "x", hop) for hop in hops[1:]), image_rows)[0]
    other = shift(own, "c", 1)

    many = image_rows.shape[0]
    parts = 3
    image_wide, inverse_image, coef, keep, send = call(
        functools.partial(pairs_kernel, chunk=many // parts, quarter=quarter),
        [
            shape(many, width, dtype=bf16),
            shape(many, 1),
            shape(many, 8 * half, dtype=bf16),
            shape(4 * half, width),
            shape(4 * half, width, dtype=bf16),
        ],
        [smem, smem, hbm, vmem, vmem],
        [pltpu.VMEM((many, width), bf16), pltpu.SemaphoreType.DMA((parts,))],
        limit=20,
    )(at, level, image_rows, own, other)
    got = shift(send, "c", 1)
    image_part = call(
        functools.partial(images_kernel, chunk=many // parts),
        [shape(many, width, dtype=bf16)],
        [vmem] * 5,
        [pltpu.VMEM((many, width), bf16), pltpu.SemaphoreType.DMA((parts,))],
        limit=16,
        out_specs=[hbm],
    )(image_wide, inverse_image, coef, own, other)[0]
    near, *far = call(
        split_kernel,
        [shape(half, width)] + [shape(half, width, dtype=bf16)] * 3,
        [vmem] * 2 + [hbm],
    )(keep, got, image_part)
    far = [shift(far[index], "x", 4 - hop) for index, hop in enumerate(hops[1:])]

    image_part = lax.psum_scatter(image_part, "z", scatter_dimension=0, tiled=True)

    keep, send = call(
        join_kernel,
        [shape(quarter, width), shape(quarter, width, dtype=bf16)],
        [vmem] * 4,
    )(near, *far)
    grad_mixed = call(
        head_kernel, [shape(quarter, width, dtype=bf16)], [vmem] * 5, limit=10
    )(keep, shift(send, "yh", 1), state, head, norm2_gain)[0]
    grad_mixed = lax.all_gather(grad_mixed, ("yl", "c"), axis=0, tiled=True)
    keep, send, rest = call(
        backward_kernel,
        [
            shape(block, 2 * share),
            shape(block, 2 * share, dtype=bf16),
            shape(block, share, dtype=bf16),
        ],
        [smem, vmem, hbm, hbm, vmem, vmem, vmem],
        [
            pltpu.VMEM((block, pad), f32),
            pltpu.VMEM((block, width), f32),
            pltpu.SemaphoreType.DMA((2,)),
        ],
        limit=16,
    )(at, grad_mixed, pre, scaled_in, norm1_gain, fc1, fc2)
    keep, send = call(
        halve_kernel,
        [shape(block, share), shape(block, share, dtype=bf16)],
        [smem, vmem, vmem],
    )(at, keep, shift(send, "c", 1))
    grad_hidden = call(hidden_kernel, [shape(block, share)], [vmem] * 3)(
        keep, shift(send, "yl", 1), rest
    )[0]

    keep, send = call(
        lambda at, kept, *out: halve_kernel(at, kept, None, *out),
        [shape(half, 2 * share), shape(half, 2 * share, dtype=bf16)],
        [smem, vmem],
    )(at, image_part)
    keep, send = call(
        core_kernel,
        [shape(half, share), shape(half, share, dtype=bf16)],
        [smem, vmem, vmem],
    )(at, keep, shift(send, "yl", 1))
    grad_images = call(rows_kernel, [shape(block, share)], [smem, vmem, vmem])(
        at, keep, shift(send, "c", 1)
    )[0]
    return (grad_images, grad_hidden)


def solution(mesh):
    grid = Mesh(mesh.devices.reshape(8, 4, 2, 2, 2), ("z", "x", "yh", "yl", "c"))
    dp, mp = ("z", "x", "yh"), ("yl", "c")
    placed = (
        P(dp, None),
        P(dp, None),
        P(),
        P(),
        P(None, mp),
        P(mp),
        P(mp, None),
        P(),
        P(),
        P(),
        P(),
        P(),
    )
    return jax.shard_map(
        shards,
        mesh=grid,
        in_specs=placed,
        out_specs=(P(dp, mp), P(dp, mp)),
        check_vma=False,
    )
```

```python
import functools

import jax
import jax.numpy as jnp
from jax import lax
from jax.experimental import pallas as pl
from jax.experimental.pallas import tpu as pltpu
from jax.sharding import Mesh, PartitionSpec as P

eps = 1e-06
hops = (0, 1, 3, 2)
f32 = jnp.float32
bf16 = jnp.bfloat16


def normalize(values, gain, shift):
    mean = jnp.mean(values, axis=-1, keepdims=True)
    centered = values - mean
    inverse = lax.rsqrt(jnp.mean(centered * centered, axis=-1, keepdims=True) + eps)
    scaled = centered * inverse
    return (scaled * gain + shift, scaled, inverse)


def gelu_slope(values):
    factor = 0.7978845608028654
    inner = factor * (values + 0.044715 * values * values * values)
    tangent = jnp.tanh(inner)
    return 0.5 * (1.0 + tangent) + 0.5 * values * (1.0 - tangent * tangent) * factor * (
        1.0 + 3.0 * 0.044715 * values * values
    )


def norm_back(upstream, gain, scaled, inverse):
    grad = upstream * gain
    return inverse * (
        grad
        - jnp.mean(grad, axis=-1, keepdims=True)
        - scaled * jnp.mean(grad * scaled, axis=-1, keepdims=True)
    )


def contract_rows(left, right):
    return lax.dot_general(left, right, (((0,), (0,)), ((), ())), preferred_element_type=f32)


def contract_cols(left, right):
    return lax.dot_general(left, right, (((1,), (1,)), ((), ())), preferred_element_type=f32)


def shift(values, axes, step):
    size = lax.axis_size(axes)
    return lax.ppermute(values, axes, [(i, (i + step) % size) for i in range(size)])


def columns(values, share):
    even = jnp.concatenate([values[..., :share], values[..., 2 * share : 3 * share]], axis=-1)
    odd = jnp.concatenate([values[..., share : 2 * share], values[..., 3 * share :]], axis=-1)
    return even, odd


vmem = pl.BlockSpec(memory_space=pltpu.VMEM)
smem = pl.BlockSpec(memory_space=pltpu.SMEM)
hbm = pl.BlockSpec(memory_space=pltpu.HBM)
anywhere = pl.BlockSpec(memory_space=pl.ANY)


def call(kernel, outs, in_specs, scratch=(), limit=6, out_specs=None, first=False):
    if first:
        body = kernel

        def kernel(*refs):
            inputs = len(in_specs)
            body(*refs[:inputs], refs[-1], *refs[inputs:-1])

    return pl.pallas_call(
        kernel,
        out_shape=outs,
        in_specs=in_specs,
        out_specs=out_specs or [vmem] * len(outs),
        scratch_shapes=scratch,
        cost_estimate=pl.CostEstimate(flops=1000, bytes_accessed=1000, transcendentals=0),
        compiler_params=pltpu.CompilerParams(vmem_limit_bytes=limit * 1024 * 1024),
    )


def shape(*dims, dtype=f32):
    return jax.ShapeDtypeStruct(dims, dtype)


def forward_kernel(
    at, hidden, gain, bias, fc1, fc1_bias, fc2, pre, scaled, keep, send_c, send_y, send_b,
    rows, line1, line2, line3, w1, w2, value, norm, part, sems,
):
    loads = [
        pltpu.make_async_copy(source, target, sems.at[index])
        for index, (source, target) in enumerate(
            [(hidden, rows), (gain, line1), (bias, line2), (fc1, w1), (fc1_bias, line3), (fc2, w2)]
        )
    ]
    for load in loads:
        load.start()
    for load in loads[:3]:
        load.wait()
    units = fc1.shape[0]
    normed, norm[...], inverse = normalize(rows[...], line1[...], line2[...])
    normed = normed.astype(bf16)
    save_norm = pltpu.make_async_copy(norm, scaled, sems.at[6])
    save_norm.start()
    loads[3].wait()
    loads[4].wait()
    linear = contract_cols(normed, w1[...]) + line3[...]
    value[:, :units] = linear
    value[:, units : units + 1] = inverse
    save_pre = pltpu.make_async_copy(value, pre, sems.at[7])
    save_pre.start()
    act = jax.nn.gelu(linear, approximate=True).astype(bf16)
    loads[5].wait()
    part[...] = jnp.dot(act, w2[...], preferred_element_type=f32)
    quarter = keep.shape[0]
    side, core = at[0], at[1]

    def own(core, side):
        return pl.ds(pl.multiple_of((core * 2 + side) * quarter, quarter), quarter)

    keep[...] = rows[own(core, side), :] + part[own(core, side), :]
    send_c[...] = part[own(1 - core, side), :].astype(bf16)
    send_y[...] = part[own(core, 1 - side), :].astype(bf16)
    send_b[...] = part[own(1 - core, 1 - side), :].astype(bf16)
    save_norm.wait()
    save_pre.wait()


def embed_kernel(kept, got_c, got_y, got_b, gain, bias, head, unit, state):
    width = unit.shape[1]
    mixed = kept[...] + got_c[...].astype(f32) + got_y[...].astype(f32) + got_b[...].astype(f32)
    normed, scaled, inverse = normalize(mixed, gain[...], bias[...])
    state[:, width : 2 * width] = scaled
    embed = jnp.dot(normed.astype(bf16), head[...], preferred_element_type=f32)
    level = lax.rsqrt(jnp.sum(embed * embed, axis=-1, keepdims=True) + eps)
    unit[...] = (embed * level).astype(bf16)
    state[:, :width] = embed * level
    state[:, 2 * width : 2 * width + 1] = level
    state[:, 2 * width + 1 : 2 * width + 2] = inverse


def stack_kernel(*refs, count):
    rows = refs[0].shape[0]
    for index, ref in enumerate(refs[:count]):
        refs[-1][index * rows : (index + 1) * rows, :] = ref[...]


def pairs_kernel(at, log_scale, offset, *refs, chunk, quarter):
    images, (own, other, unit, inverse, coef, keep, send) = refs[:8], refs[8:]
    scale = jnp.exp(log_scale[...])
    half = own.shape[0]
    size = images[0].shape[0]
    for index, ref in enumerate(images):
        rows = slice(index * size, (index + 1) * size)
        wide = ref[...].astype(f32)
        level = lax.rsqrt(jnp.sum(wide * wide, axis=-1, keepdims=True) + eps)
        inverse[rows, :] = level
        unit[rows, :] = (wide * level).astype(bf16)
    diagonal = 7 * size + at[0] * quarter
    for first in range(0, unit.shape[0], chunk):
        rows = slice(first, first + chunk)
        low = unit[rows, :]
        chance = jax.nn.sigmoid(scale * contract_cols(low, own[...]) + offset[...])
        line = lax.broadcasted_iota(jnp.int32, chance.shape, 0) + (first - diagonal)
        cols = lax.broadcasted_iota(jnp.int32, chance.shape, 1)
        ident = ((line == cols) & (cols < quarter)).astype(f32)
        coef[rows, :half] = (scale * (chance - ident)).astype(bf16)
        chance = jax.nn.sigmoid(scale * contract_cols(low, other[...]) + offset[...])
        coef[rows, half:] = (scale * chance).astype(bf16)
    send[...] = contract_rows(coef[:, half:], unit[...]).astype(bf16)
    keep[...] = contract_rows(coef[:, :half], unit[...])


def images_kernel(inverse, coef, own, other, *refs, first):
    count = (len(refs)) // 2
    images, parts = refs[:count], refs[-count:]
    half = own.shape[0]
    size = images[0].shape[0]
    rows = slice(first * size, (first + count) * size)
    grad = jnp.dot(coef[rows, :half], own[...], preferred_element_type=f32)
    grad = grad + jnp.dot(coef[rows, half:], other[...], preferred_element_type=f32)
    for index, (image, part) in enumerate(zip(images, parts)):
        level = inverse[(first + index) * size : (first + index + 1) * size, :]
        direct = image[...].astype(f32) * level
        piece = grad[index * size : (index + 1) * size]
        inner = jnp.sum(direct * piece, axis=-1, keepdims=True)
        part[...] = ((piece - direct * inner) * level).astype(part.dtype)


def add_kernel(first, second, third, fourth, left, right):
    left[...] = (first[...].astype(f32) + second[...].astype(f32)).astype(bf16)
    right[...] = (third[...].astype(f32) + fourth[...].astype(f32)).astype(bf16)


def split_kernel(kept, got, after, near, *far):
    rows = near.shape[0]
    near[...] = kept[:rows, :] + got[:rows, :].astype(f32)
    for index, ref in enumerate(far):
        part = slice((index + 1) * rows, (index + 2) * rows)
        ref[...] = (kept[part, :] + got[part, :].astype(f32)).astype(bf16)


def join_kernel(near, first, second, third, after, keep, send):
    total = near[...] + first[...].astype(f32) + second[...].astype(f32) + third[...].astype(f32)
    half = keep.shape[0]
    keep[...] = total[:half]
    send[...] = total[half:].astype(bf16)


def head_kernel(kept, got, state, head, gain, grad):
    width = grad.shape[1]
    upstream = kept[...] + got[...].astype(f32)
    text_dir = state[:, :width]
    inner = jnp.sum(text_dir * upstream, axis=-1, keepdims=True)
    grad_embed = (upstream - text_dir * inner) * state[:, 2 * width : 2 * width + 1]
    grad_normed = contract_cols(grad_embed.astype(bf16), head[...])
    scaled, inverse = state[:, width : 2 * width], state[:, 2 * width + 1 : 2 * width + 2]
    grad[...] = norm_back(grad_normed, gain[...], scaled, inverse).astype(bf16)


def backward_kernel(
    at, gathered, pre, scaled, gain, fc1, fc2, keep, send, rest, value, norm, sems
):
    load_pre = pltpu.make_async_copy(pre, value, sems.at[0])
    load_norm = pltpu.make_async_copy(scaled, norm, sems.at[1])
    load_pre.start()
    load_norm.start()
    quarter = gathered.shape[0] // 4
    first, second, third, fourth = (
        gathered[index * quarter : (index + 1) * quarter, :] for index in range(4)
    )
    grad = jnp.concatenate([first, third, second, fourth], axis=0)
    share = grad.shape[1] // 4
    units = fc1.shape[0]
    core = at[1] == 0
    own = jnp.where(core, *columns(grad, share))
    rest[...] = jnp.where(at[0] == 0, own[:, :share], own[:, share:])
    grad_act = contract_cols(grad, fc2[...])
    load_pre.wait()
    grad_pre = (grad_act * gelu_slope(value[:, :units])).astype(bf16)
    part = jnp.dot(grad_pre, fc1[...], preferred_element_type=f32)
    load_norm.wait()
    part = norm_back(part, gain[...], norm[...], value[:, units : units + 1])
    even, odd = columns(part, share)
    keep[...] = jnp.where(core, even, odd)
    send[...] = jnp.where(core, odd, even).astype(bf16)


def halve_kernel(at, kept, *refs):
    keep, send = refs[-2:]
    total = kept[...]
    for ref in refs[:-2]:
        total = total + ref[...].astype(f32)
    half = keep.shape[1]
    low, high = total[:, :half], total[:, half:]
    side = at[0] == 0
    keep[...] = jnp.where(side, low, high)
    send[...] = jnp.where(side, high, low).astype(bf16)


def hidden_kernel(kept, got, rest, out):
    out[...] = rest[...].astype(f32) + (kept[...] + got[...].astype(f32))


def core_kernel(at, kept, got, keep, send):
    total = kept[...] + got[...].astype(f32)
    half = keep.shape[1]
    low, high = total[:, :half], total[:, half:]
    core = at[1] == 0
    keep[...] = jnp.where(core, low, high)
    send[...] = jnp.where(core, high, low).astype(bf16)


def rows_kernel(at, kept, got, out):
    half = kept.shape[0]
    core = at[1] == 0
    own, other = kept[...], got[...].astype(f32)
    out[:half, :] = jnp.where(core, own, other)
    out[half:, :] = jnp.where(core, other, own)


def shards(
    images,
    hidden_in,
    norm1_gain,
    norm1_bias,
    fc1,
    fc1_bias,
    fc2,
    norm2_gain,
    norm2_bias,
    head,
    log_scale,
    logit_bias,
):
    block, width = images.shape
    quarter = block // 4
    share = width // 4
    units = fc1.shape[1]
    half = block // 2
    yl_at, c_at = (lax.axis_index(a) for a in ("yl", "c"))
    at = jnp.stack([yl_at, c_at]).astype(jnp.int32)
    fc1 = fc1.T

    own_images = lax.dynamic_slice_in_dim(images, c_at * half, half, 0)
    below, above = [own_images], [own_images]
    opposite = shift(own_images, "z", 4)
    for _ in range(3):
        below.append(shift(below[-1], "z", 1))
        above.append(shift(above[-1], "z", 7))
    image_rows = [opposite, below[3], above[3], below[2], above[2], below[1], above[1], own_images]

    pad = (units // 128 + 1) * 128
    pre, scaled_in, keep, *sends = call(
        forward_kernel,
        [shape(block, pad), shape(block, width), shape(quarter, width)]
        + [shape(quarter, width, dtype=bf16)] * 3,
        [smem] + [hbm] * 6,
        [
            pltpu.VMEM((block, width), f32),
            pltpu.VMEM((width,), f32),
            pltpu.VMEM((width,), f32),
            pltpu.VMEM((units,), f32),
            pltpu.VMEM((units, width), bf16),
            pltpu.VMEM((units, width), bf16),
            pltpu.VMEM((block, pad), f32),
            pltpu.VMEM((block, width), f32),
            pltpu.VMEM((block, width), f32),
            pltpu.SemaphoreType.DMA((8,)),
        ],
        limit=62,
        out_specs=[hbm] * 2 + [vmem] * 4,
    )(at, hidden_in, norm1_gain, norm1_bias, fc1, fc1_bias, fc2)
    text_unit, state = call(
        embed_kernel,
        [shape(quarter, width, dtype=bf16), shape(quarter, 2 * width + 128)],
        [vmem] * 7,
        limit=10,
    )(
        keep,
        *(
            lax.ppermute(send, ("yl", "c"), [(i, i ^ bits) for i in range(4)])
            for send, bits in zip(sends, (1, 2, 3))
        ),
        norm2_gain,
        norm2_bias,
        head,
    )

    near = call(
        functools.partial(stack_kernel, count=2), [shape(half, width, dtype=bf16)], [vmem] * 2
    )(text_unit, shift(text_unit, "yh", 1))[0]
    own = call(
        functools.partial(stack_kernel, count=4),
        [shape(4 * half, width, dtype=bf16)],
        [vmem] * 4,
    )(near, *(shift(near, "x", hop) for hop in hops[1:]))[0]
    other = shift(own, "c", 1)

    many = 8 * half
    inverse_image, coef, keep, send = call(
        functools.partial(pairs_kernel, chunk=many // 2, quarter=quarter),
        [
            shape(many, 1),
            shape(many, 8 * half, dtype=bf16),
            shape(4 * half, width),
            shape(4 * half, width, dtype=bf16),
        ],
        [smem] + [vmem] * 12,
        [pltpu.VMEM((many, width), bf16)],
        limit=20,
        first=True,
    )(at, log_scale.reshape(1, 1), logit_bias.reshape(1, 1), *image_rows, own, other)
    got = shift(send, "c", 1)

    low = shape(half, width, dtype=bf16)
    parts = call(
        functools.partial(images_kernel, first=0), [low] * 3, [vmem] * 7, limit=12
    )(inverse_image, coef, own, other, *image_rows[:3])
    near, *far = call(
        split_kernel,
        [shape(half, width)] + [low] * 3,
        [vmem] * 2 + [anywhere],
    )(keep, got, parts[0])
    far = [shift(far[index], "x", 4 - hop) for index, hop in enumerate(hops[1:])]
    opposite = shift(parts[0], "z", 4)
    below, above = shift(parts[1], "z", 7), shift(parts[2], "z", 1)
    *parts, image_part = call(
        functools.partial(images_kernel, first=3),
        [low] * 4 + [shape(half, width)],
        [vmem] * 9,
        limit=16,
    )(inverse_image, coef, own, other, *image_rows[3:])
    for index in (0, 2):
        below, above = call(add_kernel, [low] * 2, [vmem] * 4)(
            below, parts[index], above, parts[index + 1]
        )
        below, above = shift(below, "z", 7), shift(above, "z", 1)

    keep, send = call(
        join_kernel,
        [shape(quarter, width), shape(quarter, width, dtype=bf16)],
        [vmem] * 4 + [anywhere],
    )(near, *far, image_part)
    grad_mixed = call(
        head_kernel, [shape(quarter, width, dtype=bf16)], [vmem] * 5, limit=10
    )(keep, shift(send, "yh", 1), state, head, norm2_gain)[0]
    grad_mixed = lax.all_gather(grad_mixed, ("yl", "c"), axis=0, tiled=True)
    keep, send, rest = call(
        backward_kernel,
        [
            shape(block, 2 * share),
            shape(block, 2 * share, dtype=bf16),
            shape(block, share, dtype=bf16),
        ],
        [smem, vmem, hbm, hbm, vmem, vmem, vmem],
        [
            pltpu.VMEM((block, pad), f32),
            pltpu.VMEM((block, width), f32),
            pltpu.SemaphoreType.DMA((2,)),
        ],
        limit=16,
    )(at, grad_mixed, pre, scaled_in, norm1_gain, fc1, fc2)
    keep, send = call(
        halve_kernel,
        [shape(block, share), shape(block, share, dtype=bf16)],
        [smem, vmem, vmem],
    )(at, keep, shift(send, "c", 1))
    grad_hidden = call(hidden_kernel, [shape(block, share)], [vmem] * 3)(
        keep, shift(send, "yl", 1), rest
    )[0]

    keep, send = call(
        halve_kernel,
        [shape(half, 2 * share), shape(half, 2 * share, dtype=bf16)],
        [smem] + [vmem] * 4,
    )(at, image_part, below, above, opposite)
    keep, send = call(
        core_kernel,
        [shape(half, share), shape(half, share, dtype=bf16)],
        [smem, vmem, vmem],
    )(at, keep, shift(send, "yl", 1))
    grad_images = call(rows_kernel, [shape(block, share)], [smem, vmem, vmem])(
        at, keep, shift(send, "c", 1)
    )[0]
    return (grad_images, grad_hidden)


def solution(mesh):
    grid = Mesh(mesh.devices.reshape(8, 4, 2, 2, 2), ("z", "x", "yh", "yl", "c"))
    dp, mp = ("z", "x", "yh"), ("yl", "c")
    placed = (
        P(dp, None),
        P(dp, None),
        P(),
        P(),
        P(None, mp),
        P(mp),
        P(mp, None),
        P(),
        P(),
        P(),
        P(),
        P(),
    )
    return jax.shard_map(
        shards,
        mesh=grid,
        in_specs=placed,
        out_specs=(P(dp, mp), P(dp, mp)),
        check_vma=False,
    )
```

```python
import functools

import jax
import jax.numpy as jnp
from jax import lax
from jax.experimental import pallas as pl
from jax.experimental.pallas import tpu as pltpu
from jax.sharding import Mesh, PartitionSpec as P

eps = 1e-06
hops = (0, 1, 3, 2)
f32 = jnp.float32
bf16 = jnp.bfloat16


def normalize(values, gain, shift):
    mean = jnp.mean(values, axis=-1, keepdims=True)
    centered = values - mean
    inverse = lax.rsqrt(jnp.mean(centered * centered, axis=-1, keepdims=True) + eps)
    scaled = centered * inverse
    return (scaled * gain + shift, scaled, inverse)


def gelu_slope(values):
    factor = 0.7978845608028654
    inner = factor * (values + 0.044715 * values * values * values)
    tangent = jnp.tanh(inner)
    return 0.5 * (1.0 + tangent) + 0.5 * values * (1.0 - tangent * tangent) * factor * (
        1.0 + 3.0 * 0.044715 * values * values
    )


def norm_back(upstream, gain, scaled, inverse):
    grad = upstream * gain
    return inverse * (
        grad
        - jnp.mean(grad, axis=-1, keepdims=True)
        - scaled * jnp.mean(grad * scaled, axis=-1, keepdims=True)
    )


def contract_rows(left, right):
    return lax.dot_general(left, right, (((0,), (0,)), ((), ())), preferred_element_type=f32)


def contract_cols(left, right):
    return lax.dot_general(left, right, (((1,), (1,)), ((), ())), preferred_element_type=f32)


def shift(values, axes, step):
    size = lax.axis_size(axes)
    return lax.ppermute(values, axes, [(i, (i + step) % size) for i in range(size)])


def ring(values, sign):
    size = lax.axis_size("z")
    pairs = []
    for z in range(size):
        pairs.append((2 * z, (z + sign) % size * 2))
        pairs.append((2 * z + 1, (z - sign) % size * 2 + 1))
    return lax.ppermute(values, ("z", "c"), pairs)


def columns(values, share):
    even = jnp.concatenate([values[..., :share], values[..., 2 * share : 3 * share]], axis=-1)
    odd = jnp.concatenate([values[..., share : 2 * share], values[..., 3 * share :]], axis=-1)
    return even, odd


vmem = pl.BlockSpec(memory_space=pltpu.VMEM)
smem = pl.BlockSpec(memory_space=pltpu.SMEM)
hbm = pl.BlockSpec(memory_space=pltpu.HBM)
anywhere = pl.BlockSpec(memory_space=pl.ANY)


def call(kernel, outs, in_specs, scratch=(), limit=6, out_specs=None, first=False):
    if first:
        body = kernel

        def kernel(*refs):
            inputs = len(in_specs)
            body(*refs[:inputs], refs[-1], *refs[inputs:-1])

    return pl.pallas_call(
        kernel,
        out_shape=outs,
        in_specs=in_specs,
        out_specs=out_specs or [vmem] * len(outs),
        scratch_shapes=scratch,
        cost_estimate=pl.CostEstimate(flops=1000, bytes_accessed=1000, transcendentals=0),
        compiler_params=pltpu.CompilerParams(vmem_limit_bytes=limit * 1024 * 1024),
    )


def shape(*dims, dtype=f32):
    return jax.ShapeDtypeStruct(dims, dtype)


def forward_kernel(
    at, hidden, gain, bias, fc1, fc1_bias, fc2, pre, scaled, keep, send_c, send_y, send_b,
    rows, line1, line2, line3, w1, w2, value, norm, part, sems,
):
    loads = [
        pltpu.make_async_copy(source, target, sems.at[index])
        for index, (source, target) in enumerate(
            [
                (hidden, rows),
                (gain, line1),
                (bias, line2),
                (fc1, w1),
                (fc1_bias, line3),
                (fc2, w2),
            ]
        )
    ]
    for load in loads:
        load.start()
    for load in loads[:3]:
        load.wait()
    units = fc1.shape[0]
    normed, norm[...], inverse = normalize(rows[...], line1[...], line2[...])
    normed = normed.astype(bf16)
    save_norm = pltpu.make_async_copy(norm, scaled, sems.at[6])
    save_norm.start()
    loads[3].wait()
    loads[4].wait()
    linear = contract_cols(normed, w1[...]) + line3[...]
    value[:, :units] = linear
    value[:, units : units + 1] = inverse
    save_pre = pltpu.make_async_copy(value, pre, sems.at[7])
    save_pre.start()
    act = jax.nn.gelu(linear, approximate=True).astype(bf16)
    loads[5].wait()
    part[...] = jnp.dot(act, w2[...], preferred_element_type=f32)
    quarter = keep.shape[0]
    side, core = at[0], at[1]

    def own(core, side):
        return pl.ds(pl.multiple_of((core * 2 + side) * quarter, quarter), quarter)

    keep[...] = rows[own(core, side), :] + part[own(core, side), :]
    send_c[...] = part[own(1 - core, side), :].astype(bf16)
    send_y[...] = part[own(core, 1 - side), :].astype(bf16)
    send_b[...] = part[own(1 - core, 1 - side), :].astype(bf16)
    save_norm.wait()
    save_pre.wait()


def embed_kernel(kept, got_c, got_y, got_b, gain, bias, head, after, unit, state):
    width = unit.shape[1]
    mixed = kept[...] + got_c[...].astype(f32) + got_y[...].astype(f32) + got_b[...].astype(f32)
    normed, scaled, inverse = normalize(mixed, gain[...], bias[...])
    state[:, width : 2 * width] = scaled
    embed = jnp.dot(normed.astype(bf16), head[...], preferred_element_type=f32)
    level = lax.rsqrt(jnp.sum(embed * embed, axis=-1, keepdims=True) + eps)
    unit[...] = (embed * level).astype(bf16)
    state[:, :width] = embed * level
    state[:, 2 * width : 2 * width + 1] = level
    state[:, 2 * width + 1 : 2 * width + 2] = inverse


def stack_kernel(*refs, count):
    rows = refs[0].shape[0]
    for index, ref in enumerate(refs[:count]):
        refs[-1][index * rows : (index + 1) * rows, :] = ref[...]


def parts_kernel(at, first, second, third, half, send):
    rows = half.shape[0]
    own = pl.ds(pl.multiple_of(at[1] * rows, rows), rows)
    other = pl.ds(pl.multiple_of((1 - at[1]) * rows, rows), rows)
    half[...] = third[own, :]
    for index, ref in enumerate((third, second, first)):
        send[index * rows : (index + 1) * rows, :] = ref[other, :]


def pairs_kernel(
    at, log_scale, offset, fourth, third, second, first, across, images, own, other,
    unit, image_rows, inverse, coef, keep, send, *, chunk, quarter,
):
    scale = jnp.exp(log_scale[...])
    half = own.shape[0]
    size = fourth.shape[0]
    mine = pl.ds(pl.multiple_of(at[1] * size, size), size)

    def put(index, values):
        rows = slice(index * size, (index + 1) * size)
        image_rows[rows, :] = values
        wide = values.astype(f32)
        level = lax.rsqrt(jnp.sum(wide * wide, axis=-1, keepdims=True) + eps)
        inverse[rows, :] = level
        unit[rows, :] = (wide * level).astype(bf16)

    put(0, fourth[...])
    for index in range(3):
        put(1 + index, across[index * size : (index + 1) * size, :])
    for index, ref in enumerate((third, second, first, images)):
        put(4 + index, ref[mine, :])
    diagonal = 7 * size + at[0] * quarter
    for start in range(0, unit.shape[0], chunk):
        rows = slice(start, start + chunk)
        low = unit[rows, :]
        chance = jax.nn.sigmoid(scale * contract_cols(low, own[...]) + offset[...])
        line = lax.broadcasted_iota(jnp.int32, chance.shape, 0) + (start - diagonal)
        cols = lax.broadcasted_iota(jnp.int32, chance.shape, 1)
        ident = ((line == cols) & (cols < quarter)).astype(f32)
        coef[rows, :half] = (scale * (chance - ident)).astype(bf16)
        chance = jax.nn.sigmoid(scale * contract_cols(low, other[...]) + offset[...])
        coef[rows, half:] = (scale * chance).astype(bf16)
    send[...] = contract_rows(coef[:, half:], unit[...]).astype(bf16)
    keep[...] = contract_rows(coef[:, :half], unit[...])


def images_kernel(images, inverse, coef, own, other, *parts, first):
    half = own.shape[0]
    size = images.shape[0] // 8
    rows = slice(first * size, (first + 4) * size)
    grad = jnp.dot(coef[rows, :half], own[...], preferred_element_type=f32)
    grad = grad + jnp.dot(coef[rows, half:], other[...], preferred_element_type=f32)
    level = inverse[rows, :]
    direct = images[rows, :].astype(f32) * level
    inner = jnp.sum(direct * grad, axis=-1, keepdims=True)
    grad = (grad - direct * inner) * level
    start = 0
    for part in parts:
        count = part.shape[0]
        part[...] = grad[start : start + count].astype(part.dtype)
        start += count


def pass_kernel(own, across, got, out, *, index):
    size = own.shape[0]
    if got.shape[0] == size:
        out[:size, :] = (own[...].astype(f32) + got[...].astype(f32)).astype(bf16)
        out[size:, :] = across[index * size : (index + 1) * size, :]
    else:
        out[:size, :] = (own[...].astype(f32) + got[:size, :].astype(f32)).astype(bf16)
        part = across[index * size : (index + 1) * size, :].astype(f32)
        out[size:, :] = (part + got[size:, :].astype(f32)).astype(bf16)


def owner_kernel(at, own, got, keep, send):
    size = own.shape[0]
    core = at[1] == 0
    share = own.shape[1] // 4
    mine = own[...] + got[:size, :].astype(f32)
    theirs = got[size:, :].astype(f32)
    low, high = jnp.where(core, mine, theirs), jnp.where(core, theirs, mine)
    for index, rows in enumerate((low, high)):
        place = slice(index * size, (index + 1) * size)
        even, odd = columns(rows, share)
        keep[place, :] = jnp.where(core, even, odd)
        send[place, :] = jnp.where(core, odd, even).astype(bf16)


def split_kernel(kept, got, after, near, *far):
    rows = near.shape[0]
    near[...] = kept[:rows, :] + got[:rows, :].astype(f32)
    for index, ref in enumerate(far):
        part = slice((index + 1) * rows, (index + 2) * rows)
        ref[...] = (kept[part, :] + got[part, :].astype(f32)).astype(bf16)


def join_kernel(near, first, second, third, after, keep, send):
    total = near[...] + first[...].astype(f32) + second[...].astype(f32) + third[...].astype(f32)
    half = keep.shape[0]
    keep[...] = total[:half]
    send[...] = total[half:].astype(bf16)


def head_kernel(kept, got, state, head, gain, after, grad):
    width = grad.shape[1]
    upstream = kept[...] + got[...].astype(f32)
    text_dir = state[:, :width]
    inner = jnp.sum(text_dir * upstream, axis=-1, keepdims=True)
    grad_embed = (upstream - text_dir * inner) * state[:, 2 * width : 2 * width + 1]
    grad_normed = contract_cols(grad_embed.astype(bf16), head[...])
    scaled, inverse = state[:, width : 2 * width], state[:, 2 * width + 1 : 2 * width + 2]
    grad[...] = norm_back(grad_normed, gain[...], scaled, inverse).astype(bf16)


def backward_kernel(
    at, gathered, pre, scaled, gain, fc1, fc2, after, keep, send, rest, value, norm, sems
):
    load_pre = pltpu.make_async_copy(pre, value, sems.at[0])
    load_norm = pltpu.make_async_copy(scaled, norm, sems.at[1])
    load_pre.start()
    load_norm.start()
    quarter = gathered.shape[0] // 4
    first, second, third, fourth = (
        gathered[index * quarter : (index + 1) * quarter, :] for index in range(4)
    )
    grad = jnp.concatenate([first, third, second, fourth], axis=0)
    share = grad.shape[1] // 4
    units = fc1.shape[0]
    core = at[1] == 0
    own = jnp.where(core, *columns(grad, share))
    rest[...] = jnp.where(at[0] == 0, own[:, :share], own[:, share:])
    grad_act = contract_cols(grad, fc2[...])
    load_pre.wait()
    grad_pre = (grad_act * gelu_slope(value[:, :units])).astype(bf16)
    part = jnp.dot(grad_pre, fc1[...], preferred_element_type=f32)
    load_norm.wait()
    part = norm_back(part, gain[...], norm[...], value[:, units : units + 1])
    even, odd = columns(part, share)
    keep[...] = jnp.where(core, even, odd)
    send[...] = jnp.where(core, odd, even).astype(bf16)


def halve_kernel(at, kept, got, keep, send):
    total = kept[...] + got[...].astype(f32)
    half = keep.shape[1]
    low, high = total[:, :half], total[:, half:]
    side = at[0] == 0
    keep[...] = jnp.where(side, low, high)
    send[...] = jnp.where(side, high, low).astype(bf16)


def hidden_kernel(kept, got, rest, out):
    out[...] = rest[...].astype(f32) + (kept[...] + got[...].astype(f32))


def total_kernel(kept, got, out):
    out[...] = kept[...] + got[...].astype(f32)


def shards(
    images,
    hidden_in,
    norm1_gain,
    norm1_bias,
    fc1,
    fc1_bias,
    fc2,
    norm2_gain,
    norm2_bias,
    head,
    log_scale,
    logit_bias,
):
    block, width = images.shape
    quarter = block // 4
    share = width // 4
    units = fc1.shape[1]
    half = block // 2
    yl_at, c_at = (lax.axis_index(a) for a in ("yl", "c"))
    at = jnp.stack([yl_at, c_at]).astype(jnp.int32)
    fc1 = fc1.T

    low = shape(half, width, dtype=bf16)
    first = ring(images, 1)
    second = ring(first, 1)
    third = ring(second, 1)
    fourth, across = call(
        parts_kernel,
        [low, shape(3 * half, width, dtype=bf16)],
        [smem] + [vmem] * 3,
    )(at, first, second, third)
    fourth, across = ring(fourth, 1), shift(across, "c", 1)

    pad = (units // 128 + 1) * 128
    pre, scaled_in, keep, *sends = call(
        forward_kernel,
        [shape(block, pad), shape(block, width), shape(quarter, width)]
        + [shape(quarter, width, dtype=bf16)] * 3,
        [smem] + [hbm] * 6,
        [
            pltpu.VMEM((block, width), f32),
            pltpu.VMEM((width,), f32),
            pltpu.VMEM((width,), f32),
            pltpu.VMEM((units,), f32),
            pltpu.VMEM((units, width), bf16),
            pltpu.VMEM((units, width), bf16),
            pltpu.VMEM((block, pad), f32),
            pltpu.VMEM((block, width), f32),
            pltpu.VMEM((block, width), f32),
            pltpu.SemaphoreType.DMA((8,)),
        ],
        limit=58,
        out_specs=[hbm] * 2 + [vmem] * 4,
    )(at, hidden_in, norm1_gain, norm1_bias, fc1, fc1_bias, fc2)
    text_unit, state = call(
        embed_kernel,
        [shape(quarter, width, dtype=bf16), shape(quarter, 2 * width + 128)],
        [vmem] * 7 + [anywhere],
        limit=10,
    )(
        keep,
        *(
            lax.ppermute(send, ("yl", "c"), [(i, i ^ bits) for i in range(4)])
            for send, bits in zip(sends, (1, 2, 3))
        ),
        norm2_gain,
        norm2_bias,
        head,
        first,
    )

    near = call(
        functools.partial(stack_kernel, count=2), [shape(half, width, dtype=bf16)], [vmem] * 2 + [anywhere]
    )(text_unit, shift(text_unit, "yh", 1), second)[0]
    own = call(
        functools.partial(stack_kernel, count=4),
        [shape(4 * half, width, dtype=bf16)],
        [vmem] * 4 + [anywhere] * 2,
    )(near, *(shift(near, "x", hop) for hop in hops[1:]), fourth, across)[0]
    other = shift(own, "c", 1)

    many = 8 * half
    image_rows, inverse_image, coef, keep, send = call(
        functools.partial(pairs_kernel, chunk=many // 2, quarter=quarter),
        [
            shape(many, width, dtype=bf16),
            shape(many, 1),
            shape(many, 8 * half, dtype=bf16),
            shape(4 * half, width),
            shape(4 * half, width, dtype=bf16),
        ],
        [smem] + [vmem] * 10,
        [pltpu.VMEM((many, width), bf16)],
        limit=20,
        first=True,
    )(
        at,
        log_scale.reshape(1, 1),
        logit_bias.reshape(1, 1),
        fourth,
        third,
        second,
        first,
        across,
        images,
        own,
        other,
    )
    got = shift(send, "c", 1)

    fourth, across = call(
        functools.partial(images_kernel, first=0),
        [low, shape(3 * half, width, dtype=bf16)],
        [vmem] * 5,
        limit=12,
    )(image_rows, inverse_image, coef, own, other)
    near, *far = call(
        split_kernel,
        [shape(half, width)] + [low] * 3,
        [vmem] * 2 + [anywhere],
    )(keep, got, fourth)
    far = [shift(far[index], "x", 4 - hop) for index, hop in enumerate(hops[1:])]
    fourth, across = ring(fourth, -1), shift(across, "c", 1)
    *parts, image_part = call(
        functools.partial(images_kernel, first=4),
        [low] * 3 + [shape(half, width)],
        [vmem] * 5,
        limit=12,
    )(image_rows, inverse_image, coef, own, other)
    moved = [fourth]
    for index in range(3):
        moving = call(
            functools.partial(pass_kernel, index=index),
            [shape(block, width, dtype=bf16)],
            [vmem] * 3,
        )(parts[index], across, moved[-1])[0]
        moved.append(ring(moving, -1))

    keep, send = call(
        join_kernel,
        [shape(quarter, width), shape(quarter, width, dtype=bf16)],
        [vmem] * 4 + [anywhere],
    )(near, *far, moved[1])
    grad_mixed = call(
        head_kernel, [shape(quarter, width, dtype=bf16)], [vmem] * 5 + [anywhere], limit=10
    )(keep, shift(send, "yh", 1), state, head, norm2_gain, moved[2])[0]
    grad_mixed = lax.all_gather(grad_mixed, ("yl", "c"), axis=0, tiled=True)
    keep, send, rest = call(
        backward_kernel,
        [
            shape(block, 2 * share),
            shape(block, 2 * share, dtype=bf16),
            shape(block, share, dtype=bf16),
        ],
        [smem, vmem, hbm, hbm, vmem, vmem, vmem, anywhere],
        [
            pltpu.VMEM((block, pad), f32),
            pltpu.VMEM((block, width), f32),
            pltpu.SemaphoreType.DMA((2,)),
        ],
        limit=16,
    )(at, grad_mixed, pre, scaled_in, norm1_gain, fc1, fc2, moved[3])
    keep, send = call(
        halve_kernel,
        [shape(block, share), shape(block, share, dtype=bf16)],
        [smem, vmem, vmem],
    )(at, keep, shift(send, "c", 1))
    grad_hidden = call(hidden_kernel, [shape(block, share)], [vmem] * 3)(
        keep, shift(send, "yl", 1), rest
    )[0]

    keep, send = call(
        owner_kernel,
        [shape(block, 2 * share), shape(block, 2 * share, dtype=bf16)],
        [smem] + [vmem] * 2,
    )(at, image_part, moved[3])
    keep, send = call(
        halve_kernel,
        [shape(block, share), shape(block, share, dtype=bf16)],
        [smem, vmem, vmem],
    )(at, keep, shift(send, "c", 1))
    grad_images = call(total_kernel, [shape(block, share)], [vmem] * 2)(
        keep, shift(send, "yl", 1)
    )[0]
    return (grad_images, grad_hidden)


def solution(mesh):
    grid = Mesh(mesh.devices.reshape(8, 4, 2, 2, 2), ("z", "x", "yh", "yl", "c"))
    dp, mp = ("z", "x", "yh"), ("yl", "c")
    placed = (
        P(dp, None),
        P(dp, None),
        P(),
        P(),
        P(None, mp),
        P(mp),
        P(mp, None),
        P(),
        P(),
        P(),
        P(),
        P(),
    )
    return jax.shard_map(
        shards,
        mesh=grid,
        in_specs=placed,
        out_specs=(P(dp, mp), P(dp, mp)),
        check_vma=False,
    )
```

```python
import functools

import jax
import jax.numpy as jnp
from jax import lax
from jax.experimental import pallas as pl
from jax.experimental.pallas import tpu as pltpu
from jax.sharding import Mesh, PartitionSpec as P

eps = 1e-06
hops = (0, 1, 3, 2)
f32 = jnp.float32
bf16 = jnp.bfloat16


def normalize(values, gain, shift):
    mean = jnp.mean(values, axis=-1, keepdims=True)
    centered = values - mean
    inverse = lax.rsqrt(jnp.mean(centered * centered, axis=-1, keepdims=True) + eps)
    scaled = centered * inverse
    return (scaled * gain + shift, scaled, inverse)


def gelu_slope(values):
    factor = 0.7978845608028654
    inner = factor * (values + 0.044715 * values * values * values)
    tangent = jnp.tanh(inner)
    return 0.5 * (1.0 + tangent) + 0.5 * values * (1.0 - tangent * tangent) * factor * (
        1.0 + 3.0 * 0.044715 * values * values
    )


def norm_back(upstream, gain, scaled, inverse):
    grad = upstream * gain
    return inverse * (
        grad
        - jnp.mean(grad, axis=-1, keepdims=True)
        - scaled * jnp.mean(grad * scaled, axis=-1, keepdims=True)
    )


def contract_rows(left, right):
    return lax.dot_general(left, right, (((0,), (0,)), ((), ())), preferred_element_type=f32)


def contract_cols(left, right):
    return lax.dot_general(left, right, (((1,), (1,)), ((), ())), preferred_element_type=f32)


def shift(values, axes, step):
    size = lax.axis_size(axes)
    return lax.ppermute(values, axes, [(i, (i + step) % size) for i in range(size)])


def ring(values, sign):
    size = lax.axis_size("z")
    pairs = []
    for z in range(size):
        pairs.append((2 * z, (z + sign) % size * 2))
        pairs.append((2 * z + 1, (z - sign) % size * 2 + 1))
    return lax.ppermute(values, ("z", "c"), pairs)


def columns(values, share):
    even = jnp.concatenate([values[..., :share], values[..., 2 * share : 3 * share]], axis=-1)
    odd = jnp.concatenate([values[..., share : 2 * share], values[..., 3 * share :]], axis=-1)
    return even, odd


vmem = pl.BlockSpec(memory_space=pltpu.VMEM)
smem = pl.BlockSpec(memory_space=pltpu.SMEM)
hbm = pl.BlockSpec(memory_space=pltpu.HBM)
anywhere = pl.BlockSpec(memory_space=pl.ANY)


def call(kernel, outs, in_specs, scratch=(), limit=6, out_specs=None, cost=1000):
    return pl.pallas_call(
        kernel,
        out_shape=outs,
        in_specs=in_specs,
        out_specs=out_specs or [vmem] * len(outs),
        scratch_shapes=scratch,
        cost_estimate=pl.CostEstimate(flops=300*cost, bytes_accessed=cost, transcendentals=0),
        compiler_params=pltpu.CompilerParams(vmem_limit_bytes=limit * 1024 * 1024),
    )


def shape(*dims, dtype=f32):
    return jax.ShapeDtypeStruct(dims, dtype)


def forward_kernel(
    at, hidden, gain, bias, fc1, fc1_bias, fc2, pre, scaled, keep, send_c, send_y, send_b,
    rows, line1, line2, line3, w1, w2, value, norm, part, sems,
):
    loads = [
        pltpu.make_async_copy(source, target, sems.at[index])
        for index, (source, target) in enumerate(
            [
                (hidden, rows),
                (gain, line1),
                (bias, line2),
                (fc1, w1),
                (fc1_bias, line3),
                (fc2, w2),
            ]
        )
    ]
    for load in loads:
        load.start()
    for load in loads[:3]:
        load.wait()
    units = fc1.shape[0]
    normed, norm[...], inverse = normalize(rows[...], line1[...], line2[...])
    normed = normed.astype(bf16)
    save_norm = pltpu.make_async_copy(norm, scaled, sems.at[6])
    save_norm.start()
    loads[3].wait()
    loads[4].wait()
    linear = contract_cols(normed, w1[...]) + line3[...]
    value[:, :units] = linear
    value[:, units : units + 1] = inverse
    save_pre = pltpu.make_async_copy(value, pre, sems.at[7])
    save_pre.start()
    act = jax.nn.gelu(linear, approximate=True).astype(bf16)
    loads[5].wait()
    part[...] = jnp.dot(act, w2[...], preferred_element_type=f32)
    quarter = keep.shape[0]
    side, core = at[0], at[1]

    def own(core, side):
        return pl.ds(pl.multiple_of((core * 2 + side) * quarter, quarter), quarter)

    keep[...] = rows[own(core, side), :] + part[own(core, side), :]
    send_c[...] = part[own(1 - core, side), :].astype(bf16)
    send_y[...] = part[own(core, 1 - side), :].astype(bf16)
    send_b[...] = part[own(1 - core, 1 - side), :].astype(bf16)
    save_norm.wait()
    save_pre.wait()


def embed_kernel(kept, got_c, got_y, got_b, gain, bias, head, unit, state):
    width = unit.shape[1]
    mixed = kept[...] + got_c[...].astype(f32) + got_y[...].astype(f32) + got_b[...].astype(f32)
    normed, scaled, inverse = normalize(mixed, gain[...], bias[...])
    state[:, width : 2 * width] = scaled
    embed = jnp.dot(normed.astype(bf16), head[...], preferred_element_type=f32)
    level = lax.rsqrt(jnp.sum(embed * embed, axis=-1, keepdims=True) + eps)
    unit[...] = (embed * level).astype(bf16)
    state[:, :width] = embed * level
    state[:, 2 * width : 2 * width + 1] = level
    state[:, 2 * width + 1 : 2 * width + 2] = inverse


def stack_kernel(*refs, count):
    rows = refs[0].shape[0]
    for index, ref in enumerate(refs[:count]):
        refs[-1][index * rows : (index + 1) * rows, :] = ref[...]


def parts_kernel(at, first, second, third, half, send):
    rows = half.shape[0]
    own = pl.ds(pl.multiple_of(at[1] * rows, rows), rows)
    other = pl.ds(pl.multiple_of((1 - at[1]) * rows, rows), rows)
    half[...] = third[own, :]
    for index, ref in enumerate((third, second, first)):
        send[index * rows : (index + 1) * rows, :] = ref[other, :]


def norm_kernel(at, fourth, third, second, first, across, images, unit, image_rows, inverse):
    size = fourth.shape[0]
    mine = pl.ds(pl.multiple_of(at[1] * size, size), size)

    def put(index, values):
        rows = slice(index * size, (index + 1) * size)
        image_rows[rows, :] = values
        wide = values.astype(f32)
        level = lax.rsqrt(jnp.sum(wide * wide, axis=-1, keepdims=True) + eps)
        inverse[rows, :] = level
        unit[rows, :] = (wide * level).astype(bf16)

    put(0, fourth[...])
    for index in range(3):
        put(1 + index, across[index * size : (index + 1) * size, :])
    for index, ref in enumerate((third, second, first, images)):
        put(4 + index, ref[mine, :])


def pairs_kernel(at, log_scale, offset, unit, own, other, coef, keep, send, *, chunk, quarter):
    scale = jnp.exp(log_scale[...])
    half = own.shape[0]
    size = unit.shape[0] // 8
    diagonal = 7 * size + at[0] * quarter
    for start in range(0, unit.shape[0], chunk):
        rows = slice(start, start + chunk)
        low = unit[rows, :]
        chance = jax.nn.sigmoid(scale * contract_cols(low, own[...]) + offset[...])
        line = lax.broadcasted_iota(jnp.int32, chance.shape, 0) + (start - diagonal)
        cols = lax.broadcasted_iota(jnp.int32, chance.shape, 1)
        ident = ((line == cols) & (cols < quarter)).astype(f32)
        coef[rows, :half] = (scale * (chance - ident)).astype(bf16)
        chance = jax.nn.sigmoid(scale * contract_cols(low, other[...]) + offset[...])
        coef[rows, half:] = (scale * chance).astype(bf16)
    send[...] = contract_rows(coef[:, half:], unit[...]).astype(bf16)
    keep[...] = contract_rows(coef[:, :half], unit[...])


def images_kernel(images, inverse, coef, own, other, *parts, first):
    half = own.shape[0]
    size = images.shape[0] // 8
    rows = slice(first * size, (first + 4) * size)
    grad = jnp.dot(coef[rows, :half], own[...], preferred_element_type=f32)
    grad = grad + jnp.dot(coef[rows, half:], other[...], preferred_element_type=f32)
    level = inverse[rows, :]
    direct = images[rows, :].astype(f32) * level
    inner = jnp.sum(direct * grad, axis=-1, keepdims=True)
    grad = (grad - direct * inner) * level
    start = 0
    for part in parts:
        count = part.shape[0]
        part[...] = grad[start : start + count].astype(part.dtype)
        start += count


def pass_kernel(own, across, got, after, out, *, index):
    size = own.shape[0]
    if got.shape[0] == size:
        out[:size, :] = (own[...].astype(f32) + got[...].astype(f32)).astype(bf16)
        out[size:, :] = across[index * size : (index + 1) * size, :]
    else:
        out[:size, :] = (own[...].astype(f32) + got[:size, :].astype(f32)).astype(bf16)
        part = across[index * size : (index + 1) * size, :].astype(f32)
        out[size:, :] = (part + got[size:, :].astype(f32)).astype(bf16)


def owner_kernel(at, own, got, after, keep, send):
    size = own.shape[0]
    core = at[1] == 0
    share = own.shape[1] // 4
    mine = own[...] + got[:size, :].astype(f32)
    theirs = got[size:, :].astype(f32)
    low, high = jnp.where(core, mine, theirs), jnp.where(core, theirs, mine)
    for index, rows in enumerate((low, high)):
        place = slice(index * size, (index + 1) * size)
        even, odd = columns(rows, share)
        keep[place, :] = jnp.where(core, even, odd)
        send[place, :] = jnp.where(core, odd, even).astype(bf16)


def split_kernel(kept, got, after, near, *far):
    rows = near.shape[0]
    near[...] = kept[:rows, :] + got[:rows, :].astype(f32)
    for index, ref in enumerate(far):
        part = slice((index + 1) * rows, (index + 2) * rows)
        ref[...] = (kept[part, :] + got[part, :].astype(f32)).astype(bf16)


def join_kernel(near, first, second, third, keep, send):
    total = near[...] + first[...].astype(f32) + second[...].astype(f32) + third[...].astype(f32)
    half = keep.shape[0]
    keep[...] = total[:half]
    send[...] = total[half:].astype(bf16)


def head_kernel(kept, got, state, head, gain, grad):
    width = grad.shape[1]
    upstream = kept[...] + got[...].astype(f32)
    text_dir = state[:, :width]
    inner = jnp.sum(text_dir * upstream, axis=-1, keepdims=True)
    grad_embed = (upstream - text_dir * inner) * state[:, 2 * width : 2 * width + 1]
    grad_normed = contract_cols(grad_embed.astype(bf16), head[...])
    scaled, inverse = state[:, width : 2 * width], state[:, 2 * width + 1 : 2 * width + 2]
    grad[...] = norm_back(grad_normed, gain[...], scaled, inverse).astype(bf16)


def backward_kernel(
    at, gathered, pre, scaled, gain, fc1, fc2, keep, send, rest, value, norm, sems
):
    load_pre = pltpu.make_async_copy(pre, value, sems.at[0])
    load_norm = pltpu.make_async_copy(scaled, norm, sems.at[1])
    load_pre.start()
    load_norm.start()
    quarter = gathered.shape[0] // 4
    first, second, third, fourth = (
        gathered[index * quarter : (index + 1) * quarter, :] for index in range(4)
    )
    grad = jnp.concatenate([first, third, second, fourth], axis=0)
    share = grad.shape[1] // 4
    units = fc1.shape[0]
    core = at[1] == 0
    own = jnp.where(core, *columns(grad, share))
    rest[...] = jnp.where(at[0] == 0, own[:, :share], own[:, share:])
    grad_act = contract_cols(grad, fc2[...])
    load_pre.wait()
    grad_pre = (grad_act * gelu_slope(value[:, :units])).astype(bf16)
    part = jnp.dot(grad_pre, fc1[...], preferred_element_type=f32)
    load_norm.wait()
    part = norm_back(part, gain[...], norm[...], value[:, units : units + 1])
    even, odd = columns(part, share)
    keep[...] = jnp.where(core, even, odd)
    send[...] = jnp.where(core, odd, even).astype(bf16)


def halve_kernel(at, kept, got, keep, send):
    total = kept[...] + got[...].astype(f32)
    half = keep.shape[1]
    low, high = total[:, :half], total[:, half:]
    side = at[0] == 0
    keep[...] = jnp.where(side, low, high)
    send[...] = jnp.where(side, high, low).astype(bf16)


def hidden_kernel(kept, got, rest, out):
    out[...] = rest[...].astype(f32) + (kept[...] + got[...].astype(f32))


def total_kernel(kept, got, out):
    out[...] = kept[...] + got[...].astype(f32)


def shards(
    images,
    hidden_in,
    norm1_gain,
    norm1_bias,
    fc1,
    fc1_bias,
    fc2,
    norm2_gain,
    norm2_bias,
    head,
    log_scale,
    logit_bias,
):
    block, width = images.shape
    quarter = block // 4
    share = width // 4
    units = fc1.shape[1]
    half = block // 2
    yl_at, c_at = (lax.axis_index(a) for a in ("yl", "c"))
    at = jnp.stack([yl_at, c_at]).astype(jnp.int32)
    fc1 = fc1.T

    low = shape(half, width, dtype=bf16)
    pad = (units // 128 + 1) * 128
    pre, scaled_in, keep, *sends = call(
        forward_kernel,
        [shape(block, pad), shape(block, width), shape(quarter, width)]
        + [shape(quarter, width, dtype=bf16)] * 3,
        [smem] + [hbm] * 6,
        [
            pltpu.VMEM((block, width), f32),
            pltpu.VMEM((width,), f32),
            pltpu.VMEM((width,), f32),
            pltpu.VMEM((units,), f32),
            pltpu.VMEM((units, width), bf16),
            pltpu.VMEM((units, width), bf16),
            pltpu.VMEM((block, pad), f32),
            pltpu.VMEM((block, width), f32),
            pltpu.VMEM((block, width), f32),
            pltpu.SemaphoreType.DMA((8,)),
        ],
        limit=58,
        out_specs=[hbm] * 2 + [vmem] * 4,
    )(at, hidden_in, norm1_gain, norm1_bias, fc1, fc1_bias, fc2)
    first = ring(images, 1)
    sends = [
        lax.ppermute(send, ("yl", "c"), [(i, i ^ bits) for i in range(4)])
        for send, bits in zip(sends, (1, 2, 3))
    ]
    second = ring(lax.optimization_barrier((first, sends[0]))[0], 1)
    text_unit, state = call(
        embed_kernel,
        [shape(quarter, width, dtype=bf16), shape(quarter, 2 * width + 128)],
        [vmem] * 7,
        limit=10,
        cost=10001000,
    )(
        keep,
        *sends,
        norm2_gain,
        norm2_bias,
        head,
    )

    third = ring(lax.optimization_barrier((second, text_unit))[0], 1)

    near = call(
        functools.partial(stack_kernel, count=2), [shape(half, width, dtype=bf16)], [vmem] * 2, cost=10001000
    )(text_unit, shift(text_unit, "yh", 1))[0]
    fourth, across = call(
        parts_kernel,
        [low, shape(3 * half, width, dtype=bf16)],
        [smem] + [vmem] * 3,
    )(at, first, second, third)
    own = call(
        functools.partial(stack_kernel, count=4),
        [shape(4 * half, width, dtype=bf16)],
        [vmem] * 4 + [anywhere] * 2,
        cost=1000,
    )(near, *(shift(near, "x", hop) for hop in hops[1:]), fourth, across)[0]
    fourth, across = ring(fourth, 1), shift(across, "c", 1)
    other = shift(own, "c", 1)

    many = 8 * half
    image_unit, image_rows, inverse_image = call(
        norm_kernel,
        [shape(many, width, dtype=bf16)] * 2 + [shape(many, 1)],
        [smem] + [vmem] * 6,
        limit=12,
        cost=8001000,
    )(at, fourth, third, second, first, across, images)
    coef, keep, send = call(
        functools.partial(pairs_kernel, chunk=many // 2, quarter=quarter),
        [
            shape(many, 8 * half, dtype=bf16),
            shape(4 * half, width),
            shape(4 * half, width, dtype=bf16),
        ],
        [smem] + [vmem] * 5,
        limit=20,
        cost=1000,
    )(at, log_scale.reshape(1, 1), logit_bias.reshape(1, 1), image_unit, own, other)
    got = shift(send, "c", 1)

    fourth, across = call(
        functools.partial(images_kernel, first=0),
        [low, shape(3 * half, width, dtype=bf16)],
        [vmem] * 5,
        limit=12,
    )(image_rows, inverse_image, coef, own, other)
    near, *far = call(
        split_kernel,
        [shape(half, width)] + [low] * 3,
        [vmem] * 2 + [anywhere],
    )(keep, got, fourth)
    far = [shift(far[index], "x", 4 - hop) for index, hop in enumerate(hops[1:])]
    fourth, across = ring(fourth, -1), shift(across, "c", 1)
    *parts, image_part = call(
        functools.partial(images_kernel, first=4),
        [low] * 3 + [shape(half, width)],
        [vmem] * 5,
        limit=12,
    )(image_rows, inverse_image, coef, own, other)

    def onward(index, got, after):
        moving = call(
            functools.partial(pass_kernel, index=index),
            [shape(block, width, dtype=bf16)],
            [vmem] * 3 + [anywhere],
        )(parts[index], across, got, after)[0]
        return ring(moving, -1)

    moved = onward(0, fourth, near)
    keep, send = call(
        join_kernel,
        [shape(quarter, width), shape(quarter, width, dtype=bf16)],
        [vmem] * 4,
        cost=60001000,
    )(near, *far)
    moved = onward(1, moved, keep)
    grad_mixed = call(
        head_kernel, [shape(quarter, width, dtype=bf16)], [vmem] * 5, limit=10, cost=60001000
    )(keep, shift(send, "yh", 1), state, head, norm2_gain)[0]
    grad_mixed = lax.all_gather(grad_mixed, ("yl", "c"), axis=0, tiled=True)
    moved = onward(2, moved, grad_mixed)
    keep, send, rest = call(
        backward_kernel,
        [
            shape(block, 2 * share),
            shape(block, 2 * share, dtype=bf16),
            shape(block, share, dtype=bf16),
        ],
        [smem, vmem, hbm, hbm, vmem, vmem, vmem],
        [
            pltpu.VMEM((block, pad), f32),
            pltpu.VMEM((block, width), f32),
            pltpu.SemaphoreType.DMA((2,)),
        ],
        limit=16,
        cost=15000000,
    )(at, grad_mixed, pre, scaled_in, norm1_gain, fc1, fc2)
    keep, send = call(
        halve_kernel,
        [shape(block, share), shape(block, share, dtype=bf16)],
        [smem, vmem, vmem],
    )(at, keep, shift(send, "c", 1))
    hidden_keep = keep
    grad_hidden = call(hidden_kernel, [shape(block, share)], [vmem] * 3)(
        keep, shift(send, "yl", 1), rest
    )[0]

    keep, send = call(
        owner_kernel,
        [shape(block, 2 * share), shape(block, 2 * share, dtype=bf16)],
        [smem] + [vmem] * 2 + [anywhere],
    )(at, image_part, moved, hidden_keep)
    keep, send = call(
        halve_kernel,
        [shape(block, share), shape(block, share, dtype=bf16)],
        [smem, vmem, vmem],
    )(at, keep, shift(send, "c", 1))
    grad_images = call(total_kernel, [shape(block, share)], [vmem] * 2)(
        keep, shift(send, "yl", 1)
    )[0]
    return (grad_images, grad_hidden)


def solution(mesh):
    grid = Mesh(mesh.devices.reshape(8, 4, 2, 2, 2), ("z", "x", "yh", "yl", "c"))
    dp, mp = ("z", "x", "yh"), ("yl", "c")
    placed = (
        P(dp, None),
        P(dp, None),
        P(),
        P(),
        P(None, mp),
        P(mp),
        P(mp, None),
        P(),
        P(),
        P(),
        P(),
        P(),
    )
    return jax.shard_map(
        shards,
        mesh=grid,
        in_specs=placed,
        out_specs=(P(dp, mp), P(dp, mp)),
        check_vma=False,
    )
```

```python
import functools

import jax
import jax.numpy as jnp
from jax import lax
from jax.experimental import pallas as pl
from jax.experimental.pallas import tpu as pltpu
from jax.sharding import Mesh, PartitionSpec as P

eps = 1e-06
hops = (0, 1, 3, 2)
f32 = jnp.float32
bf16 = jnp.bfloat16


def normalize(values, gain, shift):
    mean = jnp.mean(values, axis=-1, keepdims=True)
    centered = values - mean
    inverse = lax.rsqrt(jnp.mean(centered * centered, axis=-1, keepdims=True) + eps)
    scaled = centered * inverse
    return (scaled * gain + shift, scaled, inverse)


def gelu_slope(values):
    factor = 0.7978845608028654
    inner = factor * (values + 0.044715 * values * values * values)
    tangent = jnp.tanh(inner)
    return 0.5 * (1.0 + tangent) + 0.5 * values * (1.0 - tangent * tangent) * factor * (
        1.0 + 3.0 * 0.044715 * values * values
    )


def norm_back(upstream, gain, scaled, inverse):
    grad = upstream * gain
    return inverse * (
        grad
        - jnp.mean(grad, axis=-1, keepdims=True)
        - scaled * jnp.mean(grad * scaled, axis=-1, keepdims=True)
    )


def contract_rows(left, right):
    return lax.dot_general(left, right, (((0,), (0,)), ((), ())), preferred_element_type=f32)


def contract_cols(left, right):
    return lax.dot_general(left, right, (((1,), (1,)), ((), ())), preferred_element_type=f32)


def shift(values, axes, step):
    size = lax.axis_size(axes)
    return lax.ppermute(values, axes, [(i, (i + step) % size) for i in range(size)])


def ring(values, sign):
    size = lax.axis_size("z")
    pairs = []
    for z in range(size):
        pairs.append((2 * z, (z + sign) % size * 2))
        pairs.append((2 * z + 1, (z - sign) % size * 2 + 1))
    return lax.ppermute(values, ("z", "c"), pairs)


def facing(values):
    return lax.ppermute(values, ("yh", "yl"), [(0, 3), (3, 0), (1, 2), (2, 1)])


def columns(values, share):
    even = jnp.concatenate([values[..., :share], values[..., 2 * share : 3 * share]], axis=-1)
    odd = jnp.concatenate([values[..., share : 2 * share], values[..., 3 * share :]], axis=-1)
    return even, odd


vmem = pl.BlockSpec(memory_space=pltpu.VMEM)
smem = pl.BlockSpec(memory_space=pltpu.SMEM)
hbm = pl.BlockSpec(memory_space=pltpu.HBM)
anywhere = pl.BlockSpec(memory_space=pl.ANY)


def call(kernel, outs, in_specs, scratch=(), limit=6, out_specs=None, cost=1000):
    return pl.pallas_call(
        kernel,
        out_shape=outs,
        in_specs=in_specs,
        out_specs=out_specs or [vmem] * len(outs),
        scratch_shapes=scratch,
        cost_estimate=pl.CostEstimate(flops=300*cost, bytes_accessed=cost, transcendentals=0),
        compiler_params=pltpu.CompilerParams(vmem_limit_bytes=limit * 1024 * 1024),
    )


def shape(*dims, dtype=f32):
    return jax.ShapeDtypeStruct(dims, dtype)


def forward_kernel(
    at, hidden, gain, bias, fc1, fc1_bias, fc2, pre, scaled, keep, send_c, send_y, send_b,
    rows, line1, line2, line3, w1, w2, value, norm, part, sems,
):
    loads = [
        pltpu.make_async_copy(source, target, sems.at[index])
        for index, (source, target) in enumerate(
            [
                (hidden, rows),
                (gain, line1),
                (bias, line2),
                (fc1, w1),
                (fc1_bias, line3),
                (fc2, w2),
            ]
        )
    ]
    for load in loads:
        load.start()
    for load in loads[:3]:
        load.wait()
    units = fc1.shape[0]
    normed, norm[...], inverse = normalize(rows[...], line1[...], line2[...])
    normed = normed.astype(bf16)
    save_norm = pltpu.make_async_copy(norm, scaled, sems.at[6])
    save_norm.start()
    loads[3].wait()
    loads[4].wait()
    linear = contract_cols(normed, w1[...]) + line3[...]
    value[:, :units] = linear
    value[:, units : units + 1] = inverse
    save_pre = pltpu.make_async_copy(value, pre, sems.at[7])
    save_pre.start()
    act = jax.nn.gelu(linear, approximate=True).astype(bf16)
    loads[5].wait()
    part[...] = jnp.dot(act, w2[...], preferred_element_type=f32)
    quarter = keep.shape[0]
    side, core = at[0], at[1]

    def own(core, side):
        return pl.ds(pl.multiple_of((core * 2 + side) * quarter, quarter), quarter)

    keep[...] = rows[own(core, side), :] + part[own(core, side), :]
    send_c[...] = part[own(1 - core, side), :].astype(bf16)
    send_y[...] = part[own(core, 1 - side), :].astype(bf16)
    send_b[...] = part[own(1 - core, 1 - side), :].astype(bf16)
    save_norm.wait()
    save_pre.wait()


def embed_kernel(kept, got_c, got_y, got_b, gain, bias, head, unit, state):
    width = unit.shape[1]
    mixed = kept[...] + got_c[...].astype(f32) + got_y[...].astype(f32) + got_b[...].astype(f32)
    normed, scaled, inverse = normalize(mixed, gain[...], bias[...])
    state[:, width : 2 * width] = scaled
    embed = jnp.dot(normed.astype(bf16), head[...], preferred_element_type=f32)
    level = lax.rsqrt(jnp.sum(embed * embed, axis=-1, keepdims=True) + eps)
    unit[...] = (embed * level).astype(bf16)
    state[:, :width] = embed * level
    state[:, 2 * width : 2 * width + 1] = level
    state[:, 2 * width + 1 : 2 * width + 2] = inverse


def stack_kernel(*refs, count):
    rows = refs[0].shape[0]
    for index, ref in enumerate(refs[:count]):
        refs[-1][index * rows : (index + 1) * rows, :] = ref[...]


def parts_kernel(at, first, second, third, half, send):
    rows = half.shape[0]
    own = pl.ds(pl.multiple_of(at[1] * rows, rows), rows)
    other = pl.ds(pl.multiple_of((1 - at[1]) * rows, rows), rows)
    half[...] = third[own, :]
    for index, ref in enumerate((third, second, first)):
        send[index * rows : (index + 1) * rows, :] = ref[other, :]


def norm_kernel(at, fourth, third, second, first, across, images, unit, image_rows, inverse):
    size = fourth.shape[0]
    mine = pl.ds(pl.multiple_of(at[1] * size, size), size)

    def put(index, values):
        rows = slice(index * size, (index + 1) * size)
        image_rows[rows, :] = values
        wide = values.astype(f32)
        level = lax.rsqrt(jnp.sum(wide * wide, axis=-1, keepdims=True) + eps)
        inverse[rows, :] = level
        unit[rows, :] = (wide * level).astype(bf16)

    put(0, fourth[...])
    for index in range(3):
        put(1 + index, across[index * size : (index + 1) * size, :])
    for index, ref in enumerate((third, second, first, images)):
        put(4 + index, ref[mine, :])


def pairs_kernel(at, log_scale, offset, unit, own, other, coef, keep, send, *, chunk, quarter):
    scale = jnp.exp(log_scale[...])
    half = own.shape[0]
    size = unit.shape[0] // 8
    diagonal = 7 * size + at[0] * quarter
    for start in range(0, unit.shape[0], chunk):
        rows = slice(start, start + chunk)
        low = unit[rows, :]
        chance = jax.nn.sigmoid(scale * contract_cols(low, own[...]) + offset[...])
        line = lax.broadcasted_iota(jnp.int32, chance.shape, 0) + (start - diagonal)
        cols = lax.broadcasted_iota(jnp.int32, chance.shape, 1)
        ident = ((line == cols) & (cols < quarter)).astype(f32)
        coef[rows, :half] = (scale * (chance - ident)).astype(bf16)
        chance = jax.nn.sigmoid(scale * contract_cols(low, other[...]) + offset[...])
        coef[rows, half:] = (scale * chance).astype(bf16)
    send[...] = contract_rows(coef[:, half:], unit[...]).astype(bf16)
    keep[...] = contract_rows(coef[:, :half], unit[...])


def images_kernel(images, inverse, coef, own, other, *parts, first):
    half = own.shape[0]
    size = images.shape[0] // 8
    rows = slice(first * size, (first + 4) * size)
    grad = jnp.dot(coef[rows, :half], own[...], preferred_element_type=f32)
    grad = grad + jnp.dot(coef[rows, half:], other[...], preferred_element_type=f32)
    level = inverse[rows, :]
    direct = images[rows, :].astype(f32) * level
    inner = jnp.sum(direct * grad, axis=-1, keepdims=True)
    grad = (grad - direct * inner) * level
    start = 0
    for part in parts:
        count = part.shape[0]
        part[...] = grad[start : start + count].astype(part.dtype)
        start += count


def pass_kernel(own, across, got, after, out, *, index):
    size = own.shape[0]
    if got.shape[0] == size:
        out[:size, :] = (own[...].astype(f32) + got[...].astype(f32)).astype(bf16)
        out[size:, :] = across[index * size : (index + 1) * size, :]
    else:
        out[:size, :] = (own[...].astype(f32) + got[:size, :].astype(f32)).astype(bf16)
        part = across[index * size : (index + 1) * size, :].astype(f32)
        out[size:, :] = (part + got[size:, :].astype(f32)).astype(bf16)


def owner_kernel(at, own, got, after, keep, send):
    size = own.shape[0]
    core = at[1] == 0
    share = own.shape[1] // 4
    mine = own[...] + got[:size, :].astype(f32)
    theirs = got[size:, :].astype(f32)
    low, high = jnp.where(core, mine, theirs), jnp.where(core, theirs, mine)
    for index, rows in enumerate((low, high)):
        place = slice(index * size, (index + 1) * size)
        even, odd = columns(rows, share)
        keep[place, :] = jnp.where(core, even, odd)
        send[place, :] = jnp.where(core, odd, even).astype(bf16)


def split_kernel(kept, got, after, near, *far):
    rows = near.shape[0]
    near[...] = kept[:rows, :] + got[:rows, :].astype(f32)
    for index, ref in enumerate(far):
        part = slice((index + 1) * rows, (index + 2) * rows)
        ref[...] = (kept[part, :] + got[part, :].astype(f32)).astype(bf16)


def join_kernel(near, first, second, third, keep, send):
    total = near[...] + first[...].astype(f32) + second[...].astype(f32) + third[...].astype(f32)
    half = keep.shape[0]
    keep[...] = total[:half]
    send[...] = total[half:].astype(bf16)


def head_kernel(kept, got, state, head, gain, grad):
    width = grad.shape[1]
    upstream = kept[...] + got[...].astype(f32)
    text_dir = state[:, :width]
    inner = jnp.sum(text_dir * upstream, axis=-1, keepdims=True)
    grad_embed = (upstream - text_dir * inner) * state[:, 2 * width : 2 * width + 1]
    grad_normed = contract_cols(grad_embed.astype(bf16), head[...])
    scaled, inverse = state[:, width : 2 * width], state[:, 2 * width + 1 : 2 * width + 2]
    grad[...] = norm_back(grad_normed, gain[...], scaled, inverse).astype(bf16)


def backward_kernel(
    at, gathered, pre, scaled, gain, fc1, fc2, keep, send, rest, value, norm, sems
):
    load_pre = pltpu.make_async_copy(pre, value, sems.at[0])
    load_norm = pltpu.make_async_copy(scaled, norm, sems.at[1])
    load_pre.start()
    load_norm.start()
    quarter = gathered.shape[0] // 4
    first, second, third, fourth = (
        gathered[index * quarter : (index + 1) * quarter, :] for index in range(4)
    )
    grad = jnp.concatenate([first, third, second, fourth], axis=0)
    share = grad.shape[1] // 4
    units = fc1.shape[0]
    core = at[1] == 0
    own = jnp.where(core, *columns(grad, share))
    rest[...] = jnp.where(at[0] == 0, own[:, :share], own[:, share:])
    grad_act = contract_cols(grad, fc2[...])
    load_pre.wait()
    grad_pre = (grad_act * gelu_slope(value[:, :units])).astype(bf16)
    part = jnp.dot(grad_pre, fc1[...], preferred_element_type=f32)
    load_norm.wait()
    part = norm_back(part, gain[...], norm[...], value[:, units : units + 1])
    even, odd = columns(part, share)
    keep[...] = jnp.where(core, even, odd)
    send[...] = jnp.where(core, odd, even).astype(bf16)


def halve_kernel(at, kept, got, keep, send):
    total = kept[...] + got[...].astype(f32)
    half = keep.shape[1]
    low, high = total[:, :half], total[:, half:]
    side = at[0] == 0
    keep[...] = jnp.where(side, low, high)
    send[...] = jnp.where(side, high, low).astype(bf16)


def hidden_kernel(kept, got, rest, out):
    out[...] = rest[...].astype(f32) + (kept[...] + got[...].astype(f32))


def total_kernel(kept, got, out):
    out[...] = kept[...] + got[...].astype(f32)


def shards(
    images,
    hidden_in,
    norm1_gain,
    norm1_bias,
    fc1,
    fc1_bias,
    fc2,
    norm2_gain,
    norm2_bias,
    head,
    log_scale,
    logit_bias,
):
    block, width = images.shape
    quarter = block // 4
    share = width // 4
    units = fc1.shape[1]
    half = block // 2
    yl_at, c_at = (lax.axis_index(a) for a in ("yl", "c"))
    at = jnp.stack([yl_at, c_at]).astype(jnp.int32)
    fc1 = fc1.T

    low = shape(half, width, dtype=bf16)
    pad = (units // 128 + 1) * 128
    pre, scaled_in, keep, *sends = call(
        forward_kernel,
        [shape(block, pad), shape(block, width), shape(quarter, width)]
        + [shape(quarter, width, dtype=bf16)] * 3,
        [smem] + [hbm] * 6,
        [
            pltpu.VMEM((block, width), f32),
            pltpu.VMEM((width,), f32),
            pltpu.VMEM((width,), f32),
            pltpu.VMEM((units,), f32),
            pltpu.VMEM((units, width), bf16),
            pltpu.VMEM((units, width), bf16),
            pltpu.VMEM((block, pad), f32),
            pltpu.VMEM((block, width), f32),
            pltpu.VMEM((block, width), f32),
            pltpu.SemaphoreType.DMA((8,)),
        ],
        limit=58,
        out_specs=[hbm] * 2 + [vmem] * 4,
    )(at, hidden_in, norm1_gain, norm1_bias, fc1, fc1_bias, fc2)
    first = ring(images, 1)
    sends = [
        lax.ppermute(send, ("yl", "c"), [(i, i ^ bits) for i in range(4)])
        for send, bits in zip(sends, (1, 2, 3))
    ]
    second = ring(lax.optimization_barrier((first, sends[0]))[0], 1)
    text_unit, state = call(
        embed_kernel,
        [shape(quarter, width, dtype=bf16), shape(quarter, 2 * width + 128)],
        [vmem] * 7,
        limit=10,
        cost=20001000,
    )(
        keep,
        *sends,
        norm2_gain,
        norm2_bias,
        head,
    )

    third = ring(lax.optimization_barrier((second, text_unit))[0], 1)

    near = call(
        functools.partial(stack_kernel, count=2), [shape(half, width, dtype=bf16)], [vmem] * 2, cost=20001000
    )(text_unit, facing(text_unit))[0]
    fourth, across = call(
        parts_kernel,
        [low, shape(3 * half, width, dtype=bf16)],
        [smem] + [vmem] * 3,
    )(at, first, second, third)
    own = call(
        functools.partial(stack_kernel, count=4),
        [shape(4 * half, width, dtype=bf16)],
        [vmem] * 4 + [anywhere] * 2,
        cost=20001000,
    )(near, *(shift(near, "x", hop) for hop in hops[1:]), fourth, across)[0]
    fourth, across = ring(fourth, 1), shift(across, "c", 1)
    own, fourth, across = lax.optimization_barrier((own, fourth, across))
    other = shift(own, "c", 1)

    many = 8 * half
    image_unit, image_rows, inverse_image = call(
        norm_kernel,
        [shape(many, width, dtype=bf16)] * 2 + [shape(many, 1)],
        [smem] + [vmem] * 6,
        limit=12,
        cost=1000,
    )(at, fourth, third, second, first, across, images)
    coef, keep, send = call(
        functools.partial(pairs_kernel, chunk=many // 2, quarter=quarter),
        [
            shape(many, 8 * half, dtype=bf16),
            shape(4 * half, width),
            shape(4 * half, width, dtype=bf16),
        ],
        [smem] + [vmem] * 5,
        limit=20,
        cost=1000,
    )(at, log_scale.reshape(1, 1), logit_bias.reshape(1, 1), image_unit, own, other)
    got = shift(send, "c", 1)

    fourth, across = call(
        functools.partial(images_kernel, first=0),
        [low, shape(3 * half, width, dtype=bf16)],
        [vmem] * 5,
        limit=12,
    )(image_rows, inverse_image, coef, own, other)
    near, *far = call(
        split_kernel,
        [shape(half, width)] + [low] * 3,
        [vmem] * 2 + [anywhere],
    )(keep, got, fourth)
    far = [shift(far[index], "x", 4 - hop) for index, hop in enumerate(hops[1:])]
    fourth, across = ring(fourth, -1), shift(across, "c", 1)
    *parts, image_part = call(
        functools.partial(images_kernel, first=4),
        [low] * 3 + [shape(half, width)],
        [vmem] * 5,
        limit=12,
    )(image_rows, inverse_image, coef, own, other)

    def onward(index, got, after):
        moving = call(
            functools.partial(pass_kernel, index=index),
            [shape(block, width, dtype=bf16)],
            [vmem] * 3 + [anywhere],
        )(parts[index], across, got, after)[0]
        return ring(moving, -1)

    moved = onward(0, fourth, near)
    keep, send = call(
        join_kernel,
        [shape(quarter, width), shape(quarter, width, dtype=bf16)],
        [vmem] * 4,
        cost=60001000,
    )(near, *far)
    moved = onward(1, moved, keep)
    grad_mixed = call(
        head_kernel, [shape(quarter, width, dtype=bf16)], [vmem] * 5, limit=10, cost=60001000
    )(keep, facing(send), state, head, norm2_gain)[0]
    grad_mixed = lax.all_gather(grad_mixed, ("yl", "c"), axis=0, tiled=True)
    moved = onward(2, moved, grad_mixed)
    keep, send, rest = call(
        backward_kernel,
        [
            shape(block, 2 * share),
            shape(block, 2 * share, dtype=bf16),
            shape(block, share, dtype=bf16),
        ],
        [smem, vmem, hbm, hbm, vmem, vmem, vmem],
        [
            pltpu.VMEM((block, pad), f32),
            pltpu.VMEM((block, width), f32),
            pltpu.SemaphoreType.DMA((2,)),
        ],
        limit=16,
        cost=15000000,
    )(at, grad_mixed, pre, scaled_in, norm1_gain, fc1, fc2)
    keep, send = call(
        halve_kernel,
        [shape(block, share), shape(block, share, dtype=bf16)],
        [smem, vmem, vmem],
    )(at, keep, shift(send, "c", 1))
    hidden_keep = keep
    grad_hidden = call(hidden_kernel, [shape(block, share)], [vmem] * 3)(
        keep, shift(send, "yl", 1), rest
    )[0]

    keep, send = call(
        owner_kernel,
        [shape(block, 2 * share), shape(block, 2 * share, dtype=bf16)],
        [smem] + [vmem] * 2 + [anywhere],
    )(at, image_part, moved, hidden_keep)
    keep, send = call(
        halve_kernel,
        [shape(block, share), shape(block, share, dtype=bf16)],
        [smem, vmem, vmem],
    )(at, keep, shift(send, "c", 1))
    grad_images = call(total_kernel, [shape(block, share)], [vmem] * 2)(
        keep, shift(send, "yl", 1)
    )[0]
    return (grad_images, grad_hidden)


def solution(mesh):
    grid = Mesh(mesh.devices.reshape(8, 4, 2, 2, 2), ("z", "x", "yh", "yl", "c"))
    dp, mp = ("z", "x", "yh"), ("yl", "c")
    placed = (
        P(dp, None),
        P(dp, None),
        P(),
        P(),
        P(None, mp),
        P(mp),
        P(mp, None),
        P(),
        P(),
        P(),
        P(),
        P(),
    )
    return jax.shard_map(
        shards,
        mesh=grid,
        in_specs=placed,
        out_specs=(P(dp, mp), P(dp, mp)),
        check_vma=False,
    )
```

```python
import functools

import jax
import jax.numpy as jnp
from jax import lax
from jax.experimental import pallas as pl
from jax.experimental.pallas import tpu as pltpu
from jax.sharding import Mesh, PartitionSpec as P

eps = 1e-06
hops = (0, 1, 3, 2)
f32 = jnp.float32
bf16 = jnp.bfloat16


def normalize(values, gain, shift):
    mean = jnp.mean(values, axis=-1, keepdims=True)
    centered = values - mean
    inverse = lax.rsqrt(jnp.mean(centered * centered, axis=-1, keepdims=True) + eps)
    scaled = centered * inverse
    return (scaled * gain + shift, scaled, inverse)


def gelu_slope(values):
    factor = 0.7978845608028654
    inner = factor * (values + 0.044715 * values * values * values)
    tangent = jnp.tanh(inner)
    return 0.5 * (1.0 + tangent) + 0.5 * values * (1.0 - tangent * tangent) * factor * (
        1.0 + 3.0 * 0.044715 * values * values
    )


def norm_back(upstream, gain, scaled, inverse):
    grad = upstream * gain
    return inverse * (
        grad
        - jnp.mean(grad, axis=-1, keepdims=True)
        - scaled * jnp.mean(grad * scaled, axis=-1, keepdims=True)
    )


def contract_rows(left, right):
    return lax.dot_general(left, right, (((0,), (0,)), ((), ())), preferred_element_type=f32)


def contract_cols(left, right):
    return lax.dot_general(left, right, (((1,), (1,)), ((), ())), preferred_element_type=f32)


def shift(values, axes, step):
    size = lax.axis_size(axes)
    return lax.ppermute(values, axes, [(i, (i + step) % size) for i in range(size)])


def ring(values, sign):
    size = lax.axis_size("z")
    pairs = []
    for z in range(size):
        pairs.append((2 * z, (z + sign) % size * 2))
        pairs.append((2 * z + 1, (z - sign) % size * 2 + 1))
    return lax.ppermute(values, ("z", "c"), pairs)


def facing(values):
    return lax.ppermute(values, ("yh", "yl"), [(0, 3), (3, 0), (1, 2), (2, 1)])


def columns(values, share):
    even = jnp.concatenate([values[..., :share], values[..., 2 * share : 3 * share]], axis=-1)
    odd = jnp.concatenate([values[..., share : 2 * share], values[..., 3 * share :]], axis=-1)
    return even, odd


vmem = pl.BlockSpec(memory_space=pltpu.VMEM)
smem = pl.BlockSpec(memory_space=pltpu.SMEM)
hbm = pl.BlockSpec(memory_space=pltpu.HBM)
anywhere = pl.BlockSpec(memory_space=pl.ANY)


def call(kernel, outs, in_specs, scratch=(), limit=6, out_specs=None, cost=1000):
    return pl.pallas_call(
        kernel,
        out_shape=outs,
        in_specs=in_specs,
        out_specs=out_specs or [vmem] * len(outs),
        scratch_shapes=scratch,
        cost_estimate=pl.CostEstimate(flops=300*cost, bytes_accessed=cost, transcendentals=0),
        compiler_params=pltpu.CompilerParams(vmem_limit_bytes=limit * 1024 * 1024),
    )


def shape(*dims, dtype=f32):
    return jax.ShapeDtypeStruct(dims, dtype)


def forward_kernel(
    at, hidden, gain, bias, fc1, fc1_bias, fc2, pre, scaled, keep, send_c, send_y, send_b,
    rows, line1, line2, line3, w1, w2, value, norm, part, sems,
):
    loads = [
        pltpu.make_async_copy(source, target, sems.at[index])
        for index, (source, target) in enumerate(
            [
                (hidden, rows),
                (gain, line1),
                (bias, line2),
                (fc1, w1),
                (fc1_bias, line3),
                (fc2, w2),
            ]
        )
    ]
    for load in loads:
        load.start()
    for load in loads[:3]:
        load.wait()
    units = fc1.shape[0]
    normed, norm[...], inverse = normalize(rows[...], line1[...], line2[...])
    normed = normed.astype(bf16)
    save_norm = pltpu.make_async_copy(norm, scaled, sems.at[6])
    save_norm.start()
    loads[3].wait()
    loads[4].wait()
    linear = contract_cols(normed, w1[...]) + line3[...]
    value[:, :units] = linear
    value[:, units : units + 1] = inverse
    save_pre = pltpu.make_async_copy(value, pre, sems.at[7])
    save_pre.start()
    act = jax.nn.gelu(linear, approximate=True).astype(bf16)
    loads[5].wait()
    part[...] = jnp.dot(act, w2[...], preferred_element_type=f32)
    quarter = keep.shape[0]
    side, core = at[0] // 2, at[0] % 2

    def own(core, side):
        return pl.ds(pl.multiple_of((core * 2 + side) * quarter, quarter), quarter)

    keep[...] = rows[own(core, side), :] + part[own(core, side), :]
    send_c[...] = part[own(1 - core, side), :].astype(bf16)
    send_y[...] = part[own(core, 1 - side), :].astype(bf16)
    send_b[...] = part[own(1 - core, 1 - side), :].astype(bf16)
    save_norm.wait()
    save_pre.wait()


def hold_kernel(kept, got, out):
    out[...] = kept[...] + got[...].astype(f32)


def embed_kernel(kept, got_y, got_b, gain, bias, head, unit, state):
    width = unit.shape[1]
    mixed = kept[...] + got_y[...].astype(f32) + got_b[...].astype(f32)
    normed, scaled, inverse = normalize(mixed, gain[...], bias[...])
    state[:, width : 2 * width] = scaled
    embed = jnp.dot(normed.astype(bf16), head[...], preferred_element_type=f32)
    level = lax.rsqrt(jnp.sum(embed * embed, axis=-1, keepdims=True) + eps)
    unit[...] = (embed * level).astype(bf16)
    state[:, :width] = embed * level
    state[:, 2 * width : 2 * width + 1] = level
    state[:, 2 * width + 1 : 2 * width + 2] = inverse


def stack_kernel(*refs, count):
    rows = refs[0].shape[0]
    for index, ref in enumerate(refs[:count]):
        refs[-1][index * rows : (index + 1) * rows, :] = ref[...]


def parts_kernel(at, first, second, third, half, send):
    rows = half.shape[0]
    own = pl.ds(pl.multiple_of(at[0] % 2 * rows, rows), rows)
    other = pl.ds(pl.multiple_of((1 - at[0] % 2) * rows, rows), rows)
    half[...] = third[own, :]
    for index, ref in enumerate((third, second, first)):
        send[index * rows : (index + 1) * rows, :] = ref[other, :]


def norm_kernel(at, fourth, third, second, first, across, images, unit, image_rows, inverse):
    size = fourth.shape[0]
    mine = pl.ds(pl.multiple_of(at[0] % 2 * size, size), size)

    def put(index, values):
        rows = slice(index * size, (index + 1) * size)
        image_rows[rows, :] = values
        wide = values.astype(f32)
        level = lax.rsqrt(jnp.sum(wide * wide, axis=-1, keepdims=True) + eps)
        inverse[rows, :] = level
        unit[rows, :] = (wide * level).astype(bf16)

    put(0, fourth[...])
    for index in range(3):
        put(1 + index, across[index * size : (index + 1) * size, :])
    for index, ref in enumerate((third, second, first, images)):
        put(4 + index, ref[mine, :])


def near_kernel(at, log_scale, offset, unit, own, coef, *, chunk, quarter):
    scale = jnp.exp(log_scale[...])
    size = unit.shape[0] // 8
    diagonal = 7 * size + at[0] // 2 * quarter
    for start in range(0, unit.shape[0], chunk):
        rows = slice(start, start + chunk)
        chance = jax.nn.sigmoid(scale * contract_cols(unit[rows, :], own[...]) + offset[...])
        line = lax.broadcasted_iota(jnp.int32, chance.shape, 0) + (start - diagonal)
        cols = lax.broadcasted_iota(jnp.int32, chance.shape, 1)
        ident = ((line == cols) & (cols < quarter)).astype(f32)
        coef[rows, :] = (scale * (chance - ident)).astype(bf16)


def pairs_kernel(log_scale, offset, unit, other, near, coef, keep, send, *, chunk):
    scale = jnp.exp(log_scale[...])
    for start in range(0, unit.shape[0], chunk):
        rows = slice(start, start + chunk)
        chance = jax.nn.sigmoid(scale * contract_cols(unit[rows, :], other[...]) + offset[...])
        coef[rows, :] = (scale * chance).astype(bf16)
    send[...] = contract_rows(coef[...], unit[...]).astype(bf16)
    keep[...] = contract_rows(near[...], unit[...])


def images_kernel(images, inverse, near, coef, own, other, *parts, first):
    size = images.shape[0] // 8
    rows = slice(first * size, (first + 4) * size)
    grad = jnp.dot(near[rows, :], own[...], preferred_element_type=f32)
    grad = grad + jnp.dot(coef[rows, :], other[...], preferred_element_type=f32)
    level = inverse[rows, :]
    direct = images[rows, :].astype(f32) * level
    inner = jnp.sum(direct * grad, axis=-1, keepdims=True)
    grad = (grad - direct * inner) * level
    start = 0
    for part in parts:
        count = part.shape[0]
        part[...] = grad[start : start + count].astype(part.dtype)
        start += count


def pass_kernel(own, across, got, after, out, *, index):
    size = own.shape[0]
    if got.shape[0] == size:
        out[:size, :] = (own[...].astype(f32) + got[...].astype(f32)).astype(bf16)
        out[size:, :] = across[index * size : (index + 1) * size, :]
    else:
        out[:size, :] = (own[...].astype(f32) + got[:size, :].astype(f32)).astype(bf16)
        part = across[index * size : (index + 1) * size, :].astype(f32)
        out[size:, :] = (part + got[size:, :].astype(f32)).astype(bf16)


def owner_kernel(at, own, got, after, keep, send):
    size = own.shape[0]
    core = at[0] % 2 == 0
    share = own.shape[1] // 4
    mine = own[...] + got[:size, :].astype(f32)
    theirs = got[size:, :].astype(f32)
    low, high = jnp.where(core, mine, theirs), jnp.where(core, theirs, mine)
    for index, rows in enumerate((low, high)):
        place = slice(index * size, (index + 1) * size)
        even, odd = columns(rows, share)
        keep[place, :] = jnp.where(core, even, odd)
        send[place, :] = jnp.where(core, odd, even).astype(bf16)


def split_kernel(kept, got, after, near, *far):
    rows = near.shape[0]
    near[...] = kept[:rows, :] + got[:rows, :].astype(f32)
    for index, ref in enumerate(far):
        part = slice((index + 1) * rows, (index + 2) * rows)
        ref[...] = (kept[part, :] + got[part, :].astype(f32)).astype(bf16)


def join_kernel(near, first, second, third, keep, send):
    total = near[...] + first[...].astype(f32) + second[...].astype(f32) + third[...].astype(f32)
    half = keep.shape[0]
    keep[...] = total[:half]
    send[...] = total[half:].astype(bf16)


def head_kernel(kept, got, state, head, gain, grad):
    width = grad.shape[1]
    upstream = kept[...] + got[...].astype(f32)
    text_dir = state[:, :width]
    inner = jnp.sum(text_dir * upstream, axis=-1, keepdims=True)
    grad_embed = (upstream - text_dir * inner) * state[:, 2 * width : 2 * width + 1]
    grad_normed = contract_cols(grad_embed.astype(bf16), head[...])
    scaled, inverse = state[:, width : 2 * width], state[:, 2 * width + 1 : 2 * width + 2]
    grad[...] = norm_back(grad_normed, gain[...], scaled, inverse).astype(bf16)


def backward_kernel(
    at, own_rows, other_rows, pre, scaled, gain, fc1, fc2, keep, send, rest, grad, value, norm, sems
):
    load_pre = pltpu.make_async_copy(pre, value, sems.at[0])
    load_norm = pltpu.make_async_copy(scaled, norm, sems.at[1])
    load_pre.start()
    load_norm.start()
    quarter = grad.shape[0] // 4
    row_side, row_core = at[0] // 2, at[0] % 2
    for index, ref in enumerate((own_rows, other_rows)):
        start = row_core if index == 0 else 1 - row_core
        for step in range(2):
            place = start * 2 + (row_side if step == 0 else 1 - row_side)
            rows = pl.ds(pl.multiple_of(place * quarter, quarter), quarter)
            grad[rows, :] = ref[step * quarter : (step + 1) * quarter, :]
    share = grad.shape[1] // 4
    units = fc1.shape[0]
    core = at[0] % 2 == 0
    own = jnp.where(core, *columns(grad[...], share))
    rest[...] = jnp.where(at[0] // 2 == 0, own[:, :share], own[:, share:])
    grad_act = contract_cols(grad[...], fc2[...])
    load_pre.wait()
    grad_pre = (grad_act * gelu_slope(value[:, :units])).astype(bf16)
    part = jnp.dot(grad_pre, fc1[...], preferred_element_type=f32)
    load_norm.wait()
    part = norm_back(part, gain[...], norm[...], value[:, units : units + 1])
    even, odd = columns(part, share)
    keep[...] = jnp.where(core, even, odd)
    send[...] = jnp.where(core, odd, even).astype(bf16)


def halve_kernel(at, kept, got, keep, send):
    total = kept[...] + got[...].astype(f32)
    half = keep.shape[1]
    low, high = total[:, :half], total[:, half:]
    side = at[0] // 2 == 0
    keep[...] = jnp.where(side, low, high)
    send[...] = jnp.where(side, high, low).astype(bf16)


def hidden_kernel(kept, got, rest, out):
    out[...] = rest[...].astype(f32) + (kept[...] + got[...].astype(f32))


def total_kernel(kept, got, out):
    out[...] = kept[...] + got[...].astype(f32)


def shards(
    images,
    hidden_in,
    norm1_gain,
    norm1_bias,
    fc1,
    fc1_bias,
    fc2,
    norm2_gain,
    norm2_bias,
    head,
    log_scale,
    logit_bias,
):
    block, width = images.shape
    quarter = block // 4
    share = width // 4
    units = fc1.shape[1]
    half = block // 2
    at = lax.axis_index(("yl", "c")).astype(jnp.int32).reshape(1)
    fc1 = fc1.T

    low = shape(half, width, dtype=bf16)
    pad = (units // 128 + 1) * 128
    pre, scaled_in, keep, *sends = call(
        forward_kernel,
        [shape(block, pad), shape(block, width), shape(quarter, width)]
        + [shape(quarter, width, dtype=bf16)] * 3,
        [smem] + [hbm] * 6,
        [
            pltpu.VMEM((block, width), f32),
            pltpu.VMEM((width,), f32),
            pltpu.VMEM((width,), f32),
            pltpu.VMEM((units,), f32),
            pltpu.VMEM((units, width), bf16),
            pltpu.VMEM((units, width), bf16),
            pltpu.VMEM((block, pad), f32),
            pltpu.VMEM((block, width), f32),
            pltpu.VMEM((block, width), f32),
            pltpu.SemaphoreType.DMA((8,)),
        ],
        limit=58,
        out_specs=[hbm] * 2 + [vmem] * 4,
    )(at, hidden_in, norm1_gain, norm1_bias, fc1, fc1_bias, fc2)
    first = ring(images, 1)
    sends = [
        lax.ppermute(send, ("yl", "c"), [(i, i ^ bits) for i in range(4)])
        for send, bits in zip(sends, (1, 2, 3))
    ]
    keep = call(hold_kernel, [shape(quarter, width)], [vmem] * 2, cost=1000)(keep, sends[0])[0]
    second = ring(lax.optimization_barrier((first, keep))[0], 1)
    text_unit, state = call(
        embed_kernel,
        [shape(quarter, width, dtype=bf16), shape(quarter, 2 * width + 128)],
        [vmem] * 6,
        limit=10,
        cost=20001000,
    )(
        keep,
        *sends[1:],
        norm2_gain,
        norm2_bias,
        head,
    )

    third = ring(lax.optimization_barrier((second, text_unit))[0], 1)

    near = call(
        functools.partial(stack_kernel, count=2), [shape(half, width, dtype=bf16)], [vmem] * 2, cost=20001000
    )(text_unit, facing(text_unit))[0]
    fourth, across = call(
        parts_kernel,
        [low, shape(3 * half, width, dtype=bf16)],
        [smem] + [vmem] * 3,
    )(at, first, second, third)
    own = call(
        functools.partial(stack_kernel, count=4),
        [shape(4 * half, width, dtype=bf16)],
        [vmem] * 4 + [anywhere] * 2,
        cost=20001000,
    )(near, *(shift(near, "x", hop) for hop in hops[1:]), fourth, across)[0]
    fourth, across = ring(fourth, 1), shift(across, "c", 1)
    own, fourth, across = lax.optimization_barrier((own, fourth, across))
    other = shift(own, "c", 1)

    many = 8 * half
    image_unit, image_rows, inverse_image = call(
        norm_kernel,
        [shape(many, width, dtype=bf16)] * 2 + [shape(many, 1)],
        [smem] + [vmem] * 6,
        limit=12,
        cost=1000,
    )(at, fourth, third, second, first, across, images)
    level = (log_scale.reshape(1, 1), logit_bias.reshape(1, 1))
    near_coef = call(
        functools.partial(near_kernel, chunk=many // 2, quarter=quarter),
        [shape(many, 4 * half, dtype=bf16)],
        [smem] + [vmem] * 4,
        limit=12,
        cost=1000,
    )(at, *level, image_unit, own)[0]
    coef, keep, send = call(
        functools.partial(pairs_kernel, chunk=many // 2),
        [
            shape(many, 4 * half, dtype=bf16),
            shape(4 * half, width),
            shape(4 * half, width, dtype=bf16),
        ],
        [vmem] * 5,
        limit=16,
    )(*level, image_unit, other, near_coef)
    got = shift(send, "c", 1)

    fourth, across = call(
        functools.partial(images_kernel, first=0),
        [low, shape(3 * half, width, dtype=bf16)],
        [vmem] * 6,
        limit=12,
    )(image_rows, inverse_image, near_coef, coef, own, other)
    near, *far = call(
        split_kernel,
        [shape(half, width)] + [low] * 3,
        [vmem] * 2 + [anywhere],
    )(keep, got, fourth)
    far = [shift(far[index], "x", 4 - hop) for index, hop in enumerate(hops[1:])]
    fourth, across = ring(fourth, -1), shift(across, "c", 1)
    *parts, image_part = call(
        functools.partial(images_kernel, first=4),
        [low] * 3 + [shape(half, width)],
        [vmem] * 6,
        limit=12,
    )(image_rows, inverse_image, near_coef, coef, own, other)

    def onward(index, got, after):
        moving = call(
            functools.partial(pass_kernel, index=index),
            [shape(block, width, dtype=bf16)],
            [vmem] * 3 + [anywhere],
        )(parts[index], across, got, after)[0]
        return ring(moving, -1)

    moved = onward(0, fourth, near)
    keep, send = call(
        join_kernel,
        [shape(quarter, width), shape(quarter, width, dtype=bf16)],
        [vmem] * 4,
        cost=60001000,
    )(near, *far)
    moved = onward(1, moved, keep)
    grad_mixed = call(
        head_kernel, [shape(quarter, width, dtype=bf16)], [vmem] * 5, limit=10, cost=60001000
    )(keep, facing(send), state, head, norm2_gain)[0]
    moved = onward(2, moved, grad_mixed)
    grad_mixed = call(
        functools.partial(stack_kernel, count=2), [low], [vmem] * 2, cost=1000
    )(grad_mixed, shift(grad_mixed, "yl", 1))[0]
    keep, send, rest = call(
        backward_kernel,
        [
            shape(block, 2 * share),
            shape(block, 2 * share, dtype=bf16),
            shape(block, share, dtype=bf16),
        ],
        [smem, vmem, vmem, hbm, hbm, vmem, vmem, vmem],
        [
            pltpu.VMEM((block, width), bf16),
            pltpu.VMEM((block, pad), f32),
            pltpu.VMEM((block, width), f32),
            pltpu.SemaphoreType.DMA((2,)),
        ],
        limit=16,
        cost=15000000,
    )(at, grad_mixed, shift(grad_mixed, "c", 1), pre, scaled_in, norm1_gain, fc1, fc2)
    keep, send = call(
        halve_kernel,
        [shape(block, share), shape(block, share, dtype=bf16)],
        [smem, vmem, vmem],
    )(at, keep, shift(send, "c", 1))
    hidden_keep = keep
    grad_hidden = call(hidden_kernel, [shape(block, share)], [vmem] * 3)(
        keep, shift(send, "yl", 1), rest
    )[0]

    keep, send = call(
        owner_kernel,
        [shape(block, 2 * share), shape(block, 2 * share, dtype=bf16)],
        [smem] + [vmem] * 2 + [anywhere],
    )(at, image_part, moved, hidden_keep)
    keep, send = call(
        halve_kernel,
        [shape(block, share), shape(block, share, dtype=bf16)],
        [smem, vmem, vmem],
    )(at, keep, shift(send, "c", 1))
    grad_images = call(total_kernel, [shape(block, share)], [vmem] * 2)(
        keep, shift(send, "yl", 1)
    )[0]
    return (grad_images, grad_hidden)


def solution(mesh):
    grid = Mesh(mesh.devices.reshape(8, 4, 2, 2, 2), ("z", "x", "yh", "yl", "c"))
    dp, mp = ("z", "x", "yh"), ("yl", "c")
    placed = (
        P(dp, None),
        P(dp, None),
        P(),
        P(),
        P(None, mp),
        P(mp),
        P(mp, None),
        P(),
        P(),
        P(),
        P(),
        P(),
    )
    return jax.shard_map(
        shards,
        mesh=grid,
        in_specs=placed,
        out_specs=(P(dp, mp), P(dp, mp)),
        check_vma=False,
    )
```

```python
import functools

import jax
import jax.numpy as jnp
from jax import lax
from jax.experimental import pallas as pl
from jax.experimental.pallas import tpu as pltpu
from jax.sharding import Mesh, PartitionSpec as P

eps = 1e-06
hops = (0, 1, 3, 2)
f32 = jnp.float32
bf16 = jnp.bfloat16


def normalize(values, gain, shift):
    mean = jnp.mean(values, axis=-1, keepdims=True)
    centered = values - mean
    inverse = lax.rsqrt(jnp.mean(centered * centered, axis=-1, keepdims=True) + eps)
    scaled = centered * inverse
    return (scaled * gain + shift, scaled, inverse)


def gelu_slope(values):
    factor = 0.7978845608028654
    inner = factor * (values + 0.044715 * values * values * values)
    tangent = jnp.tanh(inner)
    return 0.5 * (1.0 + tangent) + 0.5 * values * (1.0 - tangent * tangent) * factor * (
        1.0 + 3.0 * 0.044715 * values * values
    )


def norm_back(upstream, gain, scaled, inverse):
    grad = upstream * gain
    return inverse * (
        grad
        - jnp.mean(grad, axis=-1, keepdims=True)
        - scaled * jnp.mean(grad * scaled, axis=-1, keepdims=True)
    )


def contract_rows(left, right):
    return lax.dot_general(left, right, (((0,), (0,)), ((), ())), preferred_element_type=f32)


def contract_cols(left, right):
    return lax.dot_general(left, right, (((1,), (1,)), ((), ())), preferred_element_type=f32)


def shift(values, axes, step):
    size = lax.axis_size(axes)
    return lax.ppermute(values, axes, [(i, (i + step) % size) for i in range(size)])


def ring(values, sign):
    size = lax.axis_size("z")
    pairs = []
    for z in range(size):
        pairs.append((2 * z, (z + sign) % size * 2))
        pairs.append((2 * z + 1, (z - sign) % size * 2 + 1))
    return lax.ppermute(values, ("z", "c"), pairs)


def facing(values):
    return lax.ppermute(values, ("yh", "yl"), [(0, 3), (3, 0), (1, 2), (2, 1)])


def columns(values, share):
    even = jnp.concatenate([values[..., :share], values[..., 2 * share : 3 * share]], axis=-1)
    odd = jnp.concatenate([values[..., share : 2 * share], values[..., 3 * share :]], axis=-1)
    return even, odd


vmem = pl.BlockSpec(memory_space=pltpu.VMEM)
smem = pl.BlockSpec(memory_space=pltpu.SMEM)
hbm = pl.BlockSpec(memory_space=pltpu.HBM)
anywhere = pl.BlockSpec(memory_space=pl.ANY)


def call(kernel, outs, in_specs, scratch=(), limit=6, out_specs=None, cost=1000):
    return pl.pallas_call(
        kernel,
        out_shape=outs,
        in_specs=in_specs,
        out_specs=out_specs or [vmem] * len(outs),
        scratch_shapes=scratch,
        cost_estimate=pl.CostEstimate(flops=300*cost, bytes_accessed=cost, transcendentals=0),
        compiler_params=pltpu.CompilerParams(vmem_limit_bytes=limit * 1024 * 1024),
    )


def shape(*dims, dtype=f32):
    return jax.ShapeDtypeStruct(dims, dtype)


def forward_kernel(
    at, hidden, gain, bias, fc1, fc1_bias, fc2, pre, scaled, keep, send_c, send_y, send_b,
    rows, line1, line2, line3, w1, w2, value, norm, part, sems,
):
    loads = [
        pltpu.make_async_copy(source, target, sems.at[index])
        for index, (source, target) in enumerate(
            [
                (hidden, rows),
                (gain, line1),
                (bias, line2),
                (fc1, w1),
                (fc1_bias, line3),
                (fc2, w2),
            ]
        )
    ]
    for load in loads:
        load.start()
    for load in loads[:3]:
        load.wait()
    units = fc1.shape[0]
    normed, norm[...], inverse = normalize(rows[...], line1[...], line2[...])
    normed = normed.astype(bf16)
    save_norm = pltpu.make_async_copy(norm, scaled, sems.at[6])
    save_norm.start()
    loads[3].wait()
    loads[4].wait()
    value[:, units : units + 1] = inverse
    acts = []
    cuts = ((0, 512), (512, units))
    for low, high in cuts:
        linear = contract_cols(normed, w1[low:high, :]) + line3[low:high]
        value[:, low:high] = linear
        acts.append(jax.nn.gelu(linear, approximate=True).astype(bf16))
    save_pre = pltpu.make_async_copy(value, pre, sems.at[7])
    save_pre.start()
    loads[5].wait()
    total = jnp.zeros(part.shape, f32)
    for (low, high), act in zip(cuts, acts):
        total = total + jnp.dot(act, w2[low:high, :], preferred_element_type=f32)
    part[...] = total
    quarter = keep.shape[0]
    side, core = at[0] // 2, at[0] % 2

    def own(core, side):
        return pl.ds(pl.multiple_of((core * 2 + side) * quarter, quarter), quarter)

    keep[...] = rows[own(core, side), :] + part[own(core, side), :]
    send_c[...] = part[own(1 - core, side), :].astype(bf16)
    send_y[...] = part[own(core, 1 - side), :].astype(bf16)
    send_b[...] = part[own(1 - core, 1 - side), :].astype(bf16)
    save_norm.wait()
    save_pre.wait()


def hold_kernel(kept, got, out):
    out[...] = kept[...] + got[...].astype(f32)


def embed_kernel(kept, got_y, got_b, gain, bias, head, unit, state):
    width = unit.shape[1]
    mixed = kept[...] + got_y[...].astype(f32) + got_b[...].astype(f32)
    normed, scaled, inverse = normalize(mixed, gain[...], bias[...])
    state[:, width : 2 * width] = scaled
    embed = jnp.dot(normed.astype(bf16), head[...], preferred_element_type=f32)
    level = lax.rsqrt(jnp.sum(embed * embed, axis=-1, keepdims=True) + eps)
    unit[...] = (embed * level).astype(bf16)
    state[:, :width] = embed * level
    state[:, 2 * width : 2 * width + 1] = level
    state[:, 2 * width + 1 : 2 * width + 2] = inverse


def stack_kernel(*refs, count):
    rows = refs[0].shape[0]
    for index, ref in enumerate(refs[:count]):
        refs[-1][index * rows : (index + 1) * rows, :] = ref[...]


def parts_kernel(at, first, second, third, half, send):
    rows = half.shape[0]
    own = pl.ds(pl.multiple_of(at[0] % 2 * rows, rows), rows)
    other = pl.ds(pl.multiple_of((1 - at[0] % 2) * rows, rows), rows)
    half[...] = third[own, :]
    for index, ref in enumerate((third, second, first)):
        send[index * rows : (index + 1) * rows, :] = ref[other, :]


def norm_kernel(at, fourth, third, second, first, across, images, unit, image_rows, inverse):
    size = fourth.shape[0]
    mine = pl.ds(pl.multiple_of(at[0] % 2 * size, size), size)

    def put(index, values):
        rows = slice(index * size, (index + 1) * size)
        image_rows[rows, :] = values
        wide = values.astype(f32)
        level = lax.rsqrt(jnp.sum(wide * wide, axis=-1, keepdims=True) + eps)
        inverse[rows, :] = level
        unit[rows, :] = (wide * level).astype(bf16)

    put(0, fourth[...])
    for index in range(3):
        put(1 + index, across[index * size : (index + 1) * size, :])
    for index, ref in enumerate((third, second, first, images)):
        put(4 + index, ref[mine, :])


def near_kernel(at, log_scale, offset, unit, own, coef, *, chunk, quarter):
    scale = jnp.exp(log_scale[...])
    size = unit.shape[0] // 8
    diagonal = 7 * size + at[0] // 2 * quarter
    for start in range(0, own.shape[0], chunk):
        rows = slice(start, start + chunk)
        chance = jax.nn.sigmoid(scale * contract_cols(own[rows, :], unit[...]) + offset[...])
        if start < quarter:
            line = lax.broadcasted_iota(jnp.int32, chance.shape, 0) + start
            cols = lax.broadcasted_iota(jnp.int32, chance.shape, 1) - diagonal
            chance = chance - ((line == cols) & (line < quarter)).astype(f32)
        coef[rows, :] = (scale * chance).astype(bf16)


def pairs_kernel(log_scale, offset, unit, other, near, coef, keep, send, *, chunk):
    scale = jnp.exp(log_scale[...])
    for start in range(0, other.shape[0], chunk):
        rows = slice(start, start + chunk)
        chance = jax.nn.sigmoid(scale * contract_cols(other[rows, :], unit[...]) + offset[...])
        low = (scale * chance).astype(bf16)
        coef[rows, :] = low
        send[rows, :] = jnp.dot(low, unit[...], preferred_element_type=f32).astype(bf16)
    keep[...] = jnp.dot(near[...], unit[...], preferred_element_type=f32)


def images_kernel(images, inverse, near, coef, own, other, *parts, first):
    size = images.shape[0] // 8
    rows = slice(first * size, (first + 4) * size)
    grad = contract_rows(near[:, rows], own[...])
    grad = grad + contract_rows(coef[:, rows], other[...])
    level = inverse[rows, :]
    direct = images[rows, :].astype(f32) * level
    inner = jnp.sum(direct * grad, axis=-1, keepdims=True)
    grad = (grad - direct * inner) * level
    start = 0
    for part in parts:
        count = part.shape[0]
        part[...] = grad[start : start + count].astype(part.dtype)
        start += count


def pass_kernel(own, across, got, after, out, *, index):
    size = own.shape[0]
    if got.shape[0] == size:
        out[:size, :] = (own[...].astype(f32) + got[...].astype(f32)).astype(bf16)
        out[size:, :] = across[index * size : (index + 1) * size, :]
    else:
        out[:size, :] = (own[...].astype(f32) + got[:size, :].astype(f32)).astype(bf16)
        part = across[index * size : (index + 1) * size, :].astype(f32)
        out[size:, :] = (part + got[size:, :].astype(f32)).astype(bf16)


def owner_kernel(at, own, got, after, keep, send):
    size = own.shape[0]
    core = at[0] % 2 == 0
    share = own.shape[1] // 4
    mine = own[...] + got[:size, :].astype(f32)
    theirs = got[size:, :].astype(f32)
    low, high = jnp.where(core, mine, theirs), jnp.where(core, theirs, mine)
    for index, rows in enumerate((low, high)):
        place = slice(index * size, (index + 1) * size)
        even, odd = columns(rows, share)
        keep[place, :] = jnp.where(core, even, odd)
        send[place, :] = jnp.where(core, odd, even).astype(bf16)


def split_kernel(kept, got, after, near, *far):
    rows = near.shape[0]
    near[...] = kept[:rows, :] + got[:rows, :].astype(f32)
    for index, ref in enumerate(far):
        part = slice((index + 1) * rows, (index + 2) * rows)
        ref[...] = (kept[part, :] + got[part, :].astype(f32)).astype(bf16)


def join_kernel(near, first, second, third, after, keep, send):
    total = near[...] + first[...].astype(f32) + second[...].astype(f32) + third[...].astype(f32)
    half = keep.shape[0]
    keep[...] = total[:half]
    send[...] = total[half:].astype(bf16)


def head_kernel(kept, got, state, head, gain, grad):
    width = grad.shape[1]
    upstream = kept[...] + got[...].astype(f32)
    text_dir = state[:, :width]
    inner = jnp.sum(text_dir * upstream, axis=-1, keepdims=True)
    grad_embed = (upstream - text_dir * inner) * state[:, 2 * width : 2 * width + 1]
    grad_normed = contract_cols(grad_embed.astype(bf16), head[...])
    scaled, inverse = state[:, width : 2 * width], state[:, 2 * width + 1 : 2 * width + 2]
    grad[...] = norm_back(grad_normed, gain[...], scaled, inverse).astype(bf16)


def slope_kernel(pre, after, out, *, units):
    out[:, :units] = gelu_slope(pre[:, :units])
    out[:, units : units + 1] = pre[:, units : units + 1]


def backward_kernel(
    at, own_rows, other_rows, slope, scaled, gain, fc1, fc2, keep, send, rest, grad
):
    quarter = grad.shape[0] // 4
    row_side, row_core = at[0] // 2, at[0] % 2
    for index, ref in enumerate((own_rows, other_rows)):
        start = row_core if index == 0 else 1 - row_core
        for step in range(2):
            place = start * 2 + (row_side if step == 0 else 1 - row_side)
            rows = pl.ds(pl.multiple_of(place * quarter, quarter), quarter)
            grad[rows, :] = ref[step * quarter : (step + 1) * quarter, :]
    share = grad.shape[1] // 4
    units = fc1.shape[0]
    core = at[0] % 2 == 0
    own = jnp.where(core, *columns(grad[...], share))
    rest[...] = jnp.where(at[0] // 2 == 0, own[:, :share], own[:, share:])
    grad_act = contract_cols(grad[...], fc2[...])
    grad_pre = (grad_act * slope[:, :units]).astype(bf16)
    part = jnp.dot(grad_pre, fc1[...], preferred_element_type=f32)
    part = norm_back(part, gain[...], scaled[...], slope[:, units : units + 1])
    even, odd = columns(part, share)
    keep[...] = jnp.where(core, even, odd)
    send[...] = jnp.where(core, odd, even).astype(bf16)


def halve_kernel(at, kept, got, keep, send):
    total = kept[...] + got[...].astype(f32)
    half = keep.shape[1]
    low, high = total[:, :half], total[:, half:]
    side = at[0] // 2 == 0
    keep[...] = jnp.where(side, low, high)
    send[...] = jnp.where(side, high, low).astype(bf16)


def hidden_kernel(kept, got, rest, out):
    out[...] = rest[...].astype(f32) + (kept[...] + got[...].astype(f32))


def total_kernel(kept, got, out):
    out[...] = kept[...] + got[...].astype(f32)


def shards(
    images,
    hidden_in,
    norm1_gain,
    norm1_bias,
    fc1,
    fc1_bias,
    fc2,
    norm2_gain,
    norm2_bias,
    head,
    log_scale,
    logit_bias,
):
    block, width = images.shape
    quarter = block // 4
    share = width // 4
    units = fc1.shape[1]
    half = block // 2
    at = lax.axis_index(("yl", "c")).astype(jnp.int32).reshape(1)
    fc1 = fc1.T

    low = shape(half, width, dtype=bf16)
    pad = (units // 128 + 1) * 128
    pre, scaled_in, keep, *sends = call(
        forward_kernel,
        [shape(block, pad), shape(block, width), shape(quarter, width)]
        + [shape(quarter, width, dtype=bf16)] * 3,
        [smem] + [hbm] * 6,
        [
            pltpu.VMEM((block, width), f32),
            pltpu.VMEM((width,), f32),
            pltpu.VMEM((width,), f32),
            pltpu.VMEM((units,), f32),
            pltpu.VMEM((units, width), bf16),
            pltpu.VMEM((units, width), bf16),
            pltpu.VMEM((block, pad), f32),
            pltpu.VMEM((block, width), f32),
            pltpu.VMEM((block, width), f32),
            pltpu.SemaphoreType.DMA((8,)),
        ],
        limit=58,
        out_specs=[hbm] * 2 + [vmem] * 4,
    )(at, hidden_in, norm1_gain, norm1_bias, fc1, fc1_bias, fc2)
    first = ring(images, 1)
    sends = [
        lax.ppermute(send, ("yl", "c"), [(i, i ^ bits) for i in range(4)])
        for send, bits in zip(sends, (1, 2, 3))
    ]
    keep = call(hold_kernel, [shape(quarter, width)], [vmem] * 2, cost=1000)(keep, sends[0])[0]
    second = ring(lax.optimization_barrier((first, keep))[0], 1)
    text_unit, state = call(
        embed_kernel,
        [shape(quarter, width, dtype=bf16), shape(quarter, 2 * width + 128)],
        [vmem] * 6,
        limit=10,
        cost=20001000,
    )(
        keep,
        *sends[1:],
        norm2_gain,
        norm2_bias,
        head,
    )

    third = ring(lax.optimization_barrier((second, text_unit))[0], 1)

    near = call(
        functools.partial(stack_kernel, count=2), [shape(half, width, dtype=bf16)], [vmem] * 2, cost=20001000
    )(text_unit, facing(text_unit))[0]
    fourth, across = call(
        parts_kernel,
        [low, shape(3 * half, width, dtype=bf16)],
        [smem] + [vmem] * 3,
    )(at, first, second, third)
    own = call(
        functools.partial(stack_kernel, count=4),
        [shape(4 * half, width, dtype=bf16)],
        [vmem] * 4 + [anywhere] * 2,
        cost=20001000,
    )(near, *(shift(near, "x", hop) for hop in hops[1:]), fourth, across)[0]
    fourth, across = ring(fourth, 1), shift(across, "c", 1)
    own, fourth, across = lax.optimization_barrier((own, fourth, across))
    other = shift(own, "c", 1)

    many = 8 * half
    image_unit, image_rows, inverse_image = call(
        norm_kernel,
        [shape(many, width, dtype=bf16)] * 2 + [shape(many, 1)],
        [smem] + [vmem] * 6,
        limit=12,
        cost=1000,
    )(at, fourth, third, second, first, across, images)
    level = (log_scale.reshape(1, 1), logit_bias.reshape(1, 1))
    near_coef = call(
        functools.partial(near_kernel, chunk=2 * half, quarter=quarter),
        [shape(4 * half, many, dtype=bf16)],
        [smem] + [vmem] * 4,
        limit=12,
        cost=1000,
    )(at, *level, image_unit, own)[0]
    coef, keep, send = call(
        functools.partial(pairs_kernel, chunk=2 * half),
        [
            shape(4 * half, many, dtype=bf16),
            shape(4 * half, width),
            shape(4 * half, width, dtype=bf16),
        ],
        [vmem] * 5,
        limit=16,
    )(*level, image_unit, other, near_coef)
    got = shift(send, "c", 1)

    fourth, across = call(
        functools.partial(images_kernel, first=0),
        [low, shape(3 * half, width, dtype=bf16)],
        [vmem] * 6,
        limit=12,
    )(image_rows, inverse_image, near_coef, coef, own, other)
    near, *far = call(
        split_kernel,
        [shape(half, width)] + [low] * 3,
        [vmem] * 2 + [anywhere],
    )(keep, got, fourth)
    far = [shift(far[index], "x", 4 - hop) for index, hop in enumerate(hops[1:])]
    fourth, across = ring(fourth, -1), shift(across, "c", 1)
    *parts, image_part = call(
        functools.partial(images_kernel, first=4),
        [low] * 3 + [shape(half, width)],
        [vmem] * 6,
        limit=12,
    )(image_rows, inverse_image, near_coef, coef, own, other)

    passed = []

    def onward(index, got, after):
        moving = call(
            functools.partial(pass_kernel, index=index),
            [shape(block, width, dtype=bf16)],
            [vmem] * 3 + [anywhere],
        )(parts[index], across, got, after)[0]
        passed.append(moving)
        return ring(moving, -1)

    moved = onward(0, fourth, near)
    slope = call(
        functools.partial(slope_kernel, units=units), [shape(block, pad)], [vmem, anywhere]
    )(pre, passed[0])[0]
    keep, send = call(
        join_kernel,
        [shape(quarter, width), shape(quarter, width, dtype=bf16)],
        [vmem] * 4 + [anywhere],
        cost=60001000,
    )(near, *far, slope)
    moved = onward(1, moved, keep)
    grad_mixed = call(
        head_kernel, [shape(quarter, width, dtype=bf16)], [vmem] * 5, limit=10, cost=60001000
    )(keep, facing(send), state, head, norm2_gain)[0]
    moved = onward(2, moved, grad_mixed)
    grad_mixed = call(
        functools.partial(stack_kernel, count=2), [low], [vmem] * 2, cost=1000
    )(grad_mixed, shift(grad_mixed, "yl", 1))[0]
    keep, send, rest = call(
        backward_kernel,
        [
            shape(block, 2 * share),
            shape(block, 2 * share, dtype=bf16),
            shape(block, share, dtype=bf16),
        ],
        [smem] + [vmem] * 7,
        [
            pltpu.VMEM((block, width), bf16),
        ],
        limit=16,
        cost=15000000,
    )(at, grad_mixed, shift(grad_mixed, "c", 1), slope, scaled_in, norm1_gain, fc1, fc2)
    keep, send = call(
        halve_kernel,
        [shape(block, share), shape(block, share, dtype=bf16)],
        [smem, vmem, vmem],
    )(at, keep, shift(send, "c", 1))
    hidden_keep = keep
    grad_hidden = call(hidden_kernel, [shape(block, share)], [vmem] * 3)(
        keep, shift(send, "yl", 1), rest
    )[0]

    keep, send = call(
        owner_kernel,
        [shape(block, 2 * share), shape(block, 2 * share, dtype=bf16)],
        [smem] + [vmem] * 2 + [anywhere],
    )(at, image_part, moved, hidden_keep)
    keep, send = call(
        halve_kernel,
        [shape(block, share), shape(block, share, dtype=bf16)],
        [smem, vmem, vmem],
    )(at, keep, shift(send, "c", 1))
    grad_images = call(total_kernel, [shape(block, share)], [vmem] * 2)(
        keep, shift(send, "yl", 1)
    )[0]
    return (grad_images, grad_hidden)


def solution(mesh):
    grid = Mesh(mesh.devices.reshape(8, 4, 2, 2, 2), ("z", "x", "yh", "yl", "c"))
    dp, mp = ("z", "x", "yh"), ("yl", "c")
    placed = (
        P(dp, None),
        P(dp, None),
        P(),
        P(),
        P(None, mp),
        P(mp),
        P(mp, None),
        P(),
        P(),
        P(),
        P(),
        P(),
    )
    return jax.shard_map(
        shards,
        mesh=grid,
        in_specs=placed,
        out_specs=(P(dp, mp), P(dp, mp)),
        check_vma=False,
    )
```

```python
import functools

import jax
import jax.numpy as jnp
from jax import lax
from jax.experimental import pallas as pl
from jax.experimental.pallas import tpu as pltpu
from jax.sharding import Mesh, PartitionSpec as P

eps = 1e-06
hops = (0, 1, 3, 2)
f32 = jnp.float32
bf16 = jnp.bfloat16


def normalize(values, gain, shift):
    mean = jnp.mean(values, axis=-1, keepdims=True)
    centered = values - mean
    inverse = lax.rsqrt(jnp.mean(centered * centered, axis=-1, keepdims=True) + eps)
    scaled = centered * inverse
    return (scaled * gain + shift, scaled, inverse)


def gelu_slope(values):
    factor = 0.7978845608028654
    inner = factor * (values + 0.044715 * values * values * values)
    tangent = jnp.tanh(inner)
    return 0.5 * (1.0 + tangent) + 0.5 * values * (1.0 - tangent * tangent) * factor * (
        1.0 + 3.0 * 0.044715 * values * values
    )


def norm_back(upstream, gain, scaled, inverse):
    grad = upstream * gain
    return inverse * (
        grad
        - jnp.mean(grad, axis=-1, keepdims=True)
        - scaled * jnp.mean(grad * scaled, axis=-1, keepdims=True)
    )


def contract_rows(left, right):
    return lax.dot_general(left, right, (((0,), (0,)), ((), ())), preferred_element_type=f32)


def contract_cols(left, right):
    return lax.dot_general(left, right, (((1,), (1,)), ((), ())), preferred_element_type=f32)


def shift(values, axes, step):
    size = lax.axis_size(axes)
    return lax.ppermute(values, axes, [(i, (i + step) % size) for i in range(size)])


def ring(values, sign):
    size = lax.axis_size("z")
    pairs = []
    for z in range(size):
        pairs.append((2 * z, (z + sign) % size * 2))
        pairs.append((2 * z + 1, (z - sign) % size * 2 + 1))
    return lax.ppermute(values, ("z", "c"), pairs)


def facing(values):
    return lax.ppermute(values, ("yh", "yl"), [(0, 3), (3, 0), (1, 2), (2, 1)])


def columns(values, share):
    even = jnp.concatenate([values[..., :share], values[..., 2 * share : 3 * share]], axis=-1)
    odd = jnp.concatenate([values[..., share : 2 * share], values[..., 3 * share :]], axis=-1)
    return even, odd


vmem = pl.BlockSpec(memory_space=pltpu.VMEM)
smem = pl.BlockSpec(memory_space=pltpu.SMEM)
hbm = pl.BlockSpec(memory_space=pltpu.HBM)
anywhere = pl.BlockSpec(memory_space=pl.ANY)


def call(kernel, outs, in_specs, scratch=(), limit=6, out_specs=None, cost=1000):
    return pl.pallas_call(
        kernel,
        out_shape=outs,
        in_specs=in_specs,
        out_specs=out_specs or [vmem] * len(outs),
        scratch_shapes=scratch,
        cost_estimate=pl.CostEstimate(flops=300*cost, bytes_accessed=cost, transcendentals=0),
        compiler_params=pltpu.CompilerParams(vmem_limit_bytes=limit * 1024 * 1024),
    )


def shape(*dims, dtype=f32):
    return jax.ShapeDtypeStruct(dims, dtype)


def forward_kernel(
    at, hidden, gain, bias, fc1, fc1_bias, fc2, pre, scaled, keep, send_c, send_y, send_b,
    rows, line1, line2, line3, w1, w2, value, norm, part, sems,
):
    loads = [
        pltpu.make_async_copy(source, target, sems.at[index])
        for index, (source, target) in enumerate(
            [
                (hidden, rows),
                (gain, line1),
                (bias, line2),
                (fc1, w1),
                (fc1_bias, line3),
                (fc2, w2),
            ]
        )
    ]
    for load in loads:
        load.start()
    for load in loads[:3]:
        load.wait()
    units = fc1.shape[0]
    normed, norm[...], inverse = normalize(rows[...], line1[...], line2[...])
    normed = normed.astype(bf16)
    save_norm = pltpu.make_async_copy(norm, scaled, sems.at[6])
    save_norm.start()
    loads[3].wait()
    loads[4].wait()
    value[:, units : units + 1] = inverse
    acts = []
    cuts = ((0, 512), (512, units))
    for low, high in cuts:
        linear = contract_cols(normed, w1[low:high, :]) + line3[low:high]
        value[:, low:high] = linear
        acts.append(jax.nn.gelu(linear, approximate=True).astype(bf16))
    save_pre = pltpu.make_async_copy(value, pre, sems.at[7])
    save_pre.start()
    loads[5].wait()
    total = jnp.zeros(part.shape, f32)
    for (low, high), act in zip(cuts, acts):
        total = total + jnp.dot(act, w2[low:high, :], preferred_element_type=f32)
    part[...] = total
    quarter = keep.shape[0]
    side, core = at[0] // 2, at[0] % 2

    def own(core, side):
        return pl.ds(pl.multiple_of((core * 2 + side) * quarter, quarter), quarter)

    keep[...] = rows[own(core, side), :] + part[own(core, side), :]
    send_c[...] = part[own(1 - core, side), :].astype(bf16)
    send_y[...] = part[own(core, 1 - side), :].astype(bf16)
    send_b[...] = part[own(1 - core, 1 - side), :].astype(bf16)
    save_norm.wait()
    save_pre.wait()


def hold_kernel(kept, got, out):
    out[...] = kept[...] + got[...].astype(f32)


def embed_kernel(kept, got_y, got_b, gain, bias, head, unit, state):
    width = unit.shape[1]
    mixed = kept[...] + got_y[...].astype(f32) + got_b[...].astype(f32)
    normed, scaled, inverse = normalize(mixed, gain[...], bias[...])
    state[:, width : 2 * width] = scaled
    embed = jnp.dot(normed.astype(bf16), head[...], preferred_element_type=f32)
    level = lax.rsqrt(jnp.sum(embed * embed, axis=-1, keepdims=True) + eps)
    unit[...] = (embed * level).astype(bf16)
    state[:, :width] = embed * level
    state[:, 2 * width : 2 * width + 1] = level
    state[:, 2 * width + 1 : 2 * width + 2] = inverse


def stack_kernel(*refs, count):
    rows = refs[0].shape[0]
    for index, ref in enumerate(refs[:count]):
        refs[-1][index * rows : (index + 1) * rows, :] = ref[...]


def parts_kernel(at, first, second, third, half, send):
    rows = half.shape[0]
    own = pl.ds(pl.multiple_of(at[0] % 2 * rows, rows), rows)
    other = pl.ds(pl.multiple_of((1 - at[0] % 2) * rows, rows), rows)
    half[...] = third[own, :]
    for index, ref in enumerate((third, second, first)):
        send[index * rows : (index + 1) * rows, :] = ref[other, :]


def norm_kernel(at, fourth, third, second, first, across, images, unit, image_rows, inverse):
    size = fourth.shape[0]
    mine = pl.ds(pl.multiple_of(at[0] % 2 * size, size), size)

    def put(index, values):
        rows = slice(index * size, (index + 1) * size)
        image_rows[rows, :] = values
        wide = values.astype(f32)
        level = lax.rsqrt(jnp.sum(wide * wide, axis=-1, keepdims=True) + eps)
        inverse[rows, :] = level
        unit[rows, :] = (wide * level).astype(bf16)

    put(0, fourth[...])
    for index in range(3):
        put(1 + index, across[index * size : (index + 1) * size, :])
    for index, ref in enumerate((third, second, first, images)):
        put(4 + index, ref[mine, :])


def near_kernel(at, log_scale, offset, unit, own, coef, *, chunk, quarter):
    scale = jnp.exp(log_scale[...])
    size = unit.shape[0] // 8
    diagonal = 7 * size + at[0] // 2 * quarter
    for start in range(0, unit.shape[0], chunk):
        rows = slice(start, start + chunk)
        chance = jax.nn.sigmoid(scale * contract_cols(unit[rows, :], own[...]) + offset[...])
        line = lax.broadcasted_iota(jnp.int32, chance.shape, 0) + (start - diagonal)
        cols = lax.broadcasted_iota(jnp.int32, chance.shape, 1)
        ident = ((line == cols) & (cols < quarter)).astype(f32)
        coef[rows, :] = (scale * (chance - ident)).astype(bf16)


def pairs_kernel(log_scale, offset, unit, other, near, coef, keep, send, *, chunk):
    scale = jnp.exp(log_scale[...])
    for start in range(0, unit.shape[0], chunk):
        rows = slice(start, start + chunk)
        chance = jax.nn.sigmoid(scale * contract_cols(unit[rows, :], other[...]) + offset[...])
        coef[rows, :] = (scale * chance).astype(bf16)
    send[...] = contract_rows(coef[...], unit[...]).astype(bf16)
    keep[...] = contract_rows(near[...], unit[...])


def images_kernel(images, inverse, near, coef, own, other, *parts, first):
    size = images.shape[0] // 8
    rows = slice(first * size, (first + 4) * size)
    grad = jnp.dot(near[rows, :], own[...], preferred_element_type=f32)
    grad = grad + jnp.dot(coef[rows, :], other[...], preferred_element_type=f32)
    level = inverse[rows, :]
    direct = images[rows, :].astype(f32) * level
    inner = jnp.sum(direct * grad, axis=-1, keepdims=True)
    grad = (grad - direct * inner) * level
    start = 0
    for part in parts:
        count = part.shape[0]
        part[...] = grad[start : start + count].astype(part.dtype)
        start += count


def pass_kernel(own, across, got, after, out, *, index):
    size = own.shape[0]
    if got.shape[0] == size:
        out[:size, :] = (own[...].astype(f32) + got[...].astype(f32)).astype(bf16)
        out[size:, :] = across[index * size : (index + 1) * size, :]
    else:
        out[:size, :] = (own[...].astype(f32) + got[:size, :].astype(f32)).astype(bf16)
        part = across[index * size : (index + 1) * size, :].astype(f32)
        out[size:, :] = (part + got[size:, :].astype(f32)).astype(bf16)


def owner_kernel(at, own, got, after, keep, send):
    size = own.shape[0]
    core = at[0] % 2 == 0
    share = own.shape[1] // 4
    mine = own[...] + got[:size, :].astype(f32)
    theirs = got[size:, :].astype(f32)
    low, high = jnp.where(core, mine, theirs), jnp.where(core, theirs, mine)
    for index, rows in enumerate((low, high)):
        place = slice(index * size, (index + 1) * size)
        even, odd = columns(rows, share)
        keep[place, :] = jnp.where(core, even, odd)
        send[place, :] = jnp.where(core, odd, even).astype(bf16)


def split_kernel(kept, got, after, near, *far):
    rows = near.shape[0]
    near[...] = kept[:rows, :] + got[:rows, :].astype(f32)
    for index, ref in enumerate(far):
        part = slice((index + 1) * rows, (index + 2) * rows)
        ref[...] = (kept[part, :] + got[part, :].astype(f32)).astype(bf16)


def join_kernel(near, first, second, third, after, keep, send):
    total = near[...] + first[...].astype(f32) + second[...].astype(f32) + third[...].astype(f32)
    half = keep.shape[0]
    keep[...] = total[:half]
    send[...] = total[half:].astype(bf16)


def head_kernel(kept, got, state, head, gain, grad):
    width = grad.shape[1]
    upstream = kept[...] + got[...].astype(f32)
    text_dir = state[:, :width]
    inner = jnp.sum(text_dir * upstream, axis=-1, keepdims=True)
    grad_embed = (upstream - text_dir * inner) * state[:, 2 * width : 2 * width + 1]
    grad_normed = contract_cols(grad_embed.astype(bf16), head[...])
    scaled, inverse = state[:, width : 2 * width], state[:, 2 * width + 1 : 2 * width + 2]
    grad[...] = norm_back(grad_normed, gain[...], scaled, inverse).astype(bf16)


def slope_kernel(pre, after, out, *, units):
    out[:, :units] = gelu_slope(pre[:, :units])
    out[:, units : units + 1] = pre[:, units : units + 1]


def backward_kernel(
    at, own_rows, other_rows, slope, scaled, gain, fc1, fc2, keep, send, rest, grad
):
    quarter = grad.shape[0] // 4
    row_side, row_core = at[0] // 2, at[0] % 2
    for index, ref in enumerate((own_rows, other_rows)):
        start = row_core if index == 0 else 1 - row_core
        for step in range(2):
            place = start * 2 + (row_side if step == 0 else 1 - row_side)
            rows = pl.ds(pl.multiple_of(place * quarter, quarter), quarter)
            grad[rows, :] = ref[step * quarter : (step + 1) * quarter, :]
    share = grad.shape[1] // 4
    units = fc1.shape[0]
    core = at[0] % 2 == 0
    own = jnp.where(core, *columns(grad[...], share))
    rest[...] = jnp.where(at[0] // 2 == 0, own[:, :share], own[:, share:])
    grad_act = contract_cols(grad[...], fc2[...])
    grad_pre = (grad_act * slope[:, :units]).astype(bf16)
    part = jnp.dot(grad_pre, fc1[...], preferred_element_type=f32)
    part = norm_back(part, gain[...], scaled[...], slope[:, units : units + 1])
    even, odd = columns(part, share)
    keep[...] = jnp.where(core, even, odd)
    send[...] = jnp.where(core, odd, even).astype(bf16)


def halve_kernel(at, kept, got, keep, send):
    total = kept[...] + got[...].astype(f32)
    half = keep.shape[1]
    low, high = total[:, :half], total[:, half:]
    side = at[0] // 2 == 0
    keep[...] = jnp.where(side, low, high)
    send[...] = jnp.where(side, high, low).astype(bf16)


def hidden_kernel(kept, got, rest, out):
    out[...] = rest[...].astype(f32) + (kept[...] + got[...].astype(f32))


def total_kernel(kept, got, out):
    out[...] = kept[...] + got[...].astype(f32)


def shards(
    images,
    hidden_in,
    norm1_gain,
    norm1_bias,
    fc1,
    fc1_bias,
    fc2,
    norm2_gain,
    norm2_bias,
    head,
    log_scale,
    logit_bias,
):
    block, width = images.shape
    quarter = block // 4
    share = width // 4
    units = fc1.shape[1]
    half = block // 2
    at = lax.axis_index(("yl", "c")).astype(jnp.int32).reshape(1)
    fc1 = fc1.T

    low = shape(half, width, dtype=bf16)
    pad = (units // 128 + 1) * 128
    pre, scaled_in, keep, *sends = call(
        forward_kernel,
        [shape(block, pad), shape(block, width), shape(quarter, width)]
        + [shape(quarter, width, dtype=bf16)] * 3,
        [smem] + [hbm] * 6,
        [
            pltpu.VMEM((block, width), f32),
            pltpu.VMEM((width,), f32),
            pltpu.VMEM((width,), f32),
            pltpu.VMEM((units,), f32),
            pltpu.VMEM((units, width), bf16),
            pltpu.VMEM((units, width), bf16),
            pltpu.VMEM((block, pad), f32),
            pltpu.VMEM((block, width), f32),
            pltpu.VMEM((block, width), f32),
            pltpu.SemaphoreType.DMA((8,)),
        ],
        limit=58,
        out_specs=[hbm] * 2 + [vmem] * 4,
    )(at, hidden_in, norm1_gain, norm1_bias, fc1, fc1_bias, fc2)
    first = ring(images, 1)
    sends = [
        lax.ppermute(send, ("yl", "c"), [(i, i ^ bits) for i in range(4)])
        for send, bits in zip(sends, (1, 2, 3))
    ]
    keep = call(hold_kernel, [shape(quarter, width)], [vmem] * 2, cost=1000)(keep, sends[0])[0]
    second = ring(lax.optimization_barrier((first, keep))[0], 1)
    text_unit, state = call(
        embed_kernel,
        [shape(quarter, width, dtype=bf16), shape(quarter, 2 * width + 128)],
        [vmem] * 6,
        limit=10,
        cost=20001000,
    )(
        keep,
        *sends[1:],
        norm2_gain,
        norm2_bias,
        head,
    )

    third = ring(lax.optimization_barrier((second, text_unit))[0], 1)

    near = call(
        functools.partial(stack_kernel, count=2), [shape(half, width, dtype=bf16)], [vmem] * 2, cost=20001000
    )(text_unit, facing(text_unit))[0]
    fourth, across = call(
        parts_kernel,
        [low, shape(3 * half, width, dtype=bf16)],
        [smem] + [vmem] * 3,
    )(at, first, second, third)
    own = call(
        functools.partial(stack_kernel, count=4),
        [shape(4 * half, width, dtype=bf16)],
        [vmem] * 4 + [anywhere] * 2,
        cost=20001000,
    )(near, *(shift(near, "x", hop) for hop in hops[1:]), fourth, across)[0]
    fourth, across = ring(fourth, 1), shift(across, "c", 1)
    own, fourth, across = lax.optimization_barrier((own, fourth, across))
    other = shift(own, "c", 1)

    many = 8 * half
    image_unit, image_rows, inverse_image = call(
        norm_kernel,
        [shape(many, width, dtype=bf16)] * 2 + [shape(many, 1)],
        [smem] + [vmem] * 6,
        limit=12,
        cost=1000,
    )(at, fourth, third, second, first, across, images)
    level = (log_scale.reshape(1, 1), logit_bias.reshape(1, 1))
    near_coef = call(
        functools.partial(near_kernel, chunk=many // 2, quarter=quarter),
        [shape(many, 4 * half, dtype=bf16)],
        [smem] + [vmem] * 4,
        limit=12,
        cost=1000,
    )(at, *level, image_unit, own)[0]
    coef, keep, send = call(
        functools.partial(pairs_kernel, chunk=many // 2),
        [
            shape(many, 4 * half, dtype=bf16),
            shape(4 * half, width),
            shape(4 * half, width, dtype=bf16),
        ],
        [vmem] * 5,
        limit=16,
    )(*level, image_unit, other, near_coef)
    got = shift(send, "c", 1)

    fourth, across = call(
        functools.partial(images_kernel, first=0),
        [low, shape(3 * half, width, dtype=bf16)],
        [vmem] * 6,
        limit=12,
    )(image_rows, inverse_image, near_coef, coef, own, other)
    near, *far = call(
        split_kernel,
        [shape(half, width)] + [low] * 3,
        [vmem] * 2 + [anywhere],
    )(keep, got, fourth)
    far = [shift(far[index], "x", 4 - hop) for index, hop in enumerate(hops[1:])]
    fourth, across = ring(fourth, -1), shift(across, "c", 1)
    *parts, image_part = call(
        functools.partial(images_kernel, first=4),
        [low] * 3 + [shape(half, width)],
        [vmem] * 6,
        limit=12,
    )(image_rows, inverse_image, near_coef, coef, own, other)

    passed = []

    def onward(index, got, after):
        moving = call(
            functools.partial(pass_kernel, index=index),
            [shape(block, width, dtype=bf16)],
            [vmem] * 3 + [anywhere],
        )(parts[index], across, got, after)[0]
        passed.append(moving)
        return ring(moving, -1)

    moved = onward(0, fourth, near)
    slope = call(
        functools.partial(slope_kernel, units=units), [shape(block, pad)], [vmem, anywhere]
    )(pre, passed[0])[0]
    moved = onward(1, moved, slope)
    keep, send = call(
        join_kernel,
        [shape(quarter, width), shape(quarter, width, dtype=bf16)],
        [vmem] * 4 + [anywhere],
        cost=60001000,
    )(near, *far, slope)
    grad_mixed = call(
        head_kernel, [shape(quarter, width, dtype=bf16)], [vmem] * 5, limit=10, cost=20001000
    )(keep, facing(send), state, head, norm2_gain)[0]
    moved = onward(2, moved, grad_mixed)
    grad_mixed = call(
        functools.partial(stack_kernel, count=2), [low], [vmem] * 2 + [anywhere], cost=1000
    )(grad_mixed, shift(grad_mixed, "yl", 1), passed[2])[0]
    keep, send, rest = call(
        backward_kernel,
        [
            shape(block, 2 * share),
            shape(block, 2 * share, dtype=bf16),
            shape(block, share, dtype=bf16),
        ],
        [smem] + [vmem] * 7,
        [
            pltpu.VMEM((block, width), bf16),
        ],
        limit=16,
        cost=1000,
    )(at, grad_mixed, shift(grad_mixed, "c", 1), slope, scaled_in, norm1_gain, fc1, fc2)
    keep, send = call(
        halve_kernel,
        [shape(block, share), shape(block, share, dtype=bf16)],
        [smem, vmem, vmem],
    )(at, keep, shift(send, "c", 1))
    hidden_keep = keep
    grad_hidden = call(hidden_kernel, [shape(block, share)], [vmem] * 3)(
        keep, shift(send, "yl", 1), rest
    )[0]

    keep, send = call(
        owner_kernel,
        [shape(block, 2 * share), shape(block, 2 * share, dtype=bf16)],
        [smem] + [vmem] * 2 + [anywhere],
    )(at, image_part, moved, hidden_keep)
    keep, send = call(
        halve_kernel,
        [shape(block, share), shape(block, share, dtype=bf16)],
        [smem, vmem, vmem],
    )(at, keep, shift(send, "c", 1))
    grad_images = call(total_kernel, [shape(block, share)], [vmem] * 2)(
        keep, shift(send, "yl", 1)
    )[0]
    return (grad_images, grad_hidden)


def solution(mesh):
    grid = Mesh(mesh.devices.reshape(8, 4, 2, 2, 2), ("z", "x", "yh", "yl", "c"))
    dp, mp = ("z", "x", "yh"), ("yl", "c")
    placed = (
        P(dp, None),
        P(dp, None),
        P(),
        P(),
        P(None, mp),
        P(mp),
        P(mp, None),
        P(),
        P(),
        P(),
        P(),
        P(),
    )
    return jax.shard_map(
        shards,
        mesh=grid,
        in_specs=placed,
        out_specs=(P(dp, mp), P(dp, mp)),
        check_vma=False,
    )
```

```python
import functools

import jax
import jax.numpy as jnp
from jax import lax
from jax.experimental import pallas as pl
from jax.experimental.pallas import tpu as pltpu
from jax.sharding import Mesh, PartitionSpec as P

eps = 1e-06
hops = (0, 1, 3, 2)
f32 = jnp.float32
bf16 = jnp.bfloat16


def normalize(values, gain, shift):
    mean = jnp.mean(values, axis=-1, keepdims=True)
    centered = values - mean
    inverse = lax.rsqrt(jnp.mean(centered * centered, axis=-1, keepdims=True) + eps)
    scaled = centered * inverse
    return (scaled * gain + shift, scaled, inverse)


def gelu_slope(values):
    factor = 0.7978845608028654
    inner = factor * (values + 0.044715 * values * values * values)
    tangent = jnp.tanh(inner)
    return 0.5 * (1.0 + tangent) + 0.5 * values * (1.0 - tangent * tangent) * factor * (
        1.0 + 3.0 * 0.044715 * values * values
    )


def norm_back(upstream, gain, scaled, inverse):
    grad = upstream * gain
    return inverse * (
        grad
        - jnp.mean(grad, axis=-1, keepdims=True)
        - scaled * jnp.mean(grad * scaled, axis=-1, keepdims=True)
    )


def contract_rows(left, right):
    return lax.dot_general(left, right, (((0,), (0,)), ((), ())), preferred_element_type=f32)


def contract_cols(left, right):
    return lax.dot_general(left, right, (((1,), (1,)), ((), ())), preferred_element_type=f32)


def shift(values, axes, step):
    size = lax.axis_size(axes)
    return lax.ppermute(values, axes, [(i, (i + step) % size) for i in range(size)])


def ring(values, sign):
    size = lax.axis_size("z")
    pairs = []
    for z in range(size):
        pairs.append((2 * z, (z + sign) % size * 2))
        pairs.append((2 * z + 1, (z - sign) % size * 2 + 1))
    return lax.ppermute(values, ("z", "c"), pairs)


def facing(values):
    return lax.ppermute(values, ("yh", "yl"), [(0, 3), (3, 0), (1, 2), (2, 1)])


def columns(values, share):
    even = jnp.concatenate([values[..., :share], values[..., 2 * share : 3 * share]], axis=-1)
    odd = jnp.concatenate([values[..., share : 2 * share], values[..., 3 * share :]], axis=-1)
    return even, odd


vmem = pl.BlockSpec(memory_space=pltpu.VMEM)
smem = pl.BlockSpec(memory_space=pltpu.SMEM)
hbm = pl.BlockSpec(memory_space=pltpu.HBM)
anywhere = pl.BlockSpec(memory_space=pl.ANY)


def call(kernel, outs, in_specs, scratch=(), limit=6, out_specs=None, cost=1000):
    return pl.pallas_call(
        kernel,
        out_shape=outs,
        in_specs=in_specs,
        out_specs=out_specs or [vmem] * len(outs),
        scratch_shapes=scratch,
        cost_estimate=pl.CostEstimate(flops=300*cost, bytes_accessed=cost, transcendentals=0),
        compiler_params=pltpu.CompilerParams(vmem_limit_bytes=limit * 1024 * 1024),
    )


def shape(*dims, dtype=f32):
    return jax.ShapeDtypeStruct(dims, dtype)


def forward_kernel(
    at, hidden, gain, bias, fc1, fc1_bias, fc2, pre, scaled, keep, send_c, send_y, send_b,
    rows, line1, line2, line3, w1, w2, value, norm, part, sems,
):
    loads = [
        pltpu.make_async_copy(source, target, sems.at[index])
        for index, (source, target) in enumerate(
            [
                (hidden, rows),
                (gain, line1),
                (bias, line2),
                (fc1, w1),
                (fc1_bias, line3),
                (fc2, w2),
            ]
        )
    ]
    for load in loads:
        load.start()
    for load in loads[:3]:
        load.wait()
    units = fc1.shape[0]
    normed, norm[...], inverse = normalize(rows[...], line1[...], line2[...])
    normed = normed.astype(bf16)
    save_norm = pltpu.make_async_copy(norm, scaled, sems.at[6])
    save_norm.start()
    loads[3].wait()
    loads[4].wait()
    value[:, units : units + 1] = inverse
    acts = []
    cuts = ((0, 512), (512, units))
    for low, high in cuts:
        linear = contract_cols(normed, w1[low:high, :]) + line3[low:high]
        value[:, low:high] = linear
        acts.append(jax.nn.gelu(linear, approximate=True).astype(bf16))
    save_pre = pltpu.make_async_copy(value, pre, sems.at[7])
    save_pre.start()
    loads[5].wait()
    total = jnp.zeros(part.shape, f32)
    for (low, high), act in zip(cuts, acts):
        total = total + jnp.dot(act, w2[low:high, :], preferred_element_type=f32)
    part[...] = total
    quarter = keep.shape[0]
    side, core = at[0] // 2, at[0] % 2

    def own(core, side):
        return pl.ds(pl.multiple_of((core * 2 + side) * quarter, quarter), quarter)

    keep[...] = rows[own(core, side), :] + part[own(core, side), :]
    send_c[...] = part[own(1 - core, side), :].astype(bf16)
    send_y[...] = part[own(core, 1 - side), :].astype(bf16)
    send_b[...] = part[own(1 - core, 1 - side), :].astype(bf16)
    save_norm.wait()
    save_pre.wait()


def hold_kernel(kept, got, out):
    out[...] = kept[...] + got[...].astype(f32)


def embed_kernel(kept, got_y, got_b, gain, bias, head, unit, state):
    width = unit.shape[1]
    mixed = kept[...] + got_y[...].astype(f32) + got_b[...].astype(f32)
    normed, scaled, inverse = normalize(mixed, gain[...], bias[...])
    state[:, width : 2 * width] = scaled
    embed = jnp.dot(normed.astype(bf16), head[...], preferred_element_type=f32)
    level = lax.rsqrt(jnp.sum(embed * embed, axis=-1, keepdims=True) + eps)
    unit[...] = (embed * level).astype(bf16)
    state[:, :width] = embed * level
    state[:, 2 * width : 2 * width + 1] = level
    state[:, 2 * width + 1 : 2 * width + 2] = inverse


def stack_kernel(*refs, count):
    rows = refs[0].shape[0]
    for index, ref in enumerate(refs[:count]):
        refs[-1][index * rows : (index + 1) * rows, :] = ref[...]


def parts_kernel(at, first, second, third, after, half, send):
    rows = half.shape[0]
    own = pl.ds(pl.multiple_of(at[0] % 2 * rows, rows), rows)
    other = pl.ds(pl.multiple_of((1 - at[0] % 2) * rows, rows), rows)
    half[...] = third[own, :]
    for index, ref in enumerate((third, second, first)):
        send[index * rows : (index + 1) * rows, :] = ref[other, :]


def level_kernel(log_scale, offset, after, level):
    level[0:1, :] = jnp.exp(jnp.full((1, level.shape[1]), log_scale[0], f32))
    level[1:2, :] = jnp.full((1, level.shape[1]), offset[0], f32)


def norm_kernel(at, fourth, third, second, first, across, images, unit, image_rows, inverse):
    size = fourth.shape[0]
    mine = pl.ds(pl.multiple_of(at[0] % 2 * size, size), size)

    def put(index, values):
        rows = slice(index * size, (index + 1) * size)
        image_rows[rows, :] = values
        wide = values.astype(f32)
        size_of = lax.rsqrt(jnp.sum(wide * wide, axis=-1, keepdims=True) + eps)
        inverse[rows, :] = size_of
        unit[rows, :] = (wide * size_of).astype(bf16)

    put(0, fourth[...])
    for index in range(3):
        put(1 + index, across[index * size : (index + 1) * size, :])
    for index, ref in enumerate((third, second, first, images)):
        put(4 + index, ref[mine, :])


def near_kernel(at, level, unit, own, coef, *, chunk, quarter):
    scale, offset = level[0:1, 0:1], level[1:2, 0:1]
    size = unit.shape[0] // 8
    diagonal = 7 * size + at[0] // 2 * quarter
    for start in range(0, unit.shape[0], chunk):
        rows = slice(start, start + chunk)
        chance = jax.nn.sigmoid(scale * contract_cols(unit[rows, :], own[...]) + offset)
        line = lax.broadcasted_iota(jnp.int32, chance.shape, 0) + (start - diagonal)
        cols = lax.broadcasted_iota(jnp.int32, chance.shape, 1)
        ident = ((line == cols) & (cols < quarter)).astype(f32)
        coef[rows, :] = (scale * (chance - ident)).astype(bf16)


def pairs_kernel(level, unit, other, near, coef, keep, send, *, chunk):
    scale, offset = level[0:1, 0:1], level[1:2, 0:1]
    for start in range(0, unit.shape[0], chunk):
        rows = slice(start, start + chunk)
        chance = jax.nn.sigmoid(scale * contract_cols(unit[rows, :], other[...]) + offset)
        coef[rows, :] = (scale * chance).astype(bf16)
    send[...] = contract_rows(coef[...], unit[...]).astype(bf16)
    keep[...] = contract_rows(near[...], unit[...])


def images_kernel(images, inverse, near, coef, own, other, *parts, first):
    size = images.shape[0] // 8
    rows = slice(first * size, (first + 4) * size)
    grad = jnp.dot(near[rows, :], own[...], preferred_element_type=f32)
    grad = grad + jnp.dot(coef[rows, :], other[...], preferred_element_type=f32)
    level = inverse[rows, :]
    direct = images[rows, :].astype(f32) * level
    inner = jnp.sum(direct * grad, axis=-1, keepdims=True)
    grad = (grad - direct * inner) * level
    start = 0
    for part in parts:
        count = part.shape[0]
        part[...] = grad[start : start + count].astype(part.dtype)
        start += count


def pass_kernel(own, across, got, after, out, *, index):
    size = own.shape[0]
    if got.shape[0] == size:
        out[:size, :] = (own[...].astype(f32) + got[...].astype(f32)).astype(bf16)
        out[size:, :] = across[index * size : (index + 1) * size, :]
    else:
        out[:size, :] = (own[...].astype(f32) + got[:size, :].astype(f32)).astype(bf16)
        part = across[index * size : (index + 1) * size, :].astype(f32)
        out[size:, :] = (part + got[size:, :].astype(f32)).astype(bf16)


def owner_kernel(at, own, got, after, keep, send):
    size = own.shape[0]
    core = at[0] % 2 == 0
    share = own.shape[1] // 4
    mine = own[...] + got[:size, :].astype(f32)
    theirs = got[size:, :].astype(f32)
    low, high = jnp.where(core, mine, theirs), jnp.where(core, theirs, mine)
    for index, rows in enumerate((low, high)):
        place = slice(index * size, (index + 1) * size)
        even, odd = columns(rows, share)
        keep[place, :] = jnp.where(core, even, odd)
        send[place, :] = jnp.where(core, odd, even).astype(bf16)


def split_kernel(kept, got, after, near, *far):
    rows = near.shape[0]
    near[...] = kept[:rows, :] + got[:rows, :].astype(f32)
    for index, ref in enumerate(far):
        part = slice((index + 1) * rows, (index + 2) * rows)
        ref[...] = (kept[part, :] + got[part, :].astype(f32)).astype(bf16)


def join_kernel(near, first, second, third, after, keep, send):
    total = near[...] + first[...].astype(f32) + second[...].astype(f32) + third[...].astype(f32)
    half = keep.shape[0]
    keep[...] = total[:half]
    send[...] = total[half:].astype(bf16)


def head_kernel(kept, got, state, head, gain, grad):
    width = grad.shape[1]
    upstream = kept[...] + got[...].astype(f32)
    text_dir = state[:, :width]
    inner = jnp.sum(text_dir * upstream, axis=-1, keepdims=True)
    grad_embed = (upstream - text_dir * inner) * state[:, 2 * width : 2 * width + 1]
    grad_normed = contract_cols(grad_embed.astype(bf16), head[...])
    scaled, inverse = state[:, width : 2 * width], state[:, 2 * width + 1 : 2 * width + 2]
    grad[...] = norm_back(grad_normed, gain[...], scaled, inverse).astype(bf16)


def slope_kernel(pre, after, out, *, units):
    out[:, :units] = gelu_slope(pre[:, :units])
    out[:, units : units + 1] = pre[:, units : units + 1]


def backward_kernel(
    at, own_rows, other_rows, slope, scaled, gain, fc1, fc2, keep, send, rest, grad
):
    quarter = grad.shape[0] // 4
    row_side, row_core = at[0] // 2, at[0] % 2
    for index, ref in enumerate((own_rows, other_rows)):
        start = row_core if index == 0 else 1 - row_core
        for step in range(2):
            place = start * 2 + (row_side if step == 0 else 1 - row_side)
            rows = pl.ds(pl.multiple_of(place * quarter, quarter), quarter)
            grad[rows, :] = ref[step * quarter : (step + 1) * quarter, :]
    share = grad.shape[1] // 4
    units = fc1.shape[0]
    core = at[0] % 2 == 0
    own = jnp.where(core, *columns(grad[...], share))
    rest[...] = jnp.where(at[0] // 2 == 0, own[:, :share], own[:, share:])
    grad_act = contract_cols(grad[...], fc2[...])
    grad_pre = (grad_act * slope[:, :units]).astype(bf16)
    part = jnp.dot(grad_pre, fc1[...], preferred_element_type=f32)
    part = norm_back(part, gain[...], scaled[...], slope[:, units : units + 1])
    even, odd = columns(part, share)
    keep[...] = jnp.where(core, even, odd)
    send[...] = jnp.where(core, odd, even).astype(bf16)


def halve_kernel(at, kept, got, keep, send):
    total = kept[...] + got[...].astype(f32)
    half = keep.shape[1]
    low, high = total[:, :half], total[:, half:]
    side = at[0] // 2 == 0
    keep[...] = jnp.where(side, low, high)
    send[...] = jnp.where(side, high, low).astype(bf16)


def hidden_kernel(kept, got, rest, out):
    out[...] = rest[...].astype(f32) + (kept[...] + got[...].astype(f32))


def total_kernel(kept, got, out):
    out[...] = kept[...] + got[...].astype(f32)


def shards(
    images,
    hidden_in,
    norm1_gain,
    norm1_bias,
    fc1,
    fc1_bias,
    fc2,
    norm2_gain,
    norm2_bias,
    head,
    log_scale,
    logit_bias,
):
    block, width = images.shape
    quarter = block // 4
    share = width // 4
    units = fc1.shape[1]
    half = block // 2
    at = lax.axis_index(("yl", "c")).astype(jnp.int32).reshape(1)
    fc1 = fc1.T

    low = shape(half, width, dtype=bf16)
    pad = (units // 128 + 1) * 128
    pre, scaled_in, keep, *sends = call(
        forward_kernel,
        [shape(block, pad), shape(block, width), shape(quarter, width)]
        + [shape(quarter, width, dtype=bf16)] * 3,
        [smem] + [hbm] * 6,
        [
            pltpu.VMEM((block, width), f32),
            pltpu.VMEM((width,), f32),
            pltpu.VMEM((width,), f32),
            pltpu.VMEM((units,), f32),
            pltpu.VMEM((units, width), bf16),
            pltpu.VMEM((units, width), bf16),
            pltpu.VMEM((block, pad), f32),
            pltpu.VMEM((block, width), f32),
            pltpu.VMEM((block, width), f32),
            pltpu.SemaphoreType.DMA((8,)),
        ],
        limit=58,
        out_specs=[hbm] * 2 + [vmem] * 4,
    )(at, hidden_in, norm1_gain, norm1_bias, fc1, fc1_bias, fc2)
    first = ring(images, 1)
    sends = [
        lax.ppermute(send, ("yl", "c"), [(i, i ^ bits) for i in range(4)])
        for send, bits in zip(sends, (1, 2, 3))
    ]
    keep = call(hold_kernel, [shape(quarter, width)], [vmem] * 2, cost=1000)(keep, sends[0])[0]
    second = ring(lax.optimization_barrier((first, keep))[0], 1)
    text_unit, state = call(
        embed_kernel,
        [shape(quarter, width, dtype=bf16), shape(quarter, 2 * width + 128)],
        [vmem] * 6,
        limit=10,
        cost=20001000,
    )(
        keep,
        *sends[1:],
        norm2_gain,
        norm2_bias,
        head,
    )

    third = ring(lax.optimization_barrier((second, text_unit))[0], 1)

    near = call(
        functools.partial(stack_kernel, count=2), [shape(half, width, dtype=bf16)], [vmem] * 2, cost=20001000
    )(text_unit, facing(text_unit))[0]
    level = call(level_kernel, [shape(2, 128)], [smem] * 2 + [anywhere])(
        log_scale, logit_bias, near
    )[0]
    fourth, across = call(
        parts_kernel,
        [low, shape(3 * half, width, dtype=bf16)],
        [smem] + [vmem] * 3 + [anywhere],
    )(at, first, second, third, level)
    own = call(
        functools.partial(stack_kernel, count=4),
        [shape(4 * half, width, dtype=bf16)],
        [vmem] * 4 + [anywhere] * 2,
        cost=20001000,
    )(near, *(shift(near, "x", hop) for hop in hops[1:]), fourth, across)[0]
    fourth, across = ring(fourth, 1), shift(across, "c", 1)
    own, fourth, across = lax.optimization_barrier((own, fourth, across))
    other = shift(own, "c", 1)

    many = 8 * half
    image_unit, image_rows, inverse_image = call(
        norm_kernel,
        [shape(many, width, dtype=bf16)] * 2 + [shape(many, 1)],
        [smem] + [vmem] * 6,
        limit=12,
        cost=1000,
    )(at, fourth, third, second, first, across, images)
    near_coef = call(
        functools.partial(near_kernel, chunk=many // 2, quarter=quarter),
        [shape(many, 4 * half, dtype=bf16)],
        [smem] + [vmem] * 3,
        limit=12,
        cost=1000,
    )(at, level, image_unit, own)[0]
    coef, keep, send = call(
        functools.partial(pairs_kernel, chunk=many // 2),
        [
            shape(many, 4 * half, dtype=bf16),
            shape(4 * half, width),
            shape(4 * half, width, dtype=bf16),
        ],
        [vmem] * 4,
        limit=16,
    )(level, image_unit, other, near_coef)
    got = shift(send, "c", 1)

    fourth, across = call(
        functools.partial(images_kernel, first=0),
        [low, shape(3 * half, width, dtype=bf16)],
        [vmem] * 6,
        limit=12,
    )(image_rows, inverse_image, near_coef, coef, own, other)
    near, *far = call(
        split_kernel,
        [shape(half, width)] + [low] * 3,
        [vmem] * 2 + [anywhere],
    )(keep, got, fourth)
    far = [shift(far[index], "x", 4 - hop) for index, hop in enumerate(hops[1:])]
    fourth, across = ring(fourth, -1), shift(across, "c", 1)
    *parts, image_part = call(
        functools.partial(images_kernel, first=4),
        [low] * 3 + [shape(half, width)],
        [vmem] * 6,
        limit=12,
    )(image_rows, inverse_image, near_coef, coef, own, other)

    passed = []

    def onward(index, got, after):
        moving = call(
            functools.partial(pass_kernel, index=index),
            [shape(block, width, dtype=bf16)],
            [vmem] * 3 + [anywhere],
        )(parts[index], across, got, after)[0]
        passed.append(moving)
        return ring(moving, -1)

    moved = onward(0, fourth, near)
    slope = call(
        functools.partial(slope_kernel, units=units), [shape(block, pad)], [vmem, anywhere]
    )(pre, passed[0])[0]
    moved = onward(1, moved, slope)
    keep, send = call(
        join_kernel,
        [shape(quarter, width), shape(quarter, width, dtype=bf16)],
        [vmem] * 4 + [anywhere],
        cost=60001000,
    )(near, *far, slope)
    grad_mixed = call(
        head_kernel, [shape(quarter, width, dtype=bf16)], [vmem] * 5, limit=10, cost=20001000
    )(keep, facing(send), state, head, norm2_gain)[0]
    moved = onward(2, moved, grad_mixed)
    grad_mixed = call(
        functools.partial(stack_kernel, count=2), [low], [vmem] * 2 + [anywhere], cost=1000
    )(grad_mixed, shift(grad_mixed, "yl", 1), passed[2])[0]
    keep, send, rest = call(
        backward_kernel,
        [
            shape(block, 2 * share),
            shape(block, 2 * share, dtype=bf16),
            shape(block, share, dtype=bf16),
        ],
        [smem] + [vmem] * 7,
        [
            pltpu.VMEM((block, width), bf16),
        ],
        limit=16,
        cost=1000,
    )(at, grad_mixed, shift(grad_mixed, "c", 1), slope, scaled_in, norm1_gain, fc1, fc2)
    keep, send = call(
        halve_kernel,
        [shape(block, share), shape(block, share, dtype=bf16)],
        [smem, vmem, vmem],
    )(at, keep, shift(send, "c", 1))
    hidden_keep = keep
    grad_hidden = call(hidden_kernel, [shape(block, share)], [vmem] * 3)(
        keep, shift(send, "yl", 1), rest
    )[0]

    keep, send = call(
        owner_kernel,
        [shape(block, 2 * share), shape(block, 2 * share, dtype=bf16)],
        [smem] + [vmem] * 2 + [anywhere],
    )(at, image_part, moved, hidden_keep)
    keep, send = call(
        halve_kernel,
        [shape(block, share), shape(block, share, dtype=bf16)],
        [smem, vmem, vmem],
    )(at, keep, shift(send, "c", 1))
    grad_images = call(total_kernel, [shape(block, share)], [vmem] * 2)(
        keep, shift(send, "yl", 1)
    )[0]
    return (grad_images, grad_hidden)


def solution(mesh):
    grid = Mesh(mesh.devices.reshape(8, 4, 2, 2, 2), ("z", "x", "yh", "yl", "c"))
    dp, mp = ("z", "x", "yh"), ("yl", "c")
    placed = (
        P(dp, None),
        P(dp, None),
        P(),
        P(),
        P(None, mp),
        P(mp),
        P(mp, None),
        P(),
        P(),
        P(),
        P(),
        P(),
    )
    return jax.shard_map(
        shards,
        mesh=grid,
        in_specs=placed,
        out_specs=(P(dp, mp), P(dp, mp)),
        check_vma=False,
    )
```

```python
import functools

import jax
import jax.numpy as jnp
from jax import lax
from jax.experimental import pallas as pl
from jax.experimental.pallas import tpu as pltpu
from jax.sharding import Mesh, PartitionSpec as P

eps = 1e-06
hops = (0, 2, 3, 1)
f32 = jnp.float32
bf16 = jnp.bfloat16


def normalize(values, gain, shift):
    mean = jnp.mean(values, axis=-1, keepdims=True)
    centered = values - mean
    inverse = lax.rsqrt(jnp.mean(centered * centered, axis=-1, keepdims=True) + eps)
    scaled = centered * inverse
    return (scaled * gain + shift, scaled, inverse)


def gelu_slope(values):
    factor = 0.7978845608028654
    inner = factor * (values + 0.044715 * values * values * values)
    tangent = jnp.tanh(inner)
    return 0.5 * (1.0 + tangent) + 0.5 * values * (1.0 - tangent * tangent) * factor * (
        1.0 + 3.0 * 0.044715 * values * values
    )


def norm_back(upstream, gain, scaled, inverse):
    grad = upstream * gain
    return inverse * (
        grad
        - jnp.mean(grad, axis=-1, keepdims=True)
        - scaled * jnp.mean(grad * scaled, axis=-1, keepdims=True)
    )


def contract_rows(left, right):
    return lax.dot_general(left, right, (((0,), (0,)), ((), ())), preferred_element_type=f32)


def contract_cols(left, right):
    return lax.dot_general(left, right, (((1,), (1,)), ((), ())), preferred_element_type=f32)


def shift(values, axes, step):
    size = lax.axis_size(axes)
    return lax.ppermute(values, axes, [(i, (i + step) % size) for i in range(size)])


def ring(values, sign):
    size = lax.axis_size("z")
    pairs = []
    for z in range(size):
        pairs.append((2 * z, (z + sign) % size * 2))
        pairs.append((2 * z + 1, (z - sign) % size * 2 + 1))
    return lax.ppermute(values, ("z", "c"), pairs)


def facing(values):
    return lax.ppermute(values, ("yh", "yl"), [(0, 3), (3, 0), (1, 2), (2, 1)])


def columns(values, share):
    even = jnp.concatenate([values[..., :share], values[..., 2 * share : 3 * share]], axis=-1)
    odd = jnp.concatenate([values[..., share : 2 * share], values[..., 3 * share :]], axis=-1)
    return even, odd


vmem = pl.BlockSpec(memory_space=pltpu.VMEM)
smem = pl.BlockSpec(memory_space=pltpu.SMEM)
hbm = pl.BlockSpec(memory_space=pltpu.HBM)
anywhere = pl.BlockSpec(memory_space=pl.ANY)


def call(kernel, outs, in_specs, scratch=(), limit=6, out_specs=None, cost=1000):
    return pl.pallas_call(
        kernel,
        out_shape=outs,
        in_specs=in_specs,
        out_specs=out_specs or [vmem] * len(outs),
        scratch_shapes=scratch,
        cost_estimate=pl.CostEstimate(flops=300*cost, bytes_accessed=cost, transcendentals=0),
        compiler_params=pltpu.CompilerParams(vmem_limit_bytes=limit * 1024 * 1024),
    )


def shape(*dims, dtype=f32):
    return jax.ShapeDtypeStruct(dims, dtype)


def forward_kernel(
    at, hidden, gain, bias, fc1, fc1_bias, fc2, pre, scaled, keep, send_c, send_y, send_b,
    rows, line1, line2, line3, w1, w2, value, norm, part, sems,
):
    loads = [
        pltpu.make_async_copy(source, target, sems.at[index])
        for index, (source, target) in enumerate(
            [
                (hidden, rows),
                (gain, line1),
                (bias, line2),
                (fc1, w1),
                (fc1_bias, line3),
                (fc2, w2),
            ]
        )
    ]
    for load in loads:
        load.start()
    for load in loads[:3]:
        load.wait()
    units = fc1.shape[0]
    normed, norm[...], inverse = normalize(rows[...], line1[...], line2[...])
    normed = normed.astype(bf16)
    save_norm = pltpu.make_async_copy(norm, scaled, sems.at[6])
    save_norm.start()
    loads[3].wait()
    loads[4].wait()
    value[:, units : units + 1] = inverse
    acts = []
    cuts = ((0, 512), (512, units))
    for low, high in cuts:
        linear = contract_cols(normed, w1[low:high, :]) + line3[low:high]
        value[:, low:high] = linear
        acts.append(jax.nn.gelu(linear, approximate=True).astype(bf16))
    save_pre = pltpu.make_async_copy(value, pre, sems.at[7])
    save_pre.start()
    loads[5].wait()
    total = jnp.zeros(part.shape, f32)
    for (low, high), act in zip(cuts, acts):
        total = total + jnp.dot(act, w2[low:high, :], preferred_element_type=f32)
    part[...] = total
    quarter = keep.shape[0]
    side, core = at[0] // 2, at[0] % 2

    def own(core, side):
        return pl.ds(pl.multiple_of((core * 2 + side) * quarter, quarter), quarter)

    keep[...] = rows[own(core, side), :] + part[own(core, side), :]
    send_c[...] = part[own(1 - core, side), :].astype(bf16)
    send_y[...] = part[own(core, 1 - side), :].astype(bf16)
    send_b[...] = part[own(1 - core, 1 - side), :].astype(bf16)
    save_norm.wait()
    save_pre.wait()


def hold_kernel(kept, got, out):
    out[...] = kept[...] + got[...].astype(f32)


def embed_kernel(kept, got_y, got_b, gain, bias, head, unit, state):
    width = unit.shape[1]
    mixed = kept[...] + got_y[...].astype(f32) + got_b[...].astype(f32)
    normed, scaled, inverse = normalize(mixed, gain[...], bias[...])
    state[:, width : 2 * width] = scaled
    embed = jnp.dot(normed.astype(bf16), head[...], preferred_element_type=f32)
    level = lax.rsqrt(jnp.sum(embed * embed, axis=-1, keepdims=True) + eps)
    unit[...] = (embed * level).astype(bf16)
    state[:, :width] = embed * level
    state[:, 2 * width : 2 * width + 1] = level
    state[:, 2 * width + 1 : 2 * width + 2] = inverse


def stack_kernel(*refs, count):
    rows = refs[0].shape[0]
    for index, ref in enumerate(refs[:count]):
        refs[-1][index * rows : (index + 1) * rows, :] = ref[...]


def parts_kernel(at, first, second, third, after, half, send):
    rows = half.shape[0]
    own = pl.ds(pl.multiple_of(at[0] % 2 * rows, rows), rows)
    other = pl.ds(pl.multiple_of((1 - at[0] % 2) * rows, rows), rows)
    half[...] = third[own, :]
    for index, ref in enumerate((third, second, first)):
        send[index * rows : (index + 1) * rows, :] = ref[other, :]


def level_kernel(log_scale, offset, after, level):
    level[0:1, :] = jnp.exp(jnp.full((1, level.shape[1]), log_scale[0], f32))
    level[1:2, :] = jnp.full((1, level.shape[1]), offset[0], f32)


def norm_kernel(at, fourth, third, second, first, across, images, unit, image_rows, inverse):
    size = fourth.shape[0]
    mine = pl.ds(pl.multiple_of(at[0] % 2 * size, size), size)

    def put(index, values):
        rows = slice(index * size, (index + 1) * size)
        image_rows[rows, :] = values
        wide = values.astype(f32)
        size_of = lax.rsqrt(jnp.sum(wide * wide, axis=-1, keepdims=True) + eps)
        inverse[rows, :] = size_of
        unit[rows, :] = (wide * size_of).astype(bf16)

    put(0, fourth[...])
    for index in range(3):
        put(1 + index, across[index * size : (index + 1) * size, :])
    for index, ref in enumerate((third, second, first, images)):
        put(4 + index, ref[mine, :])


def near_kernel(at, level, unit, own, coef, *, chunk, quarter):
    scale, offset = level[0:1, 0:1], level[1:2, 0:1]
    size = unit.shape[0] // 8
    diagonal = 7 * size + at[0] // 2 * quarter
    for start in range(0, unit.shape[0], chunk):
        rows = slice(start, start + chunk)
        chance = jax.nn.sigmoid(scale * contract_cols(unit[rows, :], own[...]) + offset)
        line = lax.broadcasted_iota(jnp.int32, chance.shape, 0) + (start - diagonal)
        cols = lax.broadcasted_iota(jnp.int32, chance.shape, 1)
        ident = ((line == cols) & (cols < quarter)).astype(f32)
        coef[rows, :] = (scale * (chance - ident)).astype(bf16)


def pairs_kernel(level, unit, other, near, coef, keep, send, *, chunk):
    scale, offset = level[0:1, 0:1], level[1:2, 0:1]
    for start in range(0, unit.shape[0], chunk):
        rows = slice(start, start + chunk)
        chance = jax.nn.sigmoid(scale * contract_cols(unit[rows, :], other[...]) + offset)
        coef[rows, :] = (scale * chance).astype(bf16)
    send[...] = contract_rows(coef[...], unit[...]).astype(bf16)
    keep[...] = contract_rows(near[...], unit[...])


def images_kernel(images, inverse, near, coef, own, other, *parts, first):
    size = images.shape[0] // 8
    rows = slice(first * size, (first + 4) * size)
    grad = jnp.dot(near[rows, :], own[...], preferred_element_type=f32)
    grad = grad + jnp.dot(coef[rows, :], other[...], preferred_element_type=f32)
    level = inverse[rows, :]
    direct = images[rows, :].astype(f32) * level
    inner = jnp.sum(direct * grad, axis=-1, keepdims=True)
    grad = (grad - direct * inner) * level
    start = 0
    for part in parts:
        count = part.shape[0]
        part[...] = grad[start : start + count].astype(part.dtype)
        start += count


def pass_kernel(own, across, got, after, out, *, index):
    size = own.shape[0]
    if got.shape[0] == size:
        out[:size, :] = (own[...].astype(f32) + got[...].astype(f32)).astype(bf16)
        out[size:, :] = across[index * size : (index + 1) * size, :]
    else:
        out[:size, :] = (own[...].astype(f32) + got[:size, :].astype(f32)).astype(bf16)
        part = across[index * size : (index + 1) * size, :].astype(f32)
        out[size:, :] = (part + got[size:, :].astype(f32)).astype(bf16)


def owner_kernel(at, own, got, after, keep, send):
    size = own.shape[0]
    core = at[0] % 2 == 0
    share = own.shape[1] // 4
    mine = own[...] + got[:size, :].astype(f32)
    theirs = got[size:, :].astype(f32)
    low, high = jnp.where(core, mine, theirs), jnp.where(core, theirs, mine)
    for index, rows in enumerate((low, high)):
        place = slice(index * size, (index + 1) * size)
        even, odd = columns(rows, share)
        keep[place, :] = jnp.where(core, even, odd)
        send[place, :] = jnp.where(core, odd, even).astype(bf16)


def split_kernel(kept, got, after, near, *far):
    rows = near.shape[0]
    near[...] = kept[:rows, :] + got[:rows, :].astype(f32)
    for index, ref in enumerate(far):
        part = slice((index + 1) * rows, (index + 2) * rows)
        ref[...] = (kept[part, :] + got[part, :].astype(f32)).astype(bf16)


def join_kernel(near, first, second, third, after, keep, send):
    total = near[...] + first[...].astype(f32) + second[...].astype(f32) + third[...].astype(f32)
    half = keep.shape[0]
    keep[...] = total[:half]
    send[...] = total[half:].astype(bf16)


def head_kernel(kept, got, state, head, gain, grad):
    width = grad.shape[1]
    upstream = kept[...] + got[...].astype(f32)
    text_dir = state[:, :width]
    inner = jnp.sum(text_dir * upstream, axis=-1, keepdims=True)
    grad_embed = (upstream - text_dir * inner) * state[:, 2 * width : 2 * width + 1]
    grad_normed = contract_cols(grad_embed.astype(bf16), head[...])
    scaled, inverse = state[:, width : 2 * width], state[:, 2 * width + 1 : 2 * width + 2]
    grad[...] = norm_back(grad_normed, gain[...], scaled, inverse).astype(bf16)


def slope_kernel(pre, after, out, *, units):
    out[:, :units] = gelu_slope(pre[:, :units])
    out[:, units : units + 1] = pre[:, units : units + 1]


def backward_kernel(
    at, own_rows, other_rows, slope, scaled, gain, fc1, fc2, keep, send, rest, grad
):
    quarter = grad.shape[0] // 4
    row_side, row_core = at[0] // 2, at[0] % 2
    for index, ref in enumerate((own_rows, other_rows)):
        start = row_core if index == 0 else 1 - row_core
        for step in range(2):
            place = start * 2 + (row_side if step == 0 else 1 - row_side)
            rows = pl.ds(pl.multiple_of(place * quarter, quarter), quarter)
            grad[rows, :] = ref[step * quarter : (step + 1) * quarter, :]
    share = grad.shape[1] // 4
    units = fc1.shape[0]
    core = at[0] % 2 == 0
    own = jnp.where(core, *columns(grad[...], share))
    rest[...] = jnp.where(at[0] // 2 == 0, own[:, :share], own[:, share:])
    grad_act = contract_cols(grad[...], fc2[...])
    grad_pre = (grad_act * slope[:, :units]).astype(bf16)
    part = jnp.dot(grad_pre, fc1[...], preferred_element_type=f32)
    part = norm_back(part, gain[...], scaled[...], slope[:, units : units + 1])
    even, odd = columns(part, share)
    keep[...] = jnp.where(core, even, odd)
    send[...] = jnp.where(core, odd, even).astype(bf16)


def halve_kernel(at, kept, got, keep, send):
    total = kept[...] + got[...].astype(f32)
    half = keep.shape[1]
    low, high = total[:, :half], total[:, half:]
    side = at[0] // 2 == 0
    keep[...] = jnp.where(side, low, high)
    send[...] = jnp.where(side, high, low).astype(bf16)


def hidden_kernel(kept, got, rest, out):
    out[...] = rest[...].astype(f32) + (kept[...] + got[...].astype(f32))


def total_kernel(kept, got, out):
    out[...] = kept[...] + got[...].astype(f32)


def shards(
    images,
    hidden_in,
    norm1_gain,
    norm1_bias,
    fc1,
    fc1_bias,
    fc2,
    norm2_gain,
    norm2_bias,
    head,
    log_scale,
    logit_bias,
):
    block, width = images.shape
    quarter = block // 4
    share = width // 4
    units = fc1.shape[1]
    half = block // 2
    at = lax.axis_index(("yl", "c")).astype(jnp.int32).reshape(1)
    fc1 = fc1.T

    low = shape(half, width, dtype=bf16)
    pad = (units // 128 + 1) * 128
    pre, scaled_in, keep, *sends = call(
        forward_kernel,
        [shape(block, pad), shape(block, width), shape(quarter, width)]
        + [shape(quarter, width, dtype=bf16)] * 3,
        [smem] + [hbm] * 6,
        [
            pltpu.VMEM((block, width), f32),
            pltpu.VMEM((width,), f32),
            pltpu.VMEM((width,), f32),
            pltpu.VMEM((units,), f32),
            pltpu.VMEM((units, width), bf16),
            pltpu.VMEM((units, width), bf16),
            pltpu.VMEM((block, pad), f32),
            pltpu.VMEM((block, width), f32),
            pltpu.VMEM((block, width), f32),
            pltpu.SemaphoreType.DMA((8,)),
        ],
        limit=58,
        out_specs=[hbm] * 2 + [vmem] * 4,
    )(at, hidden_in, norm1_gain, norm1_bias, fc1, fc1_bias, fc2)
    first = ring(images, 1)
    sends = [
        lax.ppermute(send, ("yl", "c"), [(i, i ^ bits) for i in range(4)])
        for send, bits in zip(sends, (1, 2, 3))
    ]
    keep = call(hold_kernel, [shape(quarter, width)], [vmem] * 2, cost=1000)(keep, sends[0])[0]
    second = ring(lax.optimization_barrier((first, keep))[0], 1)
    text_unit, state = call(
        embed_kernel,
        [shape(quarter, width, dtype=bf16), shape(quarter, 2 * width + 128)],
        [vmem] * 6,
        limit=10,
        cost=20001000,
    )(
        keep,
        *sends[1:],
        norm2_gain,
        norm2_bias,
        head,
    )

    third = ring(lax.optimization_barrier((second, text_unit))[0], 1)

    near = call(
        functools.partial(stack_kernel, count=2), [shape(half, width, dtype=bf16)], [vmem] * 2, cost=20001000
    )(text_unit, facing(text_unit))[0]
    level = call(level_kernel, [shape(2, 128)], [smem] * 2 + [anywhere])(
        log_scale, logit_bias, near
    )[0]
    fourth, across = call(
        parts_kernel,
        [low, shape(3 * half, width, dtype=bf16)],
        [smem] + [vmem] * 3 + [anywhere],
    )(at, first, second, third, level)
    own = call(
        functools.partial(stack_kernel, count=4),
        [shape(4 * half, width, dtype=bf16)],
        [vmem] * 4 + [anywhere] * 2,
        cost=20001000,
    )(near, *(shift(near, "x", hop) for hop in hops[1:]), fourth, across)[0]
    fourth, across = ring(fourth, 1), shift(across, "c", 1)
    own, fourth, across = lax.optimization_barrier((own, fourth, across))
    other = shift(own, "c", 1)

    many = 8 * half
    image_unit, image_rows, inverse_image = call(
        norm_kernel,
        [shape(many, width, dtype=bf16)] * 2 + [shape(many, 1)],
        [smem] + [vmem] * 6,
        limit=12,
        cost=1000,
    )(at, fourth, third, second, first, across, images)
    near_coef = call(
        functools.partial(near_kernel, chunk=many // 2, quarter=quarter),
        [shape(many, 4 * half, dtype=bf16)],
        [smem] + [vmem] * 3,
        limit=12,
        cost=1000,
    )(at, level, image_unit, own)[0]
    coef, keep, send = call(
        functools.partial(pairs_kernel, chunk=many // 2),
        [
            shape(many, 4 * half, dtype=bf16),
            shape(4 * half, width),
            shape(4 * half, width, dtype=bf16),
        ],
        [vmem] * 4,
        limit=16,
    )(level, image_unit, other, near_coef)
    got = shift(send, "c", 1)

    fourth, across = call(
        functools.partial(images_kernel, first=0),
        [low, shape(3 * half, width, dtype=bf16)],
        [vmem] * 6,
        limit=12,
    )(image_rows, inverse_image, near_coef, coef, own, other)
    near, *far = call(
        split_kernel,
        [shape(half, width)] + [low] * 3,
        [vmem] * 2 + [anywhere],
    )(keep, got, fourth)
    far = [shift(far[index], "x", 4 - hop) for index, hop in enumerate(hops[1:])]
    fourth, across = ring(fourth, -1), shift(across, "c", 1)
    *parts, image_part = call(
        functools.partial(images_kernel, first=4),
        [low] * 3 + [shape(half, width)],
        [vmem] * 6,
        limit=12,
    )(image_rows, inverse_image, near_coef, coef, own, other)

    passed = []

    def onward(index, got, after):
        moving = call(
            functools.partial(pass_kernel, index=index),
            [shape(block, width, dtype=bf16)],
            [vmem] * 3 + [anywhere],
        )(parts[index], across, got, after)[0]
        passed.append(moving)
        return ring(moving, -1)

    moved = onward(0, fourth, near)
    slope = call(
        functools.partial(slope_kernel, units=units), [shape(block, pad)], [vmem, anywhere]
    )(pre, passed[0])[0]
    moved = onward(1, moved, slope)
    keep, send = call(
        join_kernel,
        [shape(quarter, width), shape(quarter, width, dtype=bf16)],
        [vmem] * 4 + [anywhere],
        cost=60001000,
    )(near, *far, slope)
    grad_mixed = call(
        head_kernel, [shape(quarter, width, dtype=bf16)], [vmem] * 5, limit=10, cost=20001000
    )(keep, facing(send), state, head, norm2_gain)[0]
    moved = onward(2, moved, grad_mixed)
    grad_mixed = call(
        functools.partial(stack_kernel, count=2), [low], [vmem] * 2 + [anywhere], cost=1000
    )(grad_mixed, shift(grad_mixed, "yl", 1), passed[2])[0]
    keep, send, rest = call(
        backward_kernel,
        [
            shape(block, 2 * share),
            shape(block, 2 * share, dtype=bf16),
            shape(block, share, dtype=bf16),
        ],
        [smem] + [vmem] * 7,
        [
            pltpu.VMEM((block, width), bf16),
        ],
        limit=16,
        cost=1000,
    )(at, grad_mixed, shift(grad_mixed, "c", 1), slope, scaled_in, norm1_gain, fc1, fc2)
    keep, send = call(
        halve_kernel,
        [shape(block, share), shape(block, share, dtype=bf16)],
        [smem, vmem, vmem],
    )(at, keep, shift(send, "c", 1))
    hidden_keep = keep
    grad_hidden = call(hidden_kernel, [shape(block, share)], [vmem] * 3)(
        keep, shift(send, "yl", 1), rest
    )[0]

    keep, send = call(
        owner_kernel,
        [shape(block, 2 * share), shape(block, 2 * share, dtype=bf16)],
        [smem] + [vmem] * 2 + [anywhere],
    )(at, image_part, moved, hidden_keep)
    keep, send = call(
        halve_kernel,
        [shape(block, share), shape(block, share, dtype=bf16)],
        [smem, vmem, vmem],
    )(at, keep, shift(send, "c", 1))
    grad_images = call(total_kernel, [shape(block, share)], [vmem] * 2)(
        keep, shift(send, "yl", 1)
    )[0]
    return (grad_images, grad_hidden)


def solution(mesh):
    grid = Mesh(mesh.devices.reshape(8, 4, 2, 2, 2), ("z", "x", "yh", "yl", "c"))
    dp, mp = ("z", "x", "yh"), ("yl", "c")
    placed = (
        P(dp, None),
        P(dp, None),
        P(),
        P(),
        P(None, mp),
        P(mp),
        P(mp, None),
        P(),
        P(),
        P(),
        P(),
        P(),
    )
    return jax.shard_map(
        shards,
        mesh=grid,
        in_specs=placed,
        out_specs=(P(dp, mp), P(dp, mp)),
        check_vma=False,
    )
```

```python
import functools

import jax
import jax.numpy as jnp
from jax import lax
from jax.experimental import pallas as pl
from jax.experimental.pallas import tpu as pltpu
from jax.sharding import Mesh, PartitionSpec as P

eps = 1e-06
hops = (0, 2, 3, 1)
f32 = jnp.float32
bf16 = jnp.bfloat16


def normalize(values, gain, shift):
    mean = jnp.mean(values, axis=-1, keepdims=True)
    centered = values - mean
    inverse = lax.rsqrt(jnp.mean(centered * centered, axis=-1, keepdims=True) + eps)
    scaled = centered * inverse
    return (scaled * gain + shift, scaled, inverse)


def gelu_slope(values):
    factor = 0.7978845608028654
    inner = factor * (values + 0.044715 * values * values * values)
    tangent = jnp.tanh(inner)
    return 0.5 * (1.0 + tangent) + 0.5 * values * (1.0 - tangent * tangent) * factor * (
        1.0 + 3.0 * 0.044715 * values * values
    )


def norm_back(upstream, gain, scaled, inverse):
    grad = upstream * gain
    return inverse * (
        grad
        - jnp.mean(grad, axis=-1, keepdims=True)
        - scaled * jnp.mean(grad * scaled, axis=-1, keepdims=True)
    )


def contract_rows(left, right):
    return lax.dot_general(left, right, (((0,), (0,)), ((), ())), preferred_element_type=f32)


def contract_cols(left, right):
    return lax.dot_general(left, right, (((1,), (1,)), ((), ())), preferred_element_type=f32)


def shift(values, axes, step):
    size = lax.axis_size(axes)
    return lax.ppermute(values, axes, [(i, (i + step) % size) for i in range(size)])


def ring(values, sign):
    size = lax.axis_size("z")
    pairs = []
    for z in range(size):
        pairs.append((2 * z, (z + sign) % size * 2))
        pairs.append((2 * z + 1, (z - sign) % size * 2 + 1))
    return lax.ppermute(values, ("z", "c"), pairs)


def facing(values):
    return lax.ppermute(values, ("yh", "yl"), [(0, 3), (3, 0), (1, 2), (2, 1)])


def columns(values, share):
    even = jnp.concatenate([values[..., :share], values[..., 2 * share : 3 * share]], axis=-1)
    odd = jnp.concatenate([values[..., share : 2 * share], values[..., 3 * share :]], axis=-1)
    return even, odd


vmem = pl.BlockSpec(memory_space=pltpu.VMEM)
smem = pl.BlockSpec(memory_space=pltpu.SMEM)
hbm = pl.BlockSpec(memory_space=pltpu.HBM)
anywhere = pl.BlockSpec(memory_space=pl.ANY)


def call(kernel, outs, in_specs, scratch=(), limit=6, out_specs=None, cost=1000):
    return pl.pallas_call(
        kernel,
        out_shape=outs,
        in_specs=in_specs,
        out_specs=out_specs or [vmem] * len(outs),
        scratch_shapes=scratch,
        cost_estimate=pl.CostEstimate(flops=300*cost, bytes_accessed=cost, transcendentals=0),
        compiler_params=pltpu.CompilerParams(vmem_limit_bytes=limit * 1024 * 1024),
    )


def shape(*dims, dtype=f32):
    return jax.ShapeDtypeStruct(dims, dtype)


def forward_kernel(
    at, hidden, gain, bias, fc1, fc1_bias, fc2, pre, scaled, keep, send_c, send_y, send_b,
    rows, line1, line2, line3, w1, w2, value, norm, part, sems,
):
    loads = [
        pltpu.make_async_copy(source, target, sems.at[index])
        for index, (source, target) in enumerate(
            [
                (hidden, rows),
                (gain, line1),
                (bias, line2),
                (fc1, w1),
                (fc1_bias, line3),
                (fc2, w2),
            ]
        )
    ]
    for load in loads[:5]:
        load.start()
    for load in loads[:3]:
        load.wait()
    loads[5].start()
    units = fc1.shape[0]
    normed, norm[...], inverse = normalize(rows[...], line1[...], line2[...])
    normed = normed.astype(bf16)
    save_norm = pltpu.make_async_copy(norm, scaled, sems.at[6])
    save_norm.start()
    loads[3].wait()
    loads[4].wait()
    value[:, units : units + 1] = inverse
    acts = []
    cuts = ((0, 512), (512, units))
    for low, high in cuts:
        linear = contract_cols(normed, w1[low:high, :]) + line3[low:high]
        value[:, low:high] = linear
        acts.append(jax.nn.gelu(linear, approximate=True).astype(bf16))
    save_pre = pltpu.make_async_copy(value, pre, sems.at[7])
    save_pre.start()
    loads[5].wait()
    total = jnp.zeros(part.shape, f32)
    for (low, high), act in zip(cuts, acts):
        total = total + jnp.dot(act, w2[low:high, :], preferred_element_type=f32)
    part[...] = total
    quarter = keep.shape[0]
    side, core = at[0] // 2, at[0] % 2

    def own(core, side):
        return pl.ds(pl.multiple_of((core * 2 + side) * quarter, quarter), quarter)

    keep[...] = rows[own(core, side), :] + part[own(core, side), :]
    send_c[...] = part[own(1 - core, side), :].astype(bf16)
    send_y[...] = part[own(core, 1 - side), :].astype(bf16)
    send_b[...] = part[own(1 - core, 1 - side), :].astype(bf16)
    save_norm.wait()
    save_pre.wait()


def hold_kernel(kept, got, out):
    out[...] = kept[...] + got[...].astype(f32)


def embed_kernel(kept, got_y, got_b, gain, bias, head, unit, state):
    width = unit.shape[1]
    mixed = kept[...] + got_y[...].astype(f32) + got_b[...].astype(f32)
    normed, scaled, inverse = normalize(mixed, gain[...], bias[...])
    state[:, width : 2 * width] = scaled
    embed = jnp.dot(normed.astype(bf16), head[...], preferred_element_type=f32)
    level = lax.rsqrt(jnp.sum(embed * embed, axis=-1, keepdims=True) + eps)
    unit[...] = (embed * level).astype(bf16)
    state[:, :width] = embed * level
    state[:, 2 * width : 2 * width + 1] = level
    state[:, 2 * width + 1 : 2 * width + 2] = inverse


def stack_kernel(*refs, count):
    rows = refs[0].shape[0]
    for index, ref in enumerate(refs[:count]):
        refs[-1][index * rows : (index + 1) * rows, :] = ref[...]


def parts_kernel(at, first, second, third, after, half, send):
    rows = half.shape[0]
    own = pl.ds(pl.multiple_of(at[0] % 2 * rows, rows), rows)
    other = pl.ds(pl.multiple_of((1 - at[0] % 2) * rows, rows), rows)
    half[...] = third[own, :]
    for index, ref in enumerate((third, second, first)):
        send[index * rows : (index + 1) * rows, :] = ref[other, :]


def level_kernel(log_scale, offset, after, level):
    level[0:1, :] = jnp.exp(jnp.full((1, level.shape[1]), log_scale[0], f32))
    level[1:2, :] = jnp.full((1, level.shape[1]), offset[0], f32)


def norm_kernel(at, fourth, third, second, first, across, images, unit, image_rows, inverse):
    size = fourth.shape[0]
    mine = pl.ds(pl.multiple_of(at[0] % 2 * size, size), size)

    def put(index, values):
        rows = slice(index * size, (index + 1) * size)
        image_rows[rows, :] = values
        wide = values.astype(f32)
        size_of = lax.rsqrt(jnp.sum(wide * wide, axis=-1, keepdims=True) + eps)
        inverse[rows, :] = size_of
        unit[rows, :] = (wide * size_of).astype(bf16)

    put(0, fourth[...])
    for index in range(3):
        put(1 + index, across[index * size : (index + 1) * size, :])
    for index, ref in enumerate((third, second, first, images)):
        put(4 + index, ref[mine, :])


def near_kernel(at, level, unit, own, coef, *, chunk, quarter):
    scale, offset = level[0:1, 0:1], level[1:2, 0:1]
    size = unit.shape[0] // 8
    diagonal = 7 * size + at[0] // 2 * quarter
    for start in range(0, unit.shape[0], chunk):
        rows = slice(start, start + chunk)
        chance = jax.nn.sigmoid(scale * contract_cols(unit[rows, :], own[...]) + offset)
        line = lax.broadcasted_iota(jnp.int32, chance.shape, 0) + (start - diagonal)
        cols = lax.broadcasted_iota(jnp.int32, chance.shape, 1)
        ident = ((line == cols) & (cols < quarter)).astype(f32)
        coef[rows, :] = (scale * (chance - ident)).astype(bf16)


def pairs_kernel(level, unit, other, near, coef, keep, send, *, chunk):
    scale, offset = level[0:1, 0:1], level[1:2, 0:1]
    for start in range(0, unit.shape[0], chunk):
        rows = slice(start, start + chunk)
        chance = jax.nn.sigmoid(scale * contract_cols(unit[rows, :], other[...]) + offset)
        coef[rows, :] = (scale * chance).astype(bf16)
    send[...] = contract_rows(coef[...], unit[...]).astype(bf16)
    keep[...] = contract_rows(near[...], unit[...])


def images_kernel(images, inverse, near, coef, own, other, *parts, first):
    size = images.shape[0] // 8
    rows = slice(first * size, (first + 4) * size)
    grad = jnp.dot(near[rows, :], own[...], preferred_element_type=f32)
    grad = grad + jnp.dot(coef[rows, :], other[...], preferred_element_type=f32)
    level = inverse[rows, :]
    direct = images[rows, :].astype(f32) * level
    inner = jnp.sum(direct * grad, axis=-1, keepdims=True)
    grad = (grad - direct * inner) * level
    start = 0
    for part in parts:
        count = part.shape[0]
        part[...] = grad[start : start + count].astype(part.dtype)
        start += count


def pass_kernel(own, across, got, after, out, *, index):
    size = own.shape[0]
    if got.shape[0] == size:
        out[:size, :] = (own[...].astype(f32) + got[...].astype(f32)).astype(bf16)
        out[size:, :] = across[index * size : (index + 1) * size, :]
    else:
        out[:size, :] = (own[...].astype(f32) + got[:size, :].astype(f32)).astype(bf16)
        part = across[index * size : (index + 1) * size, :].astype(f32)
        out[size:, :] = (part + got[size:, :].astype(f32)).astype(bf16)


def owner_kernel(at, own, got, after, keep, send):
    size = own.shape[0]
    core = at[0] % 2 == 0
    share = own.shape[1] // 4
    mine = own[...] + got[:size, :].astype(f32)
    theirs = got[size:, :].astype(f32)
    low, high = jnp.where(core, mine, theirs), jnp.where(core, theirs, mine)
    for index, rows in enumerate((low, high)):
        place = slice(index * size, (index + 1) * size)
        even, odd = columns(rows, share)
        keep[place, :] = jnp.where(core, even, odd)
        send[place, :] = jnp.where(core, odd, even).astype(bf16)


def split_kernel(kept, got, after, near, *far):
    rows = near.shape[0]
    near[...] = kept[:rows, :] + got[:rows, :].astype(f32)
    for index, ref in enumerate(far):
        part = slice((index + 1) * rows, (index + 2) * rows)
        ref[...] = (kept[part, :] + got[part, :].astype(f32)).astype(bf16)


def join_kernel(near, first, second, third, after, keep, send):
    total = near[...] + first[...].astype(f32) + second[...].astype(f32) + third[...].astype(f32)
    half = keep.shape[0]
    keep[...] = total[:half]
    send[...] = total[half:].astype(bf16)


def head_kernel(kept, got, state, head, gain, grad):
    width = grad.shape[1]
    upstream = kept[...] + got[...].astype(f32)
    text_dir = state[:, :width]
    inner = jnp.sum(text_dir * upstream, axis=-1, keepdims=True)
    grad_embed = (upstream - text_dir * inner) * state[:, 2 * width : 2 * width + 1]
    grad_normed = contract_cols(grad_embed.astype(bf16), head[...])
    scaled, inverse = state[:, width : 2 * width], state[:, 2 * width + 1 : 2 * width + 2]
    grad[...] = norm_back(grad_normed, gain[...], scaled, inverse).astype(bf16)


def slope_kernel(pre, after, out, *, units):
    out[:, :units] = gelu_slope(pre[:, :units])
    out[:, units : units + 1] = pre[:, units : units + 1]


def backward_kernel(
    at, own_rows, other_rows, slope, scaled, gain, fc1, fc2, keep, send, rest, grad
):
    quarter = grad.shape[0] // 4
    row_side, row_core = at[0] // 2, at[0] % 2
    for index, ref in enumerate((own_rows, other_rows)):
        start = row_core if index == 0 else 1 - row_core
        for step in range(2):
            place = start * 2 + (row_side if step == 0 else 1 - row_side)
            rows = pl.ds(pl.multiple_of(place * quarter, quarter), quarter)
            grad[rows, :] = ref[step * quarter : (step + 1) * quarter, :]
    share = grad.shape[1] // 4
    units = fc1.shape[0]
    core = at[0] % 2 == 0
    own = jnp.where(core, *columns(grad[...], share))
    rest[...] = jnp.where(at[0] // 2 == 0, own[:, :share], own[:, share:])
    grad_act = contract_cols(grad[...], fc2[...])
    grad_pre = (grad_act * slope[:, :units]).astype(bf16)
    part = jnp.dot(grad_pre, fc1[...], preferred_element_type=f32)
    part = norm_back(part, gain[...], scaled[...], slope[:, units : units + 1])
    even, odd = columns(part, share)
    keep[...] = jnp.where(core, even, odd)
    send[...] = jnp.where(core, odd, even).astype(bf16)


def halve_kernel(at, kept, got, keep, send):
    total = kept[...] + got[...].astype(f32)
    half = keep.shape[1]
    low, high = total[:, :half], total[:, half:]
    side = at[0] // 2 == 0
    keep[...] = jnp.where(side, low, high)
    send[...] = jnp.where(side, high, low).astype(bf16)


def hidden_kernel(kept, got, rest, out):
    out[...] = rest[...].astype(f32) + (kept[...] + got[...].astype(f32))


def total_kernel(kept, got, out):
    out[...] = kept[...] + got[...].astype(f32)


def shards(
    images,
    hidden_in,
    norm1_gain,
    norm1_bias,
    fc1,
    fc1_bias,
    fc2,
    norm2_gain,
    norm2_bias,
    head,
    log_scale,
    logit_bias,
):
    block, width = images.shape
    quarter = block // 4
    share = width // 4
    units = fc1.shape[1]
    half = block // 2
    at = lax.axis_index(("yl", "c")).astype(jnp.int32).reshape(1)
    fc1 = fc1.T

    low = shape(half, width, dtype=bf16)
    pad = (units // 128 + 1) * 128
    pre, scaled_in, keep, *sends = call(
        forward_kernel,
        [shape(block, pad), shape(block, width), shape(quarter, width)]
        + [shape(quarter, width, dtype=bf16)] * 3,
        [smem] + [hbm] * 6,
        [
            pltpu.VMEM((block, width), f32),
            pltpu.VMEM((width,), f32),
            pltpu.VMEM((width,), f32),
            pltpu.VMEM((units,), f32),
            pltpu.VMEM((units, width), bf16),
            pltpu.VMEM((units, width), bf16),
            pltpu.VMEM((block, pad), f32),
            pltpu.VMEM((block, width), f32),
            pltpu.VMEM((block, width), f32),
            pltpu.SemaphoreType.DMA((8,)),
        ],
        limit=58,
        out_specs=[hbm] * 2 + [vmem] * 4,
    )(at, hidden_in, norm1_gain, norm1_bias, fc1, fc1_bias, fc2)
    first = ring(images, 1)
    sends = [
        lax.ppermute(send, ("yl", "c"), [(i, i ^ bits) for i in range(4)])
        for send, bits in zip(sends, (1, 2, 3))
    ]
    keep = call(hold_kernel, [shape(quarter, width)], [vmem] * 2, cost=1000)(keep, sends[0])[0]
    second = ring(lax.optimization_barrier((first, keep))[0], 1)
    text_unit, state = call(
        embed_kernel,
        [shape(quarter, width, dtype=bf16), shape(quarter, 2 * width + 128)],
        [vmem] * 6,
        limit=10,
        cost=20001000,
    )(
        keep,
        *sends[1:],
        norm2_gain,
        norm2_bias,
        head,
    )

    third = ring(lax.optimization_barrier((second, text_unit))[0], 1)

    near = call(
        functools.partial(stack_kernel, count=2), [shape(half, width, dtype=bf16)], [vmem] * 2, cost=20001000
    )(text_unit, facing(text_unit))[0]
    level = call(level_kernel, [shape(2, 128)], [smem] * 2 + [anywhere])(
        log_scale, logit_bias, near
    )[0]
    fourth, across = call(
        parts_kernel,
        [low, shape(3 * half, width, dtype=bf16)],
        [smem] + [vmem] * 3 + [anywhere],
    )(at, first, second, third, level)
    own = call(
        functools.partial(stack_kernel, count=4),
        [shape(4 * half, width, dtype=bf16)],
        [vmem] * 4 + [anywhere] * 2,
        cost=20001000,
    )(near, *(shift(near, "x", hop) for hop in hops[1:]), fourth, across)[0]
    fourth, across = ring(fourth, 1), shift(across, "c", 1)
    own, fourth, across = lax.optimization_barrier((own, fourth, across))
    other = shift(own, "c", 1)

    many = 8 * half
    image_unit, image_rows, inverse_image = call(
        norm_kernel,
        [shape(many, width, dtype=bf16)] * 2 + [shape(many, 1)],
        [smem] + [vmem] * 6,
        limit=12,
        cost=1000,
    )(at, fourth, third, second, first, across, images)
    near_coef = call(
        functools.partial(near_kernel, chunk=many // 2, quarter=quarter),
        [shape(many, 4 * half, dtype=bf16)],
        [smem] + [vmem] * 3,
        limit=12,
        cost=1000,
    )(at, level, image_unit, own)[0]
    coef, keep, send = call(
        functools.partial(pairs_kernel, chunk=many // 2),
        [
            shape(many, 4 * half, dtype=bf16),
            shape(4 * half, width),
            shape(4 * half, width, dtype=bf16),
        ],
        [vmem] * 4,
        limit=16,
    )(level, image_unit, other, near_coef)
    got = shift(send, "c", 1)

    fourth, across = call(
        functools.partial(images_kernel, first=0),
        [low, shape(3 * half, width, dtype=bf16)],
        [vmem] * 6,
        limit=12,
    )(image_rows, inverse_image, near_coef, coef, own, other)
    near, *far = call(
        split_kernel,
        [shape(half, width)] + [low] * 3,
        [vmem] * 2 + [anywhere],
    )(keep, got, fourth)
    far = [shift(far[index], "x", 4 - hop) for index, hop in enumerate(hops[1:])]
    fourth, across = ring(fourth, -1), shift(across, "c", 1)
    *parts, image_part = call(
        functools.partial(images_kernel, first=4),
        [low] * 3 + [shape(half, width)],
        [vmem] * 6,
        limit=12,
    )(image_rows, inverse_image, near_coef, coef, own, other)

    passed = []

    def onward(index, got, after):
        moving = call(
            functools.partial(pass_kernel, index=index),
            [shape(block, width, dtype=bf16)],
            [vmem] * 3 + [anywhere],
        )(parts[index], across, got, after)[0]
        passed.append(moving)
        return ring(moving, -1)

    moved = onward(0, fourth, near)
    slope = call(
        functools.partial(slope_kernel, units=units), [shape(block, pad)], [vmem, anywhere]
    )(pre, passed[0])[0]
    moved = onward(1, moved, slope)
    keep, send = call(
        join_kernel,
        [shape(quarter, width), shape(quarter, width, dtype=bf16)],
        [vmem] * 4 + [anywhere],
        cost=60001000,
    )(near, *far, slope)
    grad_mixed = call(
        head_kernel, [shape(quarter, width, dtype=bf16)], [vmem] * 5, limit=10, cost=20001000
    )(keep, facing(send), state, head, norm2_gain)[0]
    moved = onward(2, moved, grad_mixed)
    grad_mixed = call(
        functools.partial(stack_kernel, count=2), [low], [vmem] * 2 + [anywhere], cost=1000
    )(grad_mixed, shift(grad_mixed, "yl", 1), passed[2])[0]
    keep, send, rest = call(
        backward_kernel,
        [
            shape(block, 2 * share),
            shape(block, 2 * share, dtype=bf16),
            shape(block, share, dtype=bf16),
        ],
        [smem] + [vmem] * 7,
        [
            pltpu.VMEM((block, width), bf16),
        ],
        limit=16,
        cost=1000,
    )(at, grad_mixed, shift(grad_mixed, "c", 1), slope, scaled_in, norm1_gain, fc1, fc2)
    keep, send = call(
        halve_kernel,
        [shape(block, share), shape(block, share, dtype=bf16)],
        [smem, vmem, vmem],
    )(at, keep, shift(send, "c", 1))
    hidden_keep = keep
    grad_hidden = call(hidden_kernel, [shape(block, share)], [vmem] * 3)(
        keep, shift(send, "yl", 1), rest
    )[0]

    keep, send = call(
        owner_kernel,
        [shape(block, 2 * share), shape(block, 2 * share, dtype=bf16)],
        [smem] + [vmem] * 2 + [anywhere],
    )(at, image_part, moved, hidden_keep)
    keep, send = call(
        halve_kernel,
        [shape(block, share), shape(block, share, dtype=bf16)],
        [smem, vmem, vmem],
    )(at, keep, shift(send, "c", 1))
    grad_images = call(total_kernel, [shape(block, share)], [vmem] * 2)(
        keep, shift(send, "yl", 1)
    )[0]
    return (grad_images, grad_hidden)


def solution(mesh):
    grid = Mesh(mesh.devices.reshape(8, 4, 2, 2, 2), ("z", "x", "yh", "yl", "c"))
    dp, mp = ("z", "x", "yh"), ("yl", "c")
    placed = (
        P(dp, None),
        P(dp, None),
        P(),
        P(),
        P(None, mp),
        P(mp),
        P(mp, None),
        P(),
        P(),
        P(),
        P(),
        P(),
    )
    return jax.shard_map(
        shards,
        mesh=grid,
        in_specs=placed,
        out_specs=(P(dp, mp), P(dp, mp)),
        check_vma=False,
    )
```
